32 devices in a mesh: seq: 4 (over y, x), clip: 8 (over z, core).
Axes of the slice: x: 2, y: 2, z: 4, core: 2. Of those that a mesh axis runs over, the one named last changes fastest.
Arguments:
- frames_in: bfloat16 [8, 2048, 1024], P('clip', 'seq'), may hold values from -6 to 6
- text_states: bfloat16 [8, 256, 1024], P('clip'), may hold values from -6 to 6
- clip_lengths: int32 [8, 4], P('clip'), may hold values from 0 to 2048, as said below
- self_gain: float32 [1024], replicated, may hold values from 0.5 to 1.5
- self_bias: float32 [1024], replicated, may hold values from -1.5 to 1.5
- query_weight: bfloat16 [1024, 1024], replicated, may hold values from -0.1875 to 0.1875
- key_weight: bfloat16 [1024, 1024], replicated, may hold values from -0.1875 to 0.1875
- value_weight: bfloat16 [1024, 1024], replicated, may hold values from -0.1875 to 0.1875
- output_weight: bfloat16 [1024, 1024], replicated, may hold values from -0.75 to 0.75
- cross_gain: float32 [1024], replicated, may hold values from 0.5 to 1.5
- cross_bias: float32 [1024], replicated, may hold values from -1.5 to 1.5
- cross_query: bfloat16 [1024, 1024], replicated, may hold values from -0.1875 to 0.1875
- cross_key: bfloat16 [1024, 1024], replicated, may hold values from -0.1875 to 0.1875
- cross_value: bfloat16 [1024, 1024], replicated, may hold values from -0.1875 to 0.1875
- cross_output: bfloat16 [1024, 1024], replicated, may hold values from -0.75 to 0.75
- feed_gain: float32 [1024], replicated, may hold values from 0.5 to 1.5
- feed_bias: float32 [1024], replicated, may hold values from -1.5 to 1.5
- feed_upward: bfloat16 [1024, 4096], replicated, may hold values from -0.1875 to 0.1875
- feed_downward: bfloat16 [4096, 1024], replicated, may hold values from -0.09375 to 0.09375
- grad_out: bfloat16 [8, 2048, 1024], P('clip', 'seq'), may hold values from -6 to 6
Outputs:
- frames_out: bfloat16 [8, 2048, 1024], P('clip', 'seq')
- frames_grad: float32 [8, 2048, 1024], P('clip', 'seq')
- text_grad: float32 [8, 256, 1024], P('clip')
- self_gain_grad: float32 [1024], P('clip')
- self_bias_grad: float32 [1024], P('clip')
- query_grad: float32 [1024, 1024], P('clip')
- key_grad: float32 [1024, 1024], P('clip')
- value_grad: float32 [1024, 1024], P('clip')
- output_grad: float32 [1024, 1024], P('clip')
- cross_gain_grad: float32 [1024], P('clip')
- cross_bias_grad: float32 [1024], P('clip')
- cross_query_grad: float32 [1024, 1024], P('clip')
- cross_key_grad: float32 [1024, 1024], P('clip')
- cross_value_grad: float32 [1024, 1024], P('clip')
- cross_output_grad: float32 [1024, 1024], P('clip')
- feed_gain_grad: float32 [1024], P('clip')
- feed_bias_grad: float32 [1024], P('clip')
- upward_grad: float32 [1024, 4096], P('clip')
- downward_grad: float32 [4096, 1024], P('clip')
The draws below stay inside these ranges and needn't reach their ends.
Inputs may be any that keep to these rules, and one draw needn't show every extreme that they name: `clip_lengths`: in each group the lengths sum to 2048 and the first is more than 1536; where the first is 2048 the others are 0, else each of the others is 1 or more.
All inputs are finite; a program needn't handle non-finite values.
Results may differ from the reference program's by a relative error of at most 0.02.
Values may be sent and summed in bfloat16 or wider, within the bound.
A program may use at most 256 MiB of HBM per device.

```python
import jax
import jax.numpy as jnp
from jax import lax

D = 1024
HEADS = 16
HD = 64
FF = 4096
TEXT = 64
CLIPS = 4
F_DEV = 512
FRAMES = 2048
GROUPS = 8


def draw_clip_lengths(key, part):
    key = jax.random.fold_in(key, 7)
    keys = jax.random.split(key, 5)
    longs = jax.random.randint(keys[0], (GROUPS,), 0, 2)
    forced = jax.random.randint(keys[1], (), 0, GROUPS)
    longs = jnp.where(jnp.arange(GROUPS) == forced, 1, longs)
    rest = jax.random.randint(keys[2], (GROUPS,), 3, F_DEV)
    raw_one = jax.random.randint(keys[3], (GROUPS,), 0, 1 << 20)
    piece_one = 1 + raw_one % (rest - 2)
    raw_two = jax.random.randint(keys[4], (GROUPS,), 0, 1 << 20)
    piece_two = 1 + raw_two % (rest - piece_one - 1)
    piece_three = rest - piece_one - piece_two
    short = jnp.stack([FRAMES - rest, piece_one, piece_two, piece_three], axis=1)
    whole = jnp.zeros((GROUPS, CLIPS), jnp.int32).at[:, 0].set(FRAMES)
    return jnp.where(longs[:, None] == 1, whole, short).astype(jnp.int32)


def shard_levels(key, shape, shards, low, largest):
    level = 1.0
    for position, blocks in shards:
        steps = jax.random.uniform(jax.random.fold_in(jax.random.fold_in(key, 6), position), (blocks,), jnp.float32, low / len(shards), largest / len(shards))
        level = level * jnp.repeat(jnp.exp(steps), shape[position] // blocks).reshape((-1,) + (1,) * (len(shape) - 1 - position))
    return level


def noise(own_key, dims, scale, limit, shards=(), kind=jnp.bfloat16):
    entries = scale * jax.random.normal(own_key, dims, jnp.float32)
    if shards:
        entries = entries * shard_levels(own_key, dims, shards, -0.22, 0.18)
    return jnp.clip(entries, -limit, limit).astype(kind)


def setup_inputs(seed: int = 0) -> dict:
    seeds = jax.random.split(jax.random.key(seed), 21)
    return {
        "frames_in": noise(seeds[0], (GROUPS, FRAMES, D), 1.0, 6.0, ((0, 8), (1, 4))),
        "text_states": noise(seeds[1], (GROUPS, CLIPS * TEXT, D), 1.0, 6.0, ((0, 8),)),
        "clip_lengths": draw_clip_lengths(jax.random.fold_in(seeds[20], 71), 0),
        "self_gain": jnp.clip(1.0 + 0.1 * jax.random.normal(seeds[3], (D,), jnp.float32), 0.5, 1.5),
        "self_bias": noise(seeds[4], (D,), 0.3, 1.5, (), jnp.float32),
        "query_weight": noise(seeds[5], (D, D), D ** -0.5, 0.1875),
        "key_weight": noise(seeds[6], (D, D), D ** -0.5, 0.1875),
        "value_weight": noise(seeds[7], (D, D), D ** -0.5, 0.1875),
        "output_weight": noise(seeds[8], (D, D), HD ** -0.5, 0.75),
        "cross_gain": jnp.clip(1.0 + 0.1 * jax.random.normal(seeds[9], (D,), jnp.float32), 0.5, 1.5),
        "cross_bias": noise(seeds[10], (D,), 0.3, 1.5, (), jnp.float32),
        "cross_query": noise(seeds[11], (D, D), D ** -0.5, 0.1875),
        "cross_key": noise(seeds[12], (D, D), D ** -0.5, 0.1875),
        "cross_value": noise(seeds[13], (D, D), D ** -0.5, 0.1875),
        "cross_output": noise(seeds[14], (D, D), HD ** -0.5, 0.75),
        "feed_gain": jnp.clip(1.0 + 0.1 * jax.random.normal(seeds[15], (D,), jnp.float32), 0.5, 1.5),
        "feed_bias": noise(seeds[16], (D,), 0.3, 1.5, (), jnp.float32),
        "feed_upward": noise(seeds[17], (D, FF), D ** -0.5, 0.1875),
        "feed_downward": noise(seeds[18], (FF, D), FF ** -0.5, 0.09375),
        "grad_out": noise(seeds[19], (GROUPS, FRAMES, D), 1.0, 6.0, ((0, 8), (1, 4))),
    }


EPS = 1e-05
NEG = -1e+30
HIGH = lax.Precision.HIGHEST

@jax.custom_vjp
def low(v):
    return lax.optimization_barrier(v.astype(jnp.bfloat16)).astype(jnp.float32)

@jax.custom_vjp
def low_back(v):
    return v

def low_keep(v):
    return (low(v), None)

def low_pass(kept, grad):
    return (grad,)

def back_keep(v):
    return (v, None)

def back_low(kept, grad):
    return (low(grad),)
low.defvjp(low_keep, low_pass)
low_back.defvjp(back_keep, back_low)

def matmul(left, right):
    return jnp.dot(left, right, precision=HIGH)

def layer_norm(values, gain, bias):
    center = values - lax.optimization_barrier(jnp.mean(values, axis=-1, keepdims=True))
    spread = lax.optimization_barrier(jnp.mean(center * center, axis=-1, keepdims=True))
    return center * lax.rsqrt(spread + EPS) * gain + bias

def clip_bounds(lengths):
    lengths = lengths.astype(jnp.int32)
    ends = jnp.cumsum(lengths).astype(jnp.int32)
    begins = (ends - lengths).astype(jnp.int32)
    positions = jnp.arange(FRAMES, dtype=jnp.int32)
    owner = lax.optimization_barrier(jnp.sum((ends[None, :] <= positions[:, None]).astype(jnp.int32), axis=1)).astype(jnp.int32)
    slots = jnp.arange(CLIPS, dtype=jnp.int32)
    first = lax.optimization_barrier(jnp.sum(jnp.where(owner[:, None] == slots[None, :], begins[None, :], 0), axis=1)).astype(jnp.int32)
    return (owner, first)

def softmax_rows(scores):
    top = lax.optimization_barrier(jnp.max(scores, axis=-1, keepdims=True))
    expo = jnp.exp(scores - top)
    return expo / lax.optimization_barrier(jnp.sum(expo, axis=-1, keepdims=True))

def self_attention(query, keys, values, first):
    block = min(512, FRAMES)
    count = FRAMES // block
    scale = HD ** (-0.5)
    keys_split = keys.reshape(FRAMES, HEADS, HD)
    values_split = values.reshape(FRAMES, HEADS, HD)
    columns = jnp.arange(FRAMES, dtype=jnp.int32)

    def one_block(index):
        start = index * block
        rows_q = lax.dynamic_slice_in_dim(query, start, block, 0).reshape(block, HEADS, HD)
        rows = start + jnp.arange(block, dtype=jnp.int32)
        lower = lax.dynamic_slice_in_dim(first, start, block, 0)
        scores = low_back(jnp.einsum('qhe,khe->hqk', rows_q, keys_split, precision=HIGH) * scale)
        allowed = (columns[None, :] <= rows[:, None]) & (columns[None, :] >= lower[:, None])
        scores = jnp.where(allowed[None], scores, NEG)
        probs = softmax_rows(scores)
        mixed = jnp.einsum('hqk,khe->qhe', low(probs), values_split, precision=HIGH)
        return mixed.reshape(block, HEADS * HD)
    blocks_out = lax.map(jax.checkpoint(one_block), jnp.arange(count, dtype=jnp.int32))
    return blocks_out.reshape(FRAMES, HEADS * HD)

def cross_attention(query, keys, values, owner):
    scale = HD ** (-0.5)
    rows = CLIPS * TEXT
    query_split = query.reshape(FRAMES, HEADS, HD)
    keys_split = keys.reshape(rows, HEADS, HD)
    values_split = values.reshape(rows, HEADS, HD)
    key_clip = jnp.arange(rows, dtype=jnp.int32) // TEXT
    scores = low_back(jnp.einsum('qhe,khe->hqk', query_split, keys_split, precision=HIGH) * scale)
    allowed = owner[:, None] == key_clip[None, :]
    scores = jnp.where(allowed[None], scores, NEG)
    probs = softmax_rows(scores)
    mixed = jnp.einsum('hqk,khe->qhe', low(probs), values_split, precision=HIGH)
    return mixed.reshape(FRAMES, HEADS * HD)

def layer(frames, text, params, owner, first):
    self_gain, self_bias, query_weight, key_weight, value_weight, output_weight, cross_gain, cross_bias, cross_query, cross_key, cross_value, cross_output, feed_gain, feed_bias, feed_upward, feed_downward = params
    normed = low(layer_norm(frames, self_gain, self_bias))
    query = low(low_back(matmul(normed, query_weight)))
    keys = low(low_back(matmul(normed, key_weight)))
    values = low(low_back(matmul(normed, value_weight)))
    attended = low(low_back(self_attention(query, keys, values, first)))
    after_self = frames + low_back(matmul(attended, output_weight))
    normed_two = low(layer_norm(after_self, cross_gain, cross_bias))
    cross_q = low(low_back(matmul(normed_two, cross_query)))
    cross_k = low(low_back(matmul(text, cross_key)))
    cross_v = low(low_back(matmul(text, cross_value)))
    gathered = low(low_back(cross_attention(cross_q, cross_k, cross_v, owner)))
    after_cross = after_self + low_back(matmul(gathered, cross_output))
    normed_three = low(layer_norm(after_cross, feed_gain, feed_bias))
    hidden = low_back(matmul(normed_three, feed_upward))
    active = low(jax.nn.gelu(hidden, approximate=False))
    return after_cross + low_back(matmul(active, feed_downward))

def reference(frames_in, text_states, clip_lengths, self_gain, self_bias, query_weight, key_weight, value_weight, output_weight, cross_gain, cross_bias, cross_query, cross_key, cross_value, cross_output, feed_gain, feed_bias, feed_upward, feed_downward, grad_out):
    params = tuple((weight.astype(jnp.float32) for weight in (self_gain, self_bias, query_weight, key_weight, value_weight, output_weight, cross_gain, cross_bias, cross_query, cross_key, cross_value, cross_output, feed_gain, feed_bias, feed_upward, feed_downward)))

    def per_group(totals, items):
        frames, text, lengths, cotangent = items
        owner, first = clip_bounds(lengths)

        def forward(frames_f, text_f, weights):
            return layer(frames_f, text_f, weights, owner, first)
        output, pullback = jax.vjp(forward, frames.astype(jnp.float32), text.astype(jnp.float32), params)
        frame_grad, text_part, weight_grads = pullback(cotangent.astype(jnp.float32))
        totals = tuple((total + grad for total, grad in zip(totals, weight_grads)))
        return (totals, (output.astype(jnp.bfloat16), frame_grad, text_part))
    zeros = tuple((jnp.zeros(weight.shape, jnp.float32) for weight in params))
    totals, (outputs, frame_grads, text_grads) = lax.scan(per_group, zeros, (frames_in, text_states, clip_lengths, grad_out))
    return (outputs, frame_grads, text_grads, totals[0], totals[1], totals[2], totals[3], totals[4], totals[5], totals[6], totals[7], totals[8], totals[9], totals[10], totals[11], totals[12], totals[13], totals[14], totals[15])
```

```python
import math

import jax
import jax.numpy as jnp
from jax import lax
from jax.experimental import pallas as pl
from jax.experimental.pallas import tpu as pltpu
from jax.sharding import PartitionSpec as P

D = 1024
HEADS = 16
HD = 64
TEXT = 64
CLIPS = 4


EPS = 1e-05
NEG = -1e30
SQRT_HALF = 0.7071067811865476
INV_ROOT_TWO_PI = 0.3989422804014327

bf = jnp.bfloat16
f32 = jnp.float32
T, W, H, B = 2048, 256, 4, 256
C2 = math.log2(math.e) / 8.0
NT = (((1,), (1,)), ((), ()))
NN = (((1,), (0,)), ((), ()))
TN = (((0,), (0,)), ((), ()))


def dg(a, b, d):
    return lax.dot_general(a, b, d, preferred_element_type=f32)


def lanemask(rows,h):
    l=lax.broadcasted_iota(jnp.int32,(rows,W),1)
    return (l//HD)==h
def fwd_kernel(q_ref,k_ref,v_ref,first_ref,o_ref,lse_ref,s_ref):
    nb=T//B
    def qblock(i,masked):
        r0=pl.multiple_of(i*B,B)
        q=q_ref[pl.ds(r0,B),:]
        row=lax.broadcasted_iota(jnp.int32,(B,B),0); col=lax.broadcasted_iota(jnp.int32,(B,B),1)
        qm=[jnp.where(lanemask(B,h),q,jnp.zeros_like(q)) for h in range(H)]
        fst=first_ref[pl.ds(r0,B),:]
        def scores(j,carry,diag):
            c0=pl.multiple_of(j*B,B)
            k=k_ref[pl.ds(c0,B),:]
            out=[]
            for h in range(H):
                s=dg(qm[h],k,NT)
                if diag: s=jnp.where(col<=row,s,NEG)
                if masked: s=jnp.where(col+c0>=fst,s,NEG)
                s_ref[h,:,pl.ds(c0,B)]=s
                m=jnp.maximum(s[:,:128],s[:,128:])
                out.append(jnp.maximum(carry[h],m))
            return tuple(out)
        m=tuple(jnp.full((B,128),NEG,f32) for _ in range(H))
        m=lax.fori_loop(0,i,lambda j,c:scores(j,c,False),m)
        m=scores(i,m,True)
        m=[jnp.max(x,axis=1,keepdims=True) for x in m]
        def mix(j,carry):
            acc,ls=carry
            c0=pl.multiple_of(j*B,B)
            v=v_ref[pl.ds(c0,B),:]
            acc=list(acc); ls=list(ls)
            for h in range(H):
                p=jnp.exp2((s_ref[h,:,pl.ds(c0,B)]-m[h])*C2)
                ls[h]=ls[h]+p[:,:128]+p[:,128:]
                acc[h]=acc[h]+dg(p.astype(bf),v,NN)
            return tuple(acc),tuple(ls)
        acc,ls=lax.fori_loop(0,i+1,mix,(tuple(jnp.zeros((B,W),f32) for _ in range(H)),tuple(jnp.zeros((B,128),f32) for _ in range(H))))
        o=jnp.zeros((B,W),f32)
        lane=lax.broadcasted_iota(jnp.int32,(B,128),1)
        lse=jnp.zeros((B,128),f32)
        for h in range(H):
            l=jnp.sum(ls[h],axis=1,keepdims=True)
            o=jnp.where(lanemask(B,h),acc[h]/l,o)
            lse=jnp.where(lane==h,m[h]*C2+jnp.log2(l),lse)
        o_ref[pl.ds(r0,B),:]=o.astype(bf)
        lse_ref[:,pl.ds(r0,B)]=lse.T[:8]
    def body(i,c): qblock(i,False); return c
    lax.fori_loop(0,6,body,0)
    def body2(i,c): qblock(i,True); return c
    lax.fori_loop(6,8,body2,0)
def fwd(q,k,v,first):
    return pl.pallas_call(fwd_kernel,out_shape=(jax.ShapeDtypeStruct((T,W),bf),jax.ShapeDtypeStruct((8,T),f32)),
      in_specs=[pl.BlockSpec(memory_space=pltpu.VMEM)]*4,out_specs=(pl.BlockSpec(memory_space=pltpu.VMEM),)*2,
      scratch_shapes=[pltpu.VMEM((H,B,T),f32)],
      compiler_params=pltpu.CompilerParams(vmem_limit_bytes=48<<20))(q,k,v,first)

def bwd_kernel(q_ref,k_ref,v_ref,o_ref,g_ref,lse_ref,first_ref,dq_ref,dk_ref,dv_ref,dka,dva):
    nb=T//B
    dka[...]=jnp.zeros_like(dka); dva[...]=jnp.zeros_like(dva)
    def qblock(i,masked):
        r0=pl.multiple_of(i*B,B)
        q=q_ref[pl.ds(r0,B),:]; g=g_ref[pl.ds(r0,B),:]
        go=g.astype(f32)*o_ref[pl.ds(r0,B),:].astype(f32)
        hm=(lax.broadcasted_iota(jnp.int32,(8,W),1)//HD==lax.broadcasted_iota(jnp.int32,(8,W),0)).astype(f32)
        delta=lax.dot_general(hm,go,NT,precision=lax.Precision.HIGHEST,preferred_element_type=f32)
        lse=lse_ref[:,pl.ds(r0,B)]
        fst=first_ref[:,pl.ds(r0,B)]
        zero=jnp.zeros_like(q)
        qm=[jnp.where(lanemask(B,h),q,zero) for h in range(H)]
        gm=[jnp.where(lanemask(B,h),g,zero) for h in range(H)]
        kvi=lax.broadcasted_iota(jnp.int32,(B,B),0); qi=lax.broadcasted_iota(jnp.int32,(B,B),1)
        def tile(j,dq,diag):
            c0=pl.multiple_of(j*B,B)
            k=k_ref[pl.ds(c0,B),:]; v=v_ref[pl.ds(c0,B),:]
            dv=jnp.zeros((B,W),f32); dk=jnp.zeros((B,W),f32)
            for h in range(H):
                st=dg(k,qm[h],NT)
                p=jnp.exp2(st*C2-lse[h:h+1])
                if diag: p=jnp.where(kvi<=qi,p,0.0)
                if masked: p=jnp.where(kvi+c0>=fst,p,0.0)
                dp=dg(v,gm[h],NT)
                ds=(p*(dp-delta[h:h+1])).astype(bf)
                dv=dv+dg(p.astype(bf),gm[h],NN)
                dk=dk+dg(ds,qm[h],NN)
                km=jnp.where(lanemask(B,h),k,zero)
                dq=dq+dg(ds,km,TN)
            dva[pl.ds(c0,B),:]+=dv
            dka[pl.ds(c0,B),:]+=dk
            return dq
        dq=jnp.zeros((B,W),f32)
        dq=lax.fori_loop(0,i,lambda j,c:tile(j,c,False),dq)
        dq=tile(i,dq,True)
        dq_ref[pl.ds(r0,B),:]=(dq*0.125).astype(bf)
    def body(i,c): qblock(i,False); return c
    lax.fori_loop(0,6,body,0)
    def body2(i,c): qblock(i,True); return c
    lax.fori_loop(6,8,body2,0)
    dk_ref[...]=(dka[...]*0.125).astype(bf); dv_ref[...]=dva[...].astype(bf)
def bwd(q,k,v,o,g,lse,first):
    o1=jax.ShapeDtypeStruct((T,W),bf)
    return pl.pallas_call(bwd_kernel,out_shape=(o1,o1,o1),
      in_specs=[pl.BlockSpec(memory_space=pltpu.VMEM)]*7,out_specs=(pl.BlockSpec(memory_space=pltpu.VMEM),)*3,
      scratch_shapes=[pltpu.VMEM((T,W),f32)]*2,
      compiler_params=pltpu.CompilerParams(vmem_limit_bytes=48<<20))(q,k,v,o,g,lse,first)


def matmul(left, right):
    return jnp.dot(left, right, preferred_element_type=jnp.float32)


def left_times(left, right):
    return lax.dot_general(
        left, right, (((0,), (0,)), ((), ())), preferred_element_type=jnp.float32
    )


def right_times(left, right):
    return lax.dot_general(
        left, right, (((1,), (1,)), ((), ())), preferred_element_type=jnp.float32
    )


def norm_forward(values, gain, bias):
    center = values - jnp.mean(values, axis=-1, keepdims=True)
    scaled = lax.rsqrt(jnp.mean(center * center, axis=-1, keepdims=True) + EPS)
    unit = center * scaled
    return (unit * gain + bias, unit, scaled)


def norm_backward(upstream, unit, scaled, gain):
    along = upstream * gain
    inner = (
        along
        - jnp.mean(along, axis=-1, keepdims=True)
        - unit * jnp.mean(along * unit, axis=-1, keepdims=True)
    )
    return (inner * scaled, jnp.sum(upstream * unit, axis=0), jnp.sum(upstream, axis=0))


def gelu_slope(values):
    return (
        0.5 * (1.0 + lax.erf(values * SQRT_HALF))
        + values * jnp.exp(-0.5 * values * values) * INV_ROOT_TWO_PI
    )


def softmax_rows(scores):
    top = jnp.max(scores, axis=-1, keepdims=True)
    expo = jnp.exp(scores - top)
    total = jnp.sum(expo, axis=-1, keepdims=True)
    return (expo / total, top[..., 0] + jnp.log(total[..., 0]))


def shards(
    frames_in,
    text_states,
    clip_lengths,
    self_gain,
    self_bias,
    query_weight,
    key_weight,
    value_weight,
    output_weight,
    cross_gain,
    cross_bias,
    cross_query,
    cross_key,
    cross_value,
    cross_output,
    feed_gain,
    feed_bias,
    feed_upward,
    feed_downward,
    grad_out,
):
    count = lax.axis_size("seq")
    place = lax.axis_index("seq")
    local = frames_in.shape[1]
    total_frames = local * count
    block = min(512, total_frames)
    blocks = total_frames // block
    scale = HD ** (-0.5)
    lengths = clip_lengths[0]
    slot = jnp.arange(CLIPS, dtype=jnp.int32)
    ends = jnp.sum(jnp.where(slot[None, :] <= slot[:, None], lengths[None, :], 0), axis=1)
    begins = ends - lengths
    slots = jnp.arange(CLIPS, dtype=jnp.int32)
    positions = jnp.arange(total_frames, dtype=jnp.int32)
    owner_all = jnp.sum((ends[None, :] <= positions[:, None]).astype(jnp.int32), axis=1)
    first_all = jnp.sum(jnp.where(owner_all[:, None] == slots[None, :], begins[None, :], 0), axis=1)
    owner_mine = lax.dynamic_slice_in_dim(owner_all, place * local, local, 0)
    frames = frames_in[0].astype(jnp.float32)
    text = text_states[0]
    text_rows = text.shape[0]
    normed, unit_one, scale_one = norm_forward(frames, self_gain, self_bias)
    normed_low = normed.astype(jnp.bfloat16)
    query = matmul(normed_low, query_weight).astype(jnp.bfloat16)
    keys = matmul(normed_low, key_weight).astype(jnp.bfloat16)
    values = matmul(normed_low, value_weight).astype(jnp.bfloat16)
    query_heads, key_heads, value_heads = (
        lax.all_to_all(query, "seq", split_axis=1, concat_axis=0, tiled=True),
        lax.all_to_all(keys, "seq", split_axis=1, concat_axis=0, tiled=True),
        lax.all_to_all(values, "seq", split_axis=1, concat_axis=0, tiled=True),
    )
    width = query_heads.shape[1]
    heads_local = width // HD
    keys_split = key_heads.reshape(total_frames, heads_local, HD)
    values_split = value_heads.reshape(total_frames, heads_local, HD)

    attended, log_totals = fwd(query_heads, key_heads, value_heads, first_all[:, None])
    attended_frames = lax.all_to_all(attended, "seq", split_axis=0, concat_axis=1, tiled=True)
    after_self = frames + matmul(attended_frames, output_weight)
    normed_two, unit_two, scale_two = norm_forward(after_self, cross_gain, cross_bias)
    normed_two_low = normed_two.astype(jnp.bfloat16)
    cross_q = matmul(normed_two_low, cross_query).astype(jnp.bfloat16)
    cross_k = matmul(text, cross_key).astype(jnp.bfloat16)
    cross_v = matmul(text, cross_value).astype(jnp.bfloat16)
    cq_split = cross_q.reshape(local, HEADS, HD)
    ck_split = cross_k.reshape(text_rows, HEADS, HD)
    cv_split = cross_v.reshape(text_rows, HEADS, HD)
    key_clip = jnp.arange(text_rows, dtype=jnp.int32) // TEXT
    cross_allowed = owner_mine[:, None] == key_clip[None, :]
    cross_scores = (
        jnp.einsum("qhe,khe->hqk", cq_split, ck_split, preferred_element_type=jnp.float32) * scale
    )
    cross_probs, cross_log = softmax_rows(jnp.where(cross_allowed[None], cross_scores, NEG))
    cross_mixed = (
        jnp.einsum(
            "hqk,khe->qhe",
            cross_probs.astype(jnp.bfloat16),
            cv_split,
            preferred_element_type=jnp.float32,
        )
        .reshape(local, D)
        .astype(jnp.bfloat16)
    )
    after_cross = after_self + matmul(cross_mixed, cross_output)
    normed_three, unit_three, scale_three = norm_forward(after_cross, feed_gain, feed_bias)
    normed_three_low = normed_three.astype(jnp.bfloat16)
    hidden = matmul(normed_three_low, feed_upward)
    active = jax.nn.gelu(hidden, approximate=False).astype(jnp.bfloat16)
    output = after_cross + matmul(active, feed_downward)
    upstream = grad_out[0].astype(jnp.float32)
    upstream_low = upstream.astype(jnp.bfloat16)
    grad_down = left_times(active, upstream_low)
    grad_active = right_times(upstream_low, feed_downward)
    grad_hidden = (grad_active * gelu_slope(hidden)).astype(jnp.bfloat16)
    grad_up = left_times(normed_three_low, grad_hidden)
    grad_normed_three = right_times(grad_hidden, feed_upward)
    back_three, grad_feed_gain, grad_feed_bias = norm_backward(
        grad_normed_three, unit_three, scale_three, feed_gain
    )
    grad_cross = upstream + back_three
    grad_cross_low = grad_cross.astype(jnp.bfloat16)
    grad_cross_out = left_times(cross_mixed, grad_cross_low)
    grad_mixed = (
        right_times(grad_cross_low, cross_output).astype(jnp.bfloat16).reshape(local, HEADS, HD)
    )
    grad_cross_probs = jnp.einsum(
        "qhe,khe->hqk", grad_mixed, cv_split, preferred_element_type=jnp.float32
    )
    value_part = jnp.einsum(
        "hqk,qhe->khe",
        cross_probs.astype(jnp.bfloat16),
        grad_mixed,
        preferred_element_type=jnp.float32,
    ).reshape(text_rows, D)
    inner_cross = jnp.sum(cross_probs * grad_cross_probs, axis=-1, keepdims=True)
    grad_cross_scores = (cross_probs * (grad_cross_probs - inner_cross)).astype(jnp.bfloat16)
    grad_query_cross = (
        (
            jnp.einsum(
                "hqk,khe->qhe", grad_cross_scores, ck_split, preferred_element_type=jnp.float32
            )
            * scale
        )
        .reshape(local, D)
        .astype(jnp.bfloat16)
    )
    key_part = (
        jnp.einsum("hqk,qhe->khe", grad_cross_scores, cq_split, preferred_element_type=jnp.float32)
        * scale
    ).reshape(text_rows, D)
    key_total, value_total = (
        lax.psum(key_part.astype(jnp.bfloat16), "seq").astype(jnp.float32),
        lax.psum(value_part.astype(jnp.bfloat16), "seq").astype(jnp.float32),
    )
    key_low = key_total.astype(jnp.bfloat16)
    value_low = value_total.astype(jnp.bfloat16)
    text_grad = right_times(key_low, cross_key) + right_times(value_low, cross_value)
    share = text_rows // count
    text_share = lax.dynamic_slice_in_dim(text, place * share, share, 0)
    grad_cross_key = left_times(
        text_share, lax.dynamic_slice_in_dim(key_low, place * share, share, 0)
    )
    grad_cross_value = left_times(
        text_share, lax.dynamic_slice_in_dim(value_low, place * share, share, 0)
    )
    grad_cross_query = left_times(normed_two_low, grad_query_cross)
    grad_normed_two = right_times(grad_query_cross, cross_query)
    back_two, grad_cross_gain, grad_cross_bias = norm_backward(
        grad_normed_two, unit_two, scale_two, cross_gain
    )
    grad_self = grad_cross + back_two
    grad_self_low = grad_self.astype(jnp.bfloat16)
    grad_output_w = left_times(attended_frames, grad_self_low)
    grad_attended = right_times(grad_self_low, output_weight).astype(jnp.bfloat16)
    grad_heads = lax.all_to_all(grad_attended, "seq", split_axis=1, concat_axis=0, tiled=True)

    grad_query_heads, grad_key_heads, grad_value_heads = bwd(
        query_heads, key_heads, value_heads, attended, grad_heads, log_totals, first_all[None]
    )
    grad_query, grad_key, grad_value = (
        lax.all_to_all(grad_query_heads, "seq", split_axis=0, concat_axis=1, tiled=True),
        lax.all_to_all(grad_key_heads, "seq", split_axis=0, concat_axis=1, tiled=True),
        lax.all_to_all(grad_value_heads, "seq", split_axis=0, concat_axis=1, tiled=True),
    )
    grad_query_w = left_times(normed_low, grad_query)
    grad_key_w = left_times(normed_low, grad_key)
    grad_value_w = left_times(normed_low, grad_value)
    grad_normed = (
        right_times(grad_query, query_weight)
        + right_times(grad_key, key_weight)
        + right_times(grad_value, value_weight)
    )
    back_one, grad_self_gain, grad_self_bias = norm_backward(
        grad_normed, unit_one, scale_one, self_gain
    )
    frames_grad = grad_self + back_one
    def reduce_matrix(part):
        part = lax.psum_scatter(part.astype(bf), "clip", scatter_dimension=0, tiled=True)
        return lax.psum(part, "seq").astype(f32)

    vectors = lax.psum(jnp.stack([grad_self_gain, grad_self_bias, grad_cross_gain, grad_cross_bias, grad_feed_gain, grad_feed_bias]), ("clip", "seq"))
    width_out = vectors.shape[1] // lax.axis_size("clip")
    vectors = lax.dynamic_slice_in_dim(vectors, lax.axis_index("clip") * width_out, width_out, 1)
    summed = (
        vectors[0],
        vectors[1],
        reduce_matrix(grad_query_w),
        reduce_matrix(grad_key_w),
        reduce_matrix(grad_value_w),
        reduce_matrix(grad_output_w),
        vectors[2],
        vectors[3],
        reduce_matrix(grad_cross_query),
        reduce_matrix(grad_cross_key),
        reduce_matrix(grad_cross_value),
        reduce_matrix(grad_cross_out),
        vectors[4],
        vectors[5],
        reduce_matrix(grad_up),
        reduce_matrix(grad_down),
    )
    return (
        output.astype(jnp.bfloat16)[None],
        frames_grad[None],
        text_grad[None],
        summed[0],
        summed[1],
        summed[2],
        summed[3],
        summed[4],
        summed[5],
        summed[6],
        summed[7],
        summed[8],
        summed[9],
        summed[10],
        summed[11],
        summed[12],
        summed[13],
        summed[14],
        summed[15],
    )


def solution(mesh):
    return jax.shard_map(
        shards,
        mesh=mesh,
        in_specs=(
            P("clip", "seq", None),
            P("clip", None, None),
            P("clip", None),
            P(),
            P(),
            P(),
            P(),
            P(),
            P(),
            P(),
            P(),
            P(),
            P(),
            P(),
            P(),
            P(),
            P(),
            P(),
            P(),
            P("clip", "seq", None),
        ),
        out_specs=(
            P("clip", "seq", None),
            P("clip", "seq", None),
            P("clip", None, None),
            P("clip"),
            P("clip"),
            P("clip", None),
            P("clip", None),
            P("clip", None),
            P("clip", None),
            P("clip"),
            P("clip"),
            P("clip", None),
            P("clip", None),
            P("clip", None),
            P("clip", None),
            P("clip"),
            P("clip"),
            P("clip", None),
            P("clip", None),
        ),
        check_vma=False,
    )
```

```python
import functools
import math

import jax
import jax.numpy as jnp
from jax import lax
from jax.experimental import pallas as pl
from jax.experimental.pallas import tpu as pltpu
from jax.sharding import PartitionSpec as P

D = 1024
HEADS = 16
HD = 64
TEXT = 64
CLIPS = 4


EPS = 1e-05
NEG = -1e30
SQRT_HALF = 0.7071067811865476
INV_ROOT_TWO_PI = 0.3989422804014327

bf = jnp.bfloat16
f32 = jnp.float32
T, W, H, B = 2048, 256, 4, 256
C2 = math.log2(math.e) / 8.0
NT = (((1,), (1,)), ((), ()))
NN = (((1,), (0,)), ((), ()))
TN = (((0,), (0,)), ((), ()))


def dg(a, b, d):
    return lax.dot_general(a, b, d, preferred_element_type=f32)


def lanemask(rows,h):
    l=lax.broadcasted_iota(jnp.int32,(rows,W),1)
    return (l//HD)==h
def fwd_kernel(q_ref,k_ref,v_ref,first_ref,o_ref,lse_ref,s_ref):
    nb=T//B
    def qblock(i,masked):
        r0=pl.multiple_of(i*B,B)
        q=q_ref[pl.ds(r0,B),:]
        row=lax.broadcasted_iota(jnp.int32,(B,B),0); col=lax.broadcasted_iota(jnp.int32,(B,B),1)
        qm=[jnp.where(lanemask(B,h),q,jnp.zeros_like(q)) for h in range(H)]
        fst=first_ref[pl.ds(r0,B),:]
        def scores(j,carry,diag):
            c0=pl.multiple_of(j*B,B)
            k=k_ref[pl.ds(c0,B),:]
            out=[]
            for h in range(H):
                s=dg(qm[h],k,NT)
                if diag: s=jnp.where(col<=row,s,NEG)
                if masked: s=jnp.where(col+c0>=fst,s,NEG)
                s_ref[h,:,pl.ds(c0,B)]=s
                m=jnp.maximum(s[:,:128],s[:,128:])
                out.append(jnp.maximum(carry[h],m))
            return tuple(out)
        m=tuple(jnp.full((B,128),NEG,f32) for _ in range(H))
        m=lax.fori_loop(0,i,lambda j,c:scores(j,c,False),m)
        m=scores(i,m,True)
        m=[jnp.max(x,axis=1,keepdims=True) for x in m]
        def mix(j,carry):
            acc,ls=carry
            c0=pl.multiple_of(j*B,B)
            v=v_ref[pl.ds(c0,B),:]
            acc=list(acc); ls=list(ls)
            for h in range(H):
                p=jnp.exp2((s_ref[h,:,pl.ds(c0,B)]-m[h])*C2)
                ls[h]=ls[h]+p[:,:128]+p[:,128:]
                acc[h]=acc[h]+dg(p.astype(bf),v,NN)
            return tuple(acc),tuple(ls)
        acc,ls=lax.fori_loop(0,i+1,mix,(tuple(jnp.zeros((B,W),f32) for _ in range(H)),tuple(jnp.zeros((B,128),f32) for _ in range(H))))
        o=jnp.zeros((B,W),f32)
        lane=lax.broadcasted_iota(jnp.int32,(B,128),1)
        lse=jnp.zeros((B,128),f32)
        for h in range(H):
            l=jnp.sum(ls[h],axis=1,keepdims=True)
            o=jnp.where(lanemask(B,h),acc[h]/l,o)
            lse=jnp.where(lane==h,m[h]*C2+jnp.log2(l),lse)
        o_ref[pl.ds(r0,B),:]=o.astype(bf)
        lse_ref[:,pl.ds(r0,B)]=lse.T[:8]
    def body(i,c): qblock(i,False); return c
    lax.fori_loop(0,6,body,0)
    def body2(i,c): qblock(i,True); return c
    lax.fori_loop(6,8,body2,0)
def fwd(q,k,v,first):
    return pl.pallas_call(fwd_kernel,out_shape=(jax.ShapeDtypeStruct((T,W),bf),jax.ShapeDtypeStruct((8,T),f32)),
      in_specs=[pl.BlockSpec(memory_space=pltpu.VMEM)]*4,out_specs=(pl.BlockSpec(memory_space=pltpu.VMEM),)*2,
      scratch_shapes=[pltpu.VMEM((H,B,T),f32)],
      compiler_params=pltpu.CompilerParams(vmem_limit_bytes=48<<20))(q,k,v,first)

def add_blocks(out, ins, rows, cols):
    step = max(16, min(rows, 65536 // cols))

    def body(i, carry):
        r = pl.ds(pl.multiple_of(i * step, 16), step)
        total = ins[0][r, :].astype(f32)
        for one in ins[1:]:
            total = total + one[r, :].astype(f32)
        out[r, :] = total.astype(bf)
        return carry

    lax.fori_loop(0, rows // step, body, 0)


class Job:
    def __init__(self, order, part, own, bufs, sems, out, env):
        self.order, self.part, self.own, self.out, self.env = order, part, own, out, env
        self.r0, self.r1, self.r2 = bufs
        self.sems = sems
        self.pairs, self.rb, self.n = self.r0.shape
        self.q = self.n if order == "own" else self.n // env["seqs"]

    def sem(self, stage, k):
        return dict(send_sem=self.sems.at[0, stage, k], recv_sem=self.sems.at[1, stage, k])

    def copy(self, stage, k, src, dst, **where):
        return pltpu.make_async_remote_copy(
            src_ref=src, dst_ref=dst, device_id=where, device_id_type=pl.DeviceIdType.MESH, **self.sem(stage, k)
        )

    def cores(self):
        e = self.env
        return [
            self.copy(0, 0, self.part.at[:, 1 - e["c"]], self.r0, clip=2 * e["z"] + 1 - e["c"])
        ]

    def own_copy(self, p):
        return pltpu.make_async_copy(
            self.part.at[p, self.env["c"]], self.own.at[p % 2], self.sems.at[0, 4, p % 2]
        )

    def columns(self, s):
        return pl.ds(pl.multiple_of(s * self.q, 128), self.q)

    def seq(self):
        e, copies = self.env, []
        for k in range(1, e["seqs"]):
            to = lax.rem(e["s"] + k, e["seqs"])
            if self.order == "xy":
                src, dst = self.r0.at[:, :, self.columns(to)], self.r1.at[k - 1]
            else:
                src, dst = self.r1.at[0, :, self.columns(to)], self.r2.at[k - 1]
            copies.append(self.copy(1, k - 1, src, dst, seq=to))
        return copies

    def across(self):
        e, copies = self.env, []
        for k in range(1, self.pairs):
            to = lax.rem(e["z"] + k, self.pairs)
            if self.order == "xy":
                src, dst = self.r1.at[0, to], self.r2.at[k - 1]
            elif self.order == "z":
                src, dst = self.r0.at[to], self.r1.at[k - 1]
            else:
                src, dst = self.r0.at[to], self.r2.at[k - 1]
            copies.append(self.copy(2, k - 1, src, dst, clip=2 * to + e["c"]))
        return copies

    def gather(self):
        e, copies = self.env, []
        for k in range(1, e["seqs"]):
            to = lax.rem(e["s"] + k, e["seqs"])
            copies.append(
                self.copy(3, k - 1, self.r2.at[0], self.out.at[:, self.columns(e["s"])], seq=to)
            )
        return copies

    def keep(self):
        return pltpu.make_async_copy(
            self.r2.at[0], self.out.at[:, self.columns(self.env["s"])], self.sems.at[1, 4, 0]
        )

    def sum_cores(self):
        if self.own is None:
            for p in range(self.pairs):
                mine = self.part.at[p, self.env["c"]]
                add_blocks(self.r0.at[p], [self.r0.at[p], mine], self.rb, self.n)
            return
        self.own_copy(0).start()
        for p in range(self.pairs):
            if p + 1 < self.pairs:
                self.own_copy(p + 1).start()
            self.own_copy(p).wait()
            add_blocks(self.r0.at[p], [self.r0.at[p], self.own.at[p % 2]], self.rb, self.n)

    def sum_seq(self):
        e = self.env
        others = range(e["seqs"] - 1)
        if self.order == "xy":
            for p in range(self.pairs):
                mine = self.r0.at[p, :, self.columns(e["s"])]
                add_blocks(self.r1.at[0, p], [mine] + [self.r1.at[k, p] for k in others], self.rb, self.q)
        else:
            mine = self.r1.at[0, :, self.columns(e["s"])]
            add_blocks(self.r2.at[0], [mine] + [self.r2.at[k] for k in others], self.rb, self.q)

    def sum_across(self):
        e = self.env
        others = range(self.pairs - 1)
        if self.order == "xy":
            add_blocks(self.r2.at[0], [self.r1.at[0, e["z"]]] + [self.r2.at[k] for k in others], self.rb, self.q)
        elif self.order == "z":
            add_blocks(self.r1.at[0], [self.r0.at[e["z"]]] + [self.r1.at[k] for k in others], self.rb, self.n)
        else:
            add_blocks(self.r2.at[0], [self.r0.at[e["z"]]] + [self.r2.at[k] for k in others], self.rb, self.q)


def start(copies):
    for one in copies:
        one.start()


def arrive(copies):
    for one in copies:
        one.wait_recv()


def finish(copies):
    for one in copies:
        one.wait_send()


def job_bufs(order, pairs, rb, n, seqs):
    q = n if order == "own" else n // seqs
    r0 = pltpu.VMEM((pairs, rb, n), bf)
    if order == "xy":
        return [r0, pltpu.VMEM((seqs - 1, pairs, rb, q), bf), pltpu.VMEM((pairs - 1, rb, q), bf)]
    if order == "z":
        return [r0, pltpu.VMEM((pairs - 1, rb, n), bf), pltpu.VMEM((seqs - 1, rb, q), bf)]
    return [r0, pltpu.VMEM((8, 128), bf), pltpu.VMEM((pairs - 1, rb, q), bf)]

LAST = pl.DeviceIdType.MESH


def kc_kernel(seqs, pairs, *refs):
    (q_ref, k_ref, v_ref, o_ref, g_ref, lse_ref, first_ref, n1_hbm, *parts) = refs[:15]
    dq_f, dk_f, dv_f, *outs = refs[15:28]
    dq_s, dk_s, dv_s, dka, dva, n1_buf, wacc, own_up, own_down, own_one, wparts, *rest = refs[28:]
    sems, push_send, push_recv, local_sem = rest[-4:]
    bufs = rest[:-4]
    s = lax.axis_index("seq")
    b = lax.axis_index("clip")
    c, z = lax.rem(b, 2), lax.div(b, 2)
    env = dict(seqs=seqs, s=s, c=c, z=z)
    frames = T // seqs

    barrier = pltpu.get_barrier_semaphore()
    count = 1
    pl.semaphore_signal(barrier, inc=1, device_id={"clip": 2 * z + 1 - c}, device_id_type=LAST)
    for k in range(1, seqs):
        pl.semaphore_signal(barrier, inc=1, device_id={"seq": lax.rem(s + k, seqs)}, device_id_type=LAST)
        count += 1
    for k in range(1, pairs):
        pl.semaphore_signal(
            barrier, inc=1, device_id={"clip": 2 * lax.rem(z + k, pairs) + c}, device_id_type=LAST
        )
        count += 1
    pl.semaphore_wait(barrier, count)

    orders = ("xy", "z", "xy", "xy", "xy", "own", "own", "own", "own", "own")
    owns = (own_up, own_down) + (own_one,) * 3 + (None,) * 5
    jobs = []
    for t, order in enumerate(orders):
        src = parts[t] if t < 7 else wparts.at[t - 7]
        jobs.append(Job(order, src, owns[t], bufs[3 * t : 3 * t + 3], sems.at[t], outs[t], env))
    up, down, go, gcq, gco, gxk, gxv, gq, gk, gv = jobs
    early = [down, up, go, gcq, gco, gxk, gxv]
    for one in early:
        start(one.cores())
    n1_copy = pltpu.make_async_copy(n1_hbm, n1_buf, local_sem.at[0])
    n1_copy.start()

    dka[...] = jnp.zeros_like(dka)
    dva[...] = jnp.zeros_like(dva)

    def qblock(i, masked):
        r0 = pl.multiple_of(i * B, B)
        q = q_ref[pl.ds(r0, B), :]
        g = g_ref[pl.ds(r0, B), :]
        go_ = g.astype(f32) * o_ref[pl.ds(r0, B), :].astype(f32)
        hm = (
            lax.broadcasted_iota(jnp.int32, (8, W), 1) // HD == lax.broadcasted_iota(jnp.int32, (8, W), 0)
        ).astype(f32)
        delta = lax.dot_general(hm, go_, NT, precision=lax.Precision.HIGHEST, preferred_element_type=f32)
        lse = lse_ref[:, pl.ds(r0, B)]
        fst = first_ref[:, pl.ds(r0, B)]
        zero = jnp.zeros_like(q)
        qm = [jnp.where(lanemask(B, h), q, zero) for h in range(H)]
        gm = [jnp.where(lanemask(B, h), g, zero) for h in range(H)]
        kvi = lax.broadcasted_iota(jnp.int32, (B, B), 0)
        qi = lax.broadcasted_iota(jnp.int32, (B, B), 1)

        def tile(j, dq, diag):
            c0 = pl.multiple_of(j * B, B)
            k = k_ref[pl.ds(c0, B), :]
            v = v_ref[pl.ds(c0, B), :]
            dv = jnp.zeros((B, W), f32)
            dk = jnp.zeros((B, W), f32)
            for h in range(H):
                st = dg(k, qm[h], NT)
                p = jnp.exp2(st * C2 - lse[h : h + 1])
                if diag:
                    p = jnp.where(kvi <= qi, p, 0.0)
                if masked:
                    p = jnp.where(kvi + c0 >= fst, p, 0.0)
                dp = dg(v, gm[h], NT)
                ds = (p * (dp - delta[h : h + 1])).astype(bf)
                dv = dv + dg(p.astype(bf), gm[h], NN)
                dk = dk + dg(ds, qm[h], NN)
                km = jnp.where(lanemask(B, h), k, zero)
                dq = dq + dg(ds, km, TN)
            dva[pl.ds(c0, B), :] += dv
            dka[pl.ds(c0, B), :] += dk
            return dq

        dq = jnp.zeros((B, W), f32)
        dq = lax.fori_loop(0, i, lambda j, x: tile(j, x, False), dq)
        dq = tile(i, dq, True)
        dq_s[pl.ds(r0, B), :] = (dq * 0.125).astype(bf)
        dk_s[pl.ds(r0, B), :] = (dka[pl.ds(r0, B), :] * 0.125).astype(bf)
        dv_s[pl.ds(r0, B), :] = dva[pl.ds(r0, B), :].astype(bf)

    lanes = pl.ds(pl.multiple_of(s * W, 128), W)

    def pushes(owner):
        k = lax.rem(owner - s + seqs, seqs)
        rows = pl.ds(owner * frames, frames)
        return [
            pltpu.make_async_remote_copy(
                src_ref=src.at[rows, :],
                dst_ref=dst.at[:, lanes],
                send_sem=push_send.at[n, owner],
                recv_sem=push_recv.at[n, k],
                device_id={"seq": owner},
                device_id_type=LAST,
            )
            for n, (src, dst) in enumerate(((dq_s, dq_f), (dk_s, dk_f), (dv_s, dv_f)))
        ]

    def keeps(owner):
        rows = pl.ds(owner * frames, frames)
        return [
            pltpu.make_async_copy(src.at[rows, :], dst.at[:, lanes], push_send.at[n, owner])
            for n, (src, dst) in enumerate(((dq_s, dq_f), (dk_s, dk_f), (dv_s, dv_f)))
        ]

    per = frames // B
    for owner in reversed(range(seqs)):
        def block(n, x, owner=owner):
            qblock(owner * per + per - 1 - n, (owner + 1) * frames > TAIL)
            return x
        lax.fori_loop(0, per, block, 0)

        @pl.when(s != owner)
        def _():
            start(pushes(owner))

        @pl.when(s == owner)
        def _():
            start(keeps(owner))

        if owner == seqs - 1:
            arrive(down.cores())
            down.sum_cores()
            start(down.across())
            arrive(up.cores())
            up.sum_cores()
            start(up.seq())
            for one in (go, gcq, gco):
                arrive(one.cores())
                one.sum_cores()
                start(one.seq())
            for one in (gxk, gxv):
                arrive(one.cores())
                one.sum_cores()
                start(one.across())

    n1_copy.wait()
    for n, src in enumerate((dq_s, dk_s, dv_s)):
        def product(r, x, src=src):
            rows = pl.ds(pl.multiple_of(r * B, B), B)
            add = dg(n1_buf[rows, :], src[rows, :], TN)
            wacc[...] = jnp.where(r == 0, add, wacc[...] + add)
            return x
        lax.fori_loop(0, T // B, product, 0)
        rb = gq.rb
        for p in range(pairs):
            for cc in range(2):
                wparts[n, p, cc] = wacc[pl.ds((2 * p + cc) * rb, rb), :].astype(bf)
        start((gq, gk, gv)[n].cores())

    for one in (gxk, gxv):
        arrive(one.across())
        one.sum_across()
        start(one.gather())
        one.keep().start()
    for one in (gq, gk, gv):
        arrive(one.cores())
        one.sum_cores()
        start(one.across())
    arrive(up.seq())
    up.sum_seq()
    start(up.across())
    for one in (go, gcq, gco):
        arrive(one.seq())
        one.sum_seq()
        start(one.across())
    arrive(down.across())
    down.sum_across()
    start(down.seq())
    for one in (gq, gk, gv, up, go, gcq, gco):
        arrive(one.across())
        one.sum_across()
        start(one.gather())
        one.keep().start()
    arrive(down.seq())
    down.sum_seq()
    start(down.gather())
    down.keep().start()

    for owner in range(seqs):
        @pl.when(s != owner)
        def _():
            finish(pushes(owner))

        @pl.when(s == owner)
        def _():
            for one in keeps(owner):
                one.wait()
    for k in range(1, seqs):
        for n, dst in enumerate((dq_f, dk_f, dv_f)):
            pltpu.make_async_copy(
                dst.at[:, pl.ds(pl.multiple_of(lax.rem(s - k + seqs, seqs) * W, 128), W)],
                dst.at[:, pl.ds(pl.multiple_of(lax.rem(s - k + seqs, seqs) * W, 128), W)],
                push_recv.at[n, k],
            ).wait()
    for one in jobs:
        finish(one.cores())
        if one.order != "own":
            finish(one.seq())
        finish(one.across())
        finish(one.gather())
        one.keep().wait()
        arrive(one.gather())


TAIL = 1536


def kc(seqs, clips, q, k, v, o, g, lse, first, n1_all, parts):
    pairs = clips // 2
    split = []
    for one in parts:
        rows, cols = one.shape
        split.append(one.reshape(pairs, 2, rows // clips, cols))
    orders = ("xy", "z", "xy", "xy", "xy", "own", "own", "own", "own", "own")
    shapes = [p.shape for p in split] + [(pairs, 2, D // clips, W)] * 3
    bufs = []
    for order, (_, _, rb, n) in zip(orders, shapes):
        bufs += job_bufs(order, pairs, rb, n, seqs)
    widths = [n if order != "own" else n * seqs for order, (_, _, _, n) in zip(orders, shapes)]
    outs = [jax.ShapeDtypeStruct((T // seqs, D), bf)] * 3 + [
        jax.ShapeDtypeStruct((shape[2], n), bf) for shape, n in zip(shapes, widths)
    ]
    hbm = pl.BlockSpec(memory_space=pl.ANY)
    vmem = pl.BlockSpec(memory_space=pltpu.VMEM)
    rb = D // clips
    most = max(seqs, pairs)
    return pl.pallas_call(
        functools.partial(kc_kernel, seqs, pairs),
        out_shape=outs,
        in_specs=[vmem] * 7 + [hbm] + [hbm] * 5 + [vmem] * 2,
        out_specs=[hbm] * 13,
        scratch_shapes=[pltpu.VMEM((T, W), bf)] * 3
        + [pltpu.VMEM((T, W), f32)] * 2
        + [
            pltpu.VMEM((T, D), bf),
            pltpu.VMEM((D, W), f32),
            pltpu.VMEM((2,) + shapes[0][2:], bf),
            pltpu.VMEM((2,) + shapes[1][2:], bf),
            pltpu.VMEM((2, rb, D), bf),
            pltpu.VMEM((3, pairs, 2, rb, W), bf),
        ]
        + bufs
        + [
            pltpu.SemaphoreType.DMA((10, 2, 5, most)),
            pltpu.SemaphoreType.DMA((3, seqs)),
            pltpu.SemaphoreType.DMA((3, seqs)),
            pltpu.SemaphoreType.DMA((1,)),
        ],
        compiler_params=pltpu.CompilerParams(
            collective_id=1, has_side_effects=True, vmem_limit_bytes=60 * 2**20
        ),
    )(q, k, v, o, g, lse, first, n1_all, *split)


def matmul(left, right):
    return jnp.dot(left, right, preferred_element_type=jnp.float32)


def left_times(left, right):
    return lax.dot_general(
        left, right, (((0,), (0,)), ((), ())), preferred_element_type=jnp.float32
    )


def right_times(left, right):
    return lax.dot_general(
        left, right, (((1,), (1,)), ((), ())), preferred_element_type=jnp.float32
    )


def norm_forward(values, gain, bias):
    center = values - jnp.mean(values, axis=-1, keepdims=True)
    scaled = lax.rsqrt(jnp.mean(center * center, axis=-1, keepdims=True) + EPS)
    unit = center * scaled
    return (unit * gain + bias, unit, scaled)


def norm_backward(upstream, unit, scaled, gain):
    along = upstream * gain
    inner = (
        along
        - jnp.mean(along, axis=-1, keepdims=True)
        - unit * jnp.mean(along * unit, axis=-1, keepdims=True)
    )
    return (inner * scaled, jnp.sum(upstream * unit, axis=0), jnp.sum(upstream, axis=0))


def gelu_slope(values):
    return (
        0.5 * (1.0 + lax.erf(values * SQRT_HALF))
        + values * jnp.exp(-0.5 * values * values) * INV_ROOT_TWO_PI
    )


def softmax_rows(scores):
    top = jnp.max(scores, axis=-1, keepdims=True)
    expo = jnp.exp(scores - top)
    total = jnp.sum(expo, axis=-1, keepdims=True)
    return (expo / total, top[..., 0] + jnp.log(total[..., 0]))


def shards(
    frames_in,
    text_states,
    clip_lengths,
    self_gain,
    self_bias,
    query_weight,
    key_weight,
    value_weight,
    output_weight,
    cross_gain,
    cross_bias,
    cross_query,
    cross_key,
    cross_value,
    cross_output,
    feed_gain,
    feed_bias,
    feed_upward,
    feed_downward,
    grad_out,
):
    count = lax.axis_size("seq")
    place = lax.axis_index("seq")
    local = frames_in.shape[1]
    total_frames = local * count
    block = min(512, total_frames)
    blocks = total_frames // block
    scale = HD ** (-0.5)
    lengths = clip_lengths[0]
    slot = jnp.arange(CLIPS, dtype=jnp.int32)
    ends = jnp.sum(jnp.where(slot[None, :] <= slot[:, None], lengths[None, :], 0), axis=1)
    begins = ends - lengths
    slots = jnp.arange(CLIPS, dtype=jnp.int32)
    positions = jnp.arange(total_frames, dtype=jnp.int32)
    owner_all = jnp.sum((ends[None, :] <= positions[:, None]).astype(jnp.int32), axis=1)
    first_all = jnp.sum(jnp.where(owner_all[:, None] == slots[None, :], begins[None, :], 0), axis=1)
    owner_mine = lax.dynamic_slice_in_dim(owner_all, place * local, local, 0)
    frames = frames_in[0].astype(jnp.float32)
    text = text_states[0]
    text_rows = text.shape[0]
    normed, unit_one, scale_one = norm_forward(frames, self_gain, self_bias)
    normed_low = normed.astype(jnp.bfloat16)
    normed_all = lax.all_gather(normed_low, "seq", axis=0, tiled=True)
    query = matmul(normed_low, query_weight).astype(jnp.bfloat16)
    keys = matmul(normed_low, key_weight).astype(jnp.bfloat16)
    values = matmul(normed_low, value_weight).astype(jnp.bfloat16)
    query_heads, key_heads, value_heads = (
        lax.all_to_all(query, "seq", split_axis=1, concat_axis=0, tiled=True),
        lax.all_to_all(keys, "seq", split_axis=1, concat_axis=0, tiled=True),
        lax.all_to_all(values, "seq", split_axis=1, concat_axis=0, tiled=True),
    )
    width = query_heads.shape[1]
    heads_local = width // HD
    keys_split = key_heads.reshape(total_frames, heads_local, HD)
    values_split = value_heads.reshape(total_frames, heads_local, HD)

    attended, log_totals = fwd(query_heads, key_heads, value_heads, first_all[:, None])
    attended_frames = lax.all_to_all(attended, "seq", split_axis=0, concat_axis=1, tiled=True)
    after_self = frames + matmul(attended_frames, output_weight)
    normed_two, unit_two, scale_two = norm_forward(after_self, cross_gain, cross_bias)
    normed_two_low = normed_two.astype(jnp.bfloat16)
    cross_q = matmul(normed_two_low, cross_query).astype(jnp.bfloat16)
    cross_k = matmul(text, cross_key).astype(jnp.bfloat16)
    cross_v = matmul(text, cross_value).astype(jnp.bfloat16)
    cq_split = cross_q.reshape(local, HEADS, HD)
    ck_split = cross_k.reshape(text_rows, HEADS, HD)
    cv_split = cross_v.reshape(text_rows, HEADS, HD)
    key_clip = jnp.arange(text_rows, dtype=jnp.int32) // TEXT
    cross_allowed = owner_mine[:, None] == key_clip[None, :]
    cross_scores = (
        jnp.einsum("qhe,khe->hqk", cq_split, ck_split, preferred_element_type=jnp.float32) * scale
    )
    cross_probs, cross_log = softmax_rows(jnp.where(cross_allowed[None], cross_scores, NEG))
    cross_mixed = (
        jnp.einsum(
            "hqk,khe->qhe",
            cross_probs.astype(jnp.bfloat16),
            cv_split,
            preferred_element_type=jnp.float32,
        )
        .reshape(local, D)
        .astype(jnp.bfloat16)
    )
    after_cross = after_self + matmul(cross_mixed, cross_output)
    normed_three, unit_three, scale_three = norm_forward(after_cross, feed_gain, feed_bias)
    normed_three_low = normed_three.astype(jnp.bfloat16)
    hidden = matmul(normed_three_low, feed_upward)
    active = jax.nn.gelu(hidden, approximate=False).astype(jnp.bfloat16)
    output = after_cross + matmul(active, feed_downward)
    upstream = grad_out[0].astype(jnp.float32)
    upstream_low = upstream.astype(jnp.bfloat16)
    grad_down = left_times(active, upstream_low)
    grad_active = right_times(upstream_low, feed_downward)
    grad_hidden = (grad_active * gelu_slope(hidden)).astype(jnp.bfloat16)
    grad_up = left_times(normed_three_low, grad_hidden)
    grad_normed_three = right_times(grad_hidden, feed_upward)
    back_three, grad_feed_gain, grad_feed_bias = norm_backward(
        grad_normed_three, unit_three, scale_three, feed_gain
    )
    grad_cross = upstream + back_three
    grad_cross_low = grad_cross.astype(jnp.bfloat16)
    grad_cross_out = left_times(cross_mixed, grad_cross_low)
    grad_mixed = (
        right_times(grad_cross_low, cross_output).astype(jnp.bfloat16).reshape(local, HEADS, HD)
    )
    grad_cross_probs = jnp.einsum(
        "qhe,khe->hqk", grad_mixed, cv_split, preferred_element_type=jnp.float32
    )
    value_part = jnp.einsum(
        "hqk,qhe->khe",
        cross_probs.astype(jnp.bfloat16),
        grad_mixed,
        preferred_element_type=jnp.float32,
    ).reshape(text_rows, D)
    inner_cross = jnp.sum(cross_probs * grad_cross_probs, axis=-1, keepdims=True)
    grad_cross_scores = (cross_probs * (grad_cross_probs - inner_cross)).astype(jnp.bfloat16)
    grad_query_cross = (
        (
            jnp.einsum(
                "hqk,khe->qhe", grad_cross_scores, ck_split, preferred_element_type=jnp.float32
            )
            * scale
        )
        .reshape(local, D)
        .astype(jnp.bfloat16)
    )
    key_part = (
        jnp.einsum("hqk,qhe->khe", grad_cross_scores, cq_split, preferred_element_type=jnp.float32)
        * scale
    ).reshape(text_rows, D)
    key_total, value_total = (
        lax.psum(key_part.astype(jnp.bfloat16), "seq").astype(jnp.float32),
        lax.psum(value_part.astype(jnp.bfloat16), "seq").astype(jnp.float32),
    )
    key_low = key_total.astype(jnp.bfloat16)
    value_low = value_total.astype(jnp.bfloat16)
    text_grad = right_times(key_low, cross_key) + right_times(value_low, cross_value)
    share = D // count
    grad_cross_key = left_times(text, lax.dynamic_slice_in_dim(key_low, place * share, share, 1))
    grad_cross_value = left_times(text, lax.dynamic_slice_in_dim(value_low, place * share, share, 1))
    grad_cross_query = left_times(normed_two_low, grad_query_cross)
    grad_normed_two = right_times(grad_query_cross, cross_query)
    back_two, grad_cross_gain, grad_cross_bias = norm_backward(
        grad_normed_two, unit_two, scale_two, cross_gain
    )
    grad_self = grad_cross + back_two
    grad_self_low = grad_self.astype(jnp.bfloat16)
    grad_output_w = left_times(attended_frames, grad_self_low)
    grad_attended = right_times(grad_self_low, output_weight).astype(jnp.bfloat16)
    grad_heads = lax.all_to_all(grad_attended, "seq", split_axis=1, concat_axis=0, tiled=True)

    grad_query, grad_key, grad_value, *mats = kc(
        count,
        lax.axis_size("clip"),
        query_heads,
        key_heads,
        value_heads,
        attended,
        grad_heads,
        log_totals,
        first_all[None],
        normed_all,
        [
            one.astype(bf)
            for one in (
                grad_up,
                grad_down,
                grad_output_w,
                grad_cross_query,
                grad_cross_out,
                grad_cross_key,
                grad_cross_value,
            )
        ],
    )
    w_up, w_down, w_o, w_cq, w_co, w_xk, w_xv, w_q, w_k, w_v = [one.astype(f32) for one in mats]
    grad_normed = (
        right_times(grad_query, query_weight)
        + right_times(grad_key, key_weight)
        + right_times(grad_value, value_weight)
    )
    back_one, grad_self_gain, grad_self_bias = norm_backward(
        grad_normed, unit_one, scale_one, self_gain
    )
    frames_grad = grad_self + back_one
    vectors = lax.psum(jnp.stack([grad_self_gain, grad_self_bias, grad_cross_gain, grad_cross_bias, grad_feed_gain, grad_feed_bias]), ("clip", "seq"))
    width_out = vectors.shape[1] // lax.axis_size("clip")
    vectors = lax.dynamic_slice_in_dim(vectors, lax.axis_index("clip") * width_out, width_out, 1)
    summed = (
        vectors[0],
        vectors[1],
        w_q,
        w_k,
        w_v,
        w_o,
        vectors[2],
        vectors[3],
        w_cq,
        w_xk,
        w_xv,
        w_co,
        vectors[4],
        vectors[5],
        w_up,
        w_down,
    )
    return (
        output.astype(jnp.bfloat16)[None],
        frames_grad[None],
        text_grad[None],
        summed[0],
        summed[1],
        summed[2],
        summed[3],
        summed[4],
        summed[5],
        summed[6],
        summed[7],
        summed[8],
        summed[9],
        summed[10],
        summed[11],
        summed[12],
        summed[13],
        summed[14],
        summed[15],
    )


def solution(mesh):
    return jax.shard_map(
        shards,
        mesh=mesh,
        in_specs=(
            P("clip", "seq", None),
            P("clip", None, None),
            P("clip", None),
            P(),
            P(),
            P(),
            P(),
            P(),
            P(),
            P(),
            P(),
            P(),
            P(),
            P(),
            P(),
            P(),
            P(),
            P(),
            P(),
            P("clip", "seq", None),
        ),
        out_specs=(
            P("clip", "seq", None),
            P("clip", "seq", None),
            P("clip", None, None),
            P("clip"),
            P("clip"),
            P("clip", None),
            P("clip", None),
            P("clip", None),
            P("clip", None),
            P("clip"),
            P("clip"),
            P("clip", None),
            P("clip", None),
            P("clip", None),
            P("clip", None),
            P("clip"),
            P("clip"),
            P("clip", None),
            P("clip", None),
        ),
        check_vma=False,
    )
```

```python
import functools
import math

import jax
import jax.numpy as jnp
from jax import lax
from jax.experimental import pallas as pl
from jax.experimental.pallas import tpu as pltpu
from jax.sharding import PartitionSpec as P

D = 1024
HEADS = 16
HD = 64
TEXT = 64
CLIPS = 4


EPS = 1e-05
NEG = -1e30
SQRT_HALF = 0.7071067811865476
INV_ROOT_TWO_PI = 0.3989422804014327

bf = jnp.bfloat16
f32 = jnp.float32
T, W, H, B = 2048, 256, 4, 256
LOG2E = math.log2(math.e)
C2 = LOG2E / 8.0
NT = (((1,), (1,)), ((), ()))
NN = (((1,), (0,)), ((), ()))
TN = (((0,), (0,)), ((), ()))


def dg(a, b, d):
    return lax.dot_general(a, b, d, preferred_element_type=f32)


def lanemask(rows,h):
    l=lax.broadcasted_iota(jnp.int32,(rows,W),1)
    return (l//HD)==h
def fwd_kernel(q_ref,k_ref,v_ref,first_ref,o_ref,lse_ref,s_ref):
    nb=T//B
    def qblock(i,masked):
        r0=pl.multiple_of(i*B,B)
        q=q_ref[pl.ds(r0,B),:]
        row=lax.broadcasted_iota(jnp.int32,(B,B),0); col=lax.broadcasted_iota(jnp.int32,(B,B),1)
        qm=[jnp.where(lanemask(B,h),q,jnp.zeros_like(q)) for h in range(H)]
        fst=first_ref[pl.ds(r0,B),:]
        def scores(j,carry,diag):
            c0=pl.multiple_of(j*B,B)
            k=k_ref[pl.ds(c0,B),:]
            out=[]
            for h in range(H):
                s=dg(qm[h],k,NT)
                if diag: s=jnp.where(col<=row,s,NEG)
                if masked: s=jnp.where(col+c0>=fst,s,NEG)
                s_ref[h,:,pl.ds(c0,B)]=s
                m=jnp.maximum(s[:,:128],s[:,128:])
                out.append(jnp.maximum(carry[h],m))
            return tuple(out)
        m=tuple(jnp.full((B,128),NEG,f32) for _ in range(H))
        m=lax.fori_loop(0,i,lambda j,c:scores(j,c,False),m)
        m=scores(i,m,True)
        m=[jnp.max(x,axis=1,keepdims=True) for x in m]
        def mix(j,carry):
            acc,ls=carry
            c0=pl.multiple_of(j*B,B)
            v=v_ref[pl.ds(c0,B),:]
            acc=list(acc); ls=list(ls)
            for h in range(H):
                p=jnp.exp2((s_ref[h,:,pl.ds(c0,B)]-m[h])*C2)
                ls[h]=ls[h]+p[:,:128]+p[:,128:]
                acc[h]=acc[h]+dg(p.astype(bf),v,NN)
            return tuple(acc),tuple(ls)
        acc,ls=lax.fori_loop(0,i+1,mix,(tuple(jnp.zeros((B,W),f32) for _ in range(H)),tuple(jnp.zeros((B,128),f32) for _ in range(H))))
        o=jnp.zeros((B,W),f32)
        lane=lax.broadcasted_iota(jnp.int32,(B,128),1)
        lse=jnp.zeros((B,128),f32)
        for h in range(H):
            l=jnp.sum(ls[h],axis=1,keepdims=True)
            o=jnp.where(lanemask(B,h),acc[h]/l,o)
            lse=jnp.where(lane==h,m[h]*C2+jnp.log2(l),lse)
        o_ref[pl.ds(r0,B),:]=o.astype(bf)
        lse_ref[:,pl.ds(r0,B)]=lse.T[:8]
    def body(i,c): qblock(i,False); return c
    lax.fori_loop(0,6,body,0)
    def body2(i,c): qblock(i,True); return c
    lax.fori_loop(6,8,body2,0)
def fwd(q,k,v,first):
    return pl.pallas_call(fwd_kernel,out_shape=(jax.ShapeDtypeStruct((T,W),bf),jax.ShapeDtypeStruct((8,T),f32)),
      in_specs=[pl.BlockSpec(memory_space=pltpu.VMEM)]*4,out_specs=(pl.BlockSpec(memory_space=pltpu.VMEM),)*2,
      scratch_shapes=[pltpu.VMEM((H,B,T),f32)],
      compiler_params=pltpu.CompilerParams(vmem_limit_bytes=48<<20))(q,k,v,first)

def add_blocks(out, ins, rows, cols):
    step = max(16, min(rows, 65536 // cols))

    def body(i, carry):
        r = pl.ds(pl.multiple_of(i * step, 16), step)
        total = ins[0][r, :].astype(f32)
        for one in ins[1:]:
            total = total + one[r, :].astype(f32)
        out[r, :] = total.astype(bf)
        return carry

    lax.fori_loop(0, rows // step, body, 0)


def each(count, fn):
    def body(i, x):
        fn(i)
        return x

    lax.fori_loop(0, count, body, 0)


def tile_of(i, size=256):
    return pl.ds(pl.multiple_of(i * size, size), size)


def unit_rows(v):
    center = v - jnp.mean(v, axis=-1, keepdims=True)
    scaled = lax.rsqrt(jnp.mean(center * center, axis=-1, keepdims=True) + EPS)
    return center * scaled, scaled


def norm_rows(src, gain, bias, dst, rows):
    def chunk(i):
        r = tile_of(i, 64)
        unit, _ = unit_rows(src[r, :])
        dst[r, :] = (unit * gain[...] + bias[...]).astype(bf)

    each(rows // 64, chunk)


def norm_back_rows(up, src, gain, add, dst, dst_low, rows):
    def chunk(i, sums):
        r = tile_of(i, 64)
        unit, scaled = unit_rows(src[r, :])
        u = up[r, :]
        along = u * gain[...]
        inner = (
            along
            - jnp.mean(along, axis=-1, keepdims=True)
            - unit * jnp.mean(along * unit, axis=-1, keepdims=True)
        )
        total = add[r, :].astype(f32) + inner * scaled
        dst[r, :] = total
        dst_low[r, :] = total.astype(bf)
        fold = lambda v: jnp.sum(v.reshape(8, 8, v.shape[1]), axis=0)
        return sums[0] + fold(u * unit), sums[1] + fold(u)

    zero = jnp.zeros((8, src.shape[1]), f32)
    a, b = lax.fori_loop(0, rows // 64, chunk, (zero, zero))
    return jnp.sum(a, axis=0, keepdims=True), jnp.sum(b, axis=0, keepdims=True)


def remote(src, dst, send, recv, **where):
    return pltpu.make_async_remote_copy(
        src_ref=src, dst_ref=dst, send_sem=send, recv_sem=recv, device_id=where,
        device_id_type=pl.DeviceIdType.MESH,
    )


def greet(env, pairs):
    s, c, z, seqs = env["s"], env["c"], env["z"], env["seqs"]
    barrier = pltpu.get_barrier_semaphore()
    count = 1
    pl.semaphore_signal(
        barrier, inc=1, device_id={"clip": 2 * z + 1 - c}, device_id_type=pl.DeviceIdType.MESH
    )
    for k in range(1, seqs):
        pl.semaphore_signal(
            barrier, inc=1, device_id={"seq": lax.rem(s + k, seqs)}, device_id_type=pl.DeviceIdType.MESH
        )
        count += 1
    for k in range(1, pairs):
        pl.semaphore_signal(
            barrier, inc=1, device_id={"clip": 2 * lax.rem(z + k, pairs) + c},
            device_id_type=pl.DeviceIdType.MESH,
        )
        count += 1
    pl.semaphore_wait(barrier, count)


def place(seqs):
    b = lax.axis_index("clip")
    return dict(seqs=seqs, s=lax.axis_index("seq"), c=lax.rem(b, 2), z=lax.div(b, 2))


def kb_kernel(seqs, *refs):
    (
        att, x_ref, gb, ck, cv, owner, g2, b2, g3, b3,
        w_o, w_cq, w_co, w_up, w_dn, n1_hbm,
    ) = refs[:16]
    (x1, fo, vec, c_up, c_dn, c_o, c_cq, c_co, heads, n1_all, kq, vq) = refs[16:28]
    (
        ring, up_st, dn_st, up_rv, dn_rv, sq_rv, x2, n2, n3, n3t, cq, co, probs, u, ut, dh,
        acc, dn3, dck, dcv, kv_low, kv_rv, ring_sem, st_send, st_recv, out_sem, n1_sem, head_sem, kv_sem,
        own_sem,
    ) = refs[28:]
    env = place(seqs)
    s, c, z = env["s"], env["c"], env["z"]
    rows, d = x_ref.shape
    pairs, rb = up_rv.shape[0], up_rv.shape[1]
    ppc, rbd = dn_st.shape[0], dn_st.shape[2]
    steps = w_up.shape[1] // d
    width = d // seqs
    texts = ck.shape[0]
    depth = ring.shape[0]

    items = [w_o, w_cq, w_co]
    for t in range(steps):
        items += [w_up.at[:, pl.ds(t * d, d)], w_dn.at[pl.ds(t * d, d), :]]
    items += [w_co, w_cq, w_o]

    def load(i):
        return pltpu.make_async_copy(items[i], ring.at[i % depth], ring_sem.at[i % depth])

    def take(i):
        load(i).wait()
        return ring.at[i % depth]

    def drop(i):
        if i + depth < len(items):
            load(i + depth).start()

    for i in range(depth):
        load(i).start()
    greet(env, 1)

    peers = [(k, lax.rem(s + k, seqs)) for k in range(1, seqs)]
    spots = pl.ds(pl.multiple_of(s * rows, rows), rows)
    n1_out = [
        remote(n1_hbm, n1_all.at[spots, :], n1_sem.at[0, k], n1_sem.at[1, k], seq=to) for k, to in peers
    ]
    n1_own = pltpu.make_async_copy(n1_hbm, n1_all.at[spots, :], n1_sem.at[0, 0])
    start(n1_out)
    n1_own.start()

    w = take(0)

    def f(t):
        x1[:, tile_of(t)] = x_ref[:, tile_of(t)].astype(f32) + dg(att[...], w[:, tile_of(t)], NN)

    each(d // 256, f)
    drop(0)
    norm_rows(x1, g2, b2, n2, rows)
    w = take(1)

    def f(t):
        cq[:, tile_of(t)] = dg(n2[...], w[:, tile_of(t)], NN).astype(bf)

    each(d // 256, f)
    drop(1)
    half = 256
    key_clip = lax.broadcasted_iota(jnp.int32, (half, texts), 1) // TEXT

    def masked(v, h):
        lane = lax.broadcasted_iota(jnp.int32, v.shape, 1)
        return jnp.where(lane // HD == h, v, jnp.zeros_like(v))

    def f(n):
        t, r = lax.div(n, rows // half), tile_of(lax.rem(n, rows // half), half)
        allowed = owner[r, :] == key_clip
        q, k, v = cq[r, tile_of(t)], ck[:, tile_of(t)], cv[:, tile_of(t)]
        total = jnp.zeros((half, 256), f32)
        for h in range(256 // HD):
            sc = jnp.where(allowed, dg(masked(q, h), k, NT), NEG)
            p = jnp.exp2((sc - jnp.max(sc, axis=-1, keepdims=True)) * C2)
            p = (p / jnp.sum(p, axis=-1, keepdims=True)).astype(bf)
            probs[t * (256 // HD) + h, r, :] = p
            total = total + dg(p, masked(v, h), NN)
        co[r, tile_of(t)] = total.astype(bf)

    each(d // 256 * (rows // half), f)
    w = take(2)

    def f(t):
        x2[:, tile_of(t)] = x1[:, tile_of(t)] + dg(co[...], w[:, tile_of(t)], NN)

    each(d // 256, f)
    drop(2)
    norm_rows(x2, g3, b3, n3, rows)

    def turn(src, dst):
        def f(t):
            dst[tile_of(t), :] = src[:, tile_of(t)].T

        each(d // 256, f)

    turn(n3, n3t)

    def swap(n, src, dst):
        return remote(src, dst, st_send.at[n], st_recv.at[n], clip=2 * z + 1 - c)

    def up_swap(t):
        return swap(2 * t, up_st.at[0, :, 1 - c], up_rv.at[:, :, pl.ds(t * d, d)])

    def dn_swap(t):
        return swap(2 * t + 1, dn_st.at[:, 1 - c], dn_rv.at[pl.ds(t * ppc, ppc)])

    def up_out(t):
        cols = pl.ds(t * d, d)
        return pltpu.make_async_copy(up_rv.at[:, :, cols], c_up.at[:, :, cols], out_sem.at[2 * t])

    def dn_out(t):
        blocks = pl.ds(t * ppc, ppc)
        return pltpu.make_async_copy(dn_rv.at[blocks], c_dn.at[blocks], out_sem.at[2 * t + 1])

    def settle(t):
        one = up_swap(t)
        one.wait_recv()
        for p in range(pairs):
            dst = up_rv.at[p, :, pl.ds(t * d, d)]
            add_blocks(dst, [dst, up_st.at[0, p, c]], rb, d)
        one.wait_send()
        up_out(t).start()
        one = dn_swap(t)
        one.wait_recv()
        for p in range(ppc):
            dst = dn_rv.at[t * ppc + p]
            add_blocks(dst, [dst, dn_st.at[p, c]], rbd, d)
        one.wait_send()
        dn_out(t).start()

    for t in range(steps):
        wu, wd = take(3 + 2 * t), take(4 + 2 * t)

        def f(i):
            h = dg(n3[...], wu[:, tile_of(i)], NN)
            du = dg(gb[...], wd[tile_of(i), :], NT)
            part = 0.5 * (1.0 + lax.erf(h * SQRT_HALF))
            slope = part + h * jnp.exp2(h * h * (-0.5 * LOG2E)) * INV_ROOT_TWO_PI
            dh[:, tile_of(i)] = (du * slope).astype(bf)
            act = (h * part).astype(bf)
            u[:, tile_of(i)] = act
            ut[tile_of(i), :] = act.T

        each(d // 256, f)
        if t > 0:
            settle(t - 1)

        def f(i, t=t):
            a = dg(u[...], wd[:, tile_of(i)], NN)
            b = dg(dh[...], wu[tile_of(i), :], NT)
            if t == 0:
                acc[:, tile_of(i)] = a
                dn3[:, tile_of(i)] = b
            else:
                acc[:, tile_of(i)] += a
                dn3[:, tile_of(i)] += b
            g = dg(n3t[...], dh[:, tile_of(i)], NN).astype(bf)
            up_st[0, :, :, :, tile_of(i)] = g.reshape(pairs, 2, rb, 256)
            g = dg(ut[...], gb[:, tile_of(i)], NN).astype(bf)
            dn_st[:, :, :, tile_of(i)] = g.reshape(ppc, 2, rbd, 256)

        each(d // 256, f)
        drop(3 + 2 * t)
        drop(4 + 2 * t)
        up_swap(t).start()
        dn_swap(t).start()

    def f(i):
        r = tile_of(i, 64)
        fo[r, :] = (x2[r, :] + acc[r, :]).astype(bf)

    each(rows // 64, f)
    base = 3 + 2 * steps
    low = u
    sums = norm_back_rows(dn3, x2, g3, gb, acc, low, rows)
    vec[2:3, :], vec[3:4, :] = sums
    w = take(base)
    dco = dh

    def f(t):
        dco[:, tile_of(t)] = dg(low[...], w[tile_of(t), :], NT).astype(bf)

    each(d // 256, f)
    drop(base)
    settle(steps - 1)

    def grad(n, slot, a, low):
        turn(a, n3t)

        def f(t):
            g = dg(n3t[...], low[:, tile_of(t)], NN).astype(bf)
            up_st[slot, :, :, :, tile_of(t)] = g.reshape(pairs, 2, rb, 256)

        each(d // 256, f)
        grad_swap(n, slot).start()

    def grad_swap(n, slot):
        return swap(2 * steps + n, up_st.at[slot, :, 1 - c], sq_rv.at[n])

    def grad_out(n):
        return pltpu.make_async_copy(sq_rv.at[n], (c_co, c_cq, c_o)[n], out_sem.at[2 * steps + n])

    def grad_settle(n, slot):
        one = grad_swap(n, slot)
        one.wait_recv()
        for p in range(pairs):
            add_blocks(sq_rv.at[n, p], [sq_rv.at[n, p], up_st.at[slot, p, c]], rb, d)
        one.wait_send()
        grad_out(n).start()

    grad(0, 0, co, low)
    dcq = n3

    def f(t):
        k, v = ck[:, tile_of(t)], cv[:, tile_of(t)]
        sum_k = jnp.zeros((texts, 256), f32)
        sum_v = jnp.zeros((texts, 256), f32)
        for n in range(rows // half):
            r = pl.ds(n * half, half)
            q, g = cq[r, tile_of(t)], dco[r, tile_of(t)]
            out = jnp.zeros((half, 256), f32)
            for h in range(256 // HD):
                p_low = probs[t * (256 // HD) + h, r, :]
                p = p_low.astype(f32)
                dp = dg(masked(g, h), v, NT)
                inner = jnp.sum(p * dp, axis=-1, keepdims=True)
                ds = (p * (dp - inner)).astype(bf)
                out = out + dg(ds, masked(k, h), NN)
                sum_k = sum_k + dg(ds, masked(q, h), TN)
                sum_v = sum_v + dg(p_low, masked(g, h), TN)
            dcq[r, tile_of(t)] = (out * 0.125).astype(bf)
        kv_low[0, :, tile_of(t)] = (sum_k * 0.125).astype(bf)
        kv_low[1, :, tile_of(t)] = sum_v.astype(bf)

    each(d // 256, f)
    mine = pl.ds(pl.multiple_of(s * width, 128), width)
    kv_out = [
        remote(
            kv_low.at[:, :, pl.ds(pl.multiple_of(to * width, 128), width)], kv_rv.at[k - 1],
            kv_sem.at[0, k], kv_sem.at[1, k], seq=to,
        )
        for k, to in peers
    ]
    start(kv_out)
    w = take(base + 1)
    dn2 = dn3

    def f(t):
        dn2[:, tile_of(t)] = dg(dcq[...], w[tile_of(t), :], NT)

    each(d // 256, f)
    drop(base + 1)
    sums = norm_back_rows(dn2, x1, g2, acc, x1, low, rows)
    vec[0:1, :], vec[1:2, :] = sums
    vec[4:8, :] = jnp.zeros((4, d), f32)
    w = take(base + 2)
    do = dh

    def f(t):
        do[:, tile_of(t)] = dg(low[...], w[tile_of(t), :], NT).astype(bf)

    each(d // 256, f)
    head_out = [
        remote(
            do.at[:, pl.ds(pl.multiple_of(to * width, 128), width)], heads.at[spots, :],
            head_sem.at[0, k], head_sem.at[1, k], seq=to,
        )
        for k, to in peers
    ]
    head_own = pltpu.make_async_copy(do.at[:, mine], heads.at[spots, :], head_sem.at[0, 0])
    start(head_out)
    head_own.start()
    grad(1, 1, n2, dcq)
    grad_settle(0, 0)
    grad(2, 0, att, low)
    grad_settle(1, 1)
    arrive(kv_out)
    for n, dst in enumerate((kq, vq)):
        total = kv_low[n, :, mine].astype(f32)
        for k in range(1, seqs):
            total = total + kv_rv[k - 1, n].astype(f32)
        dst[...] = total.astype(bf)
    grad_settle(2, 0)
    finish(kv_out)
    head_own.wait()
    n1_own.wait()
    for one in head_out + n1_out:
        one.wait()
    for t in range(steps):
        up_out(t).wait()
        dn_out(t).wait()
    for n in range(3):
        grad_out(n).wait()


def kb(seqs, clips, att, x, gb, ck, cv, owner, g2, b2, g3, b3, w_o, w_cq, w_co, w_up, w_dn, n1):
    rows, d = x.shape
    pairs = clips // 2
    rb, rbd = d // clips, w_dn.shape[0] // clips
    steps = w_up.shape[1] // d
    ppc = pairs // steps
    texts = ck.shape[0]
    width = d // seqs
    hbm = pl.BlockSpec(memory_space=pl.ANY)
    vmem = pl.BlockSpec(memory_space=pltpu.VMEM)
    low = lambda *shape: pltpu.VMEM(shape, bf)
    full = lambda *shape: pltpu.VMEM(shape, f32)
    s_low = lambda *shape: jax.ShapeDtypeStruct(shape, bf)
    dma = pltpu.SemaphoreType.DMA
    return pl.pallas_call(
        functools.partial(kb_kernel, seqs),
        out_shape=[
            jax.ShapeDtypeStruct((rows, d), f32),
            s_low(rows, d),
            jax.ShapeDtypeStruct((8, d), f32),
            s_low(pairs, rb, steps * d),
            s_low(pairs, rbd, d),
            s_low(pairs, rb, d),
            s_low(pairs, rb, d),
            s_low(pairs, rb, d),
            s_low(rows * seqs, width),
            s_low(rows * seqs, d),
            s_low(texts, width),
            s_low(texts, width),
        ],
        in_specs=[vmem] * 10 + [hbm] * 6,
        out_specs=[vmem] * 3 + [hbm] * 7 + [vmem] * 2,
        scratch_shapes=[
            low(4, d, d),
            low(2, pairs, 2, rb, d),
            low(ppc, 2, rbd, d),
            low(pairs, rb, steps * d),
            low(pairs, rbd, d),
            low(3, pairs, rb, d),
            full(rows, d),
            low(rows, d),
            low(rows, d),
            low(d, rows),
            low(rows, d),
            low(rows, d),
            low(d // HD, rows, texts),
            low(rows, d),
            low(d, rows),
            low(rows, d),
            full(rows, d),
            full(rows, d),
            full(8, 128),
            full(8, 128),
            low(2, texts, d),
            low(seqs - 1, 2, texts, width),
            dma((4,)),
            dma((2 * steps + 3,)),
            dma((2 * steps + 3,)),
            dma((2 * steps + 3,)),
            dma((2, seqs)),
            dma((2, seqs)),
            dma((2, seqs)),
            dma((1,)),
        ],
        compiler_params=pltpu.CompilerParams(
            collective_id=2, has_side_effects=True, vmem_limit_bytes=60 * 2**20
        ),
    )(
        att, x, gb, ck, cv, owner[:, None],
        *[v[None] for v in (g2, b2, g3, b3)],
        w_o, w_cq, w_co, w_up, w_dn, n1,
    )


class Job:
    def __init__(self, order, part, bufs, sems, out, env, pairs):
        self.order, self.part, self.out, self.env, self.pairs = order, part, out, env, pairs
        self.r0, self.r1, self.r2 = bufs
        self.sems = sems
        self.rb, self.n = part.shape[-2:]
        self.q = self.n if order == "own" else self.n // env["seqs"]

    def copy(self, stage, k, src, dst, **where):
        return remote(src, dst, self.sems.at[0, stage, k], self.sems.at[1, stage, k], **where)

    def cores(self):
        e = self.env
        return [
            self.copy(0, 0, self.part.at[:, 1 - e["c"]], self.r0, clip=2 * e["z"] + 1 - e["c"])
        ]

    def mine(self):
        src = self.part.at[:, :, self.columns(self.env["s"])] if self.order == "xy" else self.part.at[self.env["z"]]
        return pltpu.make_async_copy(src, self.r0, self.sems.at[0, 4, 0])

    def columns(self, s):
        return pl.ds(pl.multiple_of(s * self.q, 128), self.q)

    def seq(self):
        e, copies = self.env, []
        for k in range(1, e["seqs"]):
            to = lax.rem(e["s"] + k, e["seqs"])
            if self.order == "xy":
                src, dst = self.part.at[:, :, self.columns(to)], self.r1.at[k - 1]
            else:
                src, dst = self.r1.at[0, :, self.columns(to)], self.r2.at[k - 1]
            copies.append(self.copy(1, k - 1, src, dst, seq=to))
        return copies

    def across(self):
        e, copies = self.env, []
        for k in range(1, self.pairs):
            to = lax.rem(e["z"] + k, self.pairs)
            if self.order == "xy":
                src, dst = self.r1.at[0, to], self.r2.at[k - 1]
            elif self.order == "z":
                src, dst = self.part.at[to], self.r1.at[k - 1]
            else:
                src, dst = self.r0.at[to], self.r2.at[k - 1]
            copies.append(self.copy(2, k - 1, src, dst, clip=2 * to + e["c"]))
        return copies

    def gather(self):
        e, copies = self.env, []
        for k in range(1, e["seqs"]):
            to = lax.rem(e["s"] + k, e["seqs"])
            copies.append(
                self.copy(3, k - 1, self.r2.at[0], self.out.at[:, self.columns(e["s"])], seq=to)
            )
        return copies

    def keep(self):
        return pltpu.make_async_copy(
            self.r2.at[0], self.out.at[:, self.columns(self.env["s"])], self.sems.at[1, 4, 0]
        )

    def sum_cores(self):
        for p in range(self.pairs):
            add_blocks(self.r0.at[p], [self.r0.at[p], self.part.at[p, self.env["c"]]], self.rb, self.n)

    def sum_seq(self):
        others = range(self.env["seqs"] - 1)
        if self.order == "xy":
            self.mine().wait()
            for p in range(self.pairs):
                add_blocks(self.r1.at[0, p], [self.r0.at[p]] + [self.r1.at[k, p] for k in others], self.rb, self.q)
        else:
            mine = self.r1.at[0, :, self.columns(self.env["s"])]
            add_blocks(self.r2.at[0], [mine] + [self.r2.at[k] for k in others], self.rb, self.q)

    def sum_across(self):
        e = self.env
        others = range(self.pairs - 1)
        if self.order == "xy":
            add_blocks(self.r2.at[0], [self.r1.at[0, e["z"]]] + [self.r2.at[k] for k in others], self.rb, self.q)
        elif self.order == "z":
            self.mine().wait()
            add_blocks(self.r1.at[0], [self.r0] + [self.r1.at[k] for k in others], self.rb, self.n)
        else:
            add_blocks(self.r2.at[0], [self.r0.at[e["z"]]] + [self.r2.at[k] for k in others], self.rb, self.q)


def start(copies):
    for one in copies:
        one.start()


def arrive(copies):
    for one in copies:
        one.wait_recv()


def finish(copies):
    for one in copies:
        one.wait_send()


def job_bufs(order, pairs, rb, n, seqs):
    q = n if order == "own" else n // seqs
    low = lambda *shape: pltpu.VMEM(shape, bf)
    if order == "xy":
        return [low(pairs, rb, q), low(seqs - 1, pairs, rb, q), low(pairs - 1, rb, q)]
    if order == "z":
        return [low(rb, n), low(pairs - 1, rb, n), low(seqs - 1, rb, q)]
    return [low(pairs, rb, q), low(16, 128), low(pairs - 1, rb, q)]


LAST = pl.DeviceIdType.MESH


def kc_kernel(seqs, pairs, *refs):
    (q_ref, k_ref, v_ref, o_ref, g_ref, lse_ref, first_ref) = refs[:7]
    (kq, vq, text, x_ref, dx1, g1, vec_in, n1_hbm, w_q, w_k, w_v, *parts) = refs[7:23]
    (frames_grad, vec, k_all, v_all, *outs) = refs[23:37]
    dq_s, dk_s, dv_s, dka, dva, n1_buf, wacc, wparts, dqkv, w_buf, dn1, vec_rv, low_buf, *rest = refs[37:]
    sems, push_send, push_recv, local_sem, kv_sem, vec_sem = rest[-6:]
    bufs = rest[:-6]
    env = place(seqs)
    s, c, z = env["s"], env["c"], env["z"]
    frames = T // seqs
    d = n1_hbm.shape[1]
    greet(env, pairs)

    orders = ORDERS
    jobs = []
    for t, order in enumerate(orders):
        src = parts[t] if t < 5 else wparts.at[t - 5]
        jobs.append(Job(order, src, bufs[3 * t : 3 * t + 3], sems.at[t], outs[t], env, pairs))
    up, down, go, gcq, gco, gxk, gxv, gq, gk, gv = jobs
    start(down.across())
    start(up.seq())
    for one in (go, gcq, gco):
        start(one.seq())
    for one in (up, down, go, gcq, gco):
        one.mine().start()
    width = kq.shape[1]
    spot = pl.ds(pl.multiple_of(s * width, 128), width)
    kv_out, kv_own = [], []
    for n, (src, dst) in enumerate(((kq, k_all), (vq, v_all))):
        for k in range(1, seqs):
            kv_out.append(
                remote(src, dst.at[:, spot], kv_sem.at[0, n, k], kv_sem.at[1, n, k], seq=lax.rem(s + k, seqs))
            )
        kv_own.append(pltpu.make_async_copy(src, dst.at[:, spot], kv_sem.at[0, n, 0]))
    start(kv_out)
    start(kv_own)
    loads = [pltpu.make_async_copy(n1_hbm, n1_buf, local_sem.at[0])]
    for n, one in enumerate((w_q, w_k, w_v)):
        loads.append(pltpu.make_async_copy(one, w_buf.at[n], local_sem.at[1 + n]))
    start(loads)

    def place_product(n, rb):
        for p in range(pairs):
            for cc in range(2):
                wparts[n, p, cc] = wacc[pl.ds((2 * p + cc) * rb, rb), :].astype(bf)

    for n, src in enumerate((kq, vq)):
        wacc[...] = dg(text[...], src[...], TN)
        place_product(n, gxk.rb)
        start((gxk, gxv)[n].cores())

    dka[...] = jnp.zeros_like(dka)
    dva[...] = jnp.zeros_like(dva)

    def qblock(i, masked):
        r0 = pl.multiple_of(i * B, B)
        q = q_ref[pl.ds(r0, B), :]
        g = g_ref[pl.ds(r0, B), :]
        go_ = g.astype(f32) * o_ref[pl.ds(r0, B), :].astype(f32)
        hm = (
            lax.broadcasted_iota(jnp.int32, (8, W), 1) // HD == lax.broadcasted_iota(jnp.int32, (8, W), 0)
        ).astype(f32)
        delta = lax.dot_general(hm, go_, NT, precision=lax.Precision.HIGHEST, preferred_element_type=f32)
        lse = lse_ref[:, pl.ds(r0, B)]
        fst = first_ref[:, pl.ds(r0, B)]
        zero = jnp.zeros_like(q)
        qm = [jnp.where(lanemask(B, h), q, zero) for h in range(H)]
        gm = [jnp.where(lanemask(B, h), g, zero) for h in range(H)]
        kvi = lax.broadcasted_iota(jnp.int32, (B, B), 0)
        qi = lax.broadcasted_iota(jnp.int32, (B, B), 1)

        def tile(j, dq, diag):
            c0 = pl.multiple_of(j * B, B)
            k = k_ref[pl.ds(c0, B), :]
            v = v_ref[pl.ds(c0, B), :]
            dv = jnp.zeros((B, W), f32)
            dk = jnp.zeros((B, W), f32)
            for h in range(H):
                st = dg(k, qm[h], NT)
                p = jnp.exp2(st * C2 - lse[h : h + 1])
                if diag:
                    p = jnp.where(kvi <= qi, p, 0.0)
                if masked:
                    p = jnp.where(kvi + c0 >= fst, p, 0.0)
                dp = dg(v, gm[h], NT)
                ds = (p * (dp - delta[h : h + 1])).astype(bf)
                dv = dv + dg(p.astype(bf), gm[h], NN)
                dk = dk + dg(ds, qm[h], NN)
                km = jnp.where(lanemask(B, h), k, zero)
                dq = dq + dg(ds, km, TN)
            dva[pl.ds(c0, B), :] += dv
            dka[pl.ds(c0, B), :] += dk
            return dq

        dq = jnp.zeros((B, W), f32)
        dq = lax.fori_loop(0, i, lambda j, x: tile(j, x, False), dq)
        dq = tile(i, dq, True)
        dq_s[pl.ds(r0, B), :] = (dq * 0.125).astype(bf)
        dk_s[pl.ds(r0, B), :] = (dka[pl.ds(r0, B), :] * 0.125).astype(bf)
        dv_s[pl.ds(r0, B), :] = dva[pl.ds(r0, B), :].astype(bf)

    lanes = pl.ds(pl.multiple_of(s * W, 128), W)
    moved = [(src, dqkv.at[n]) for n, src in enumerate((dq_s, dk_s, dv_s))]

    def pushes(owner):
        k = lax.rem(owner - s + seqs, seqs)
        rows = pl.ds(owner * frames, frames)
        return [
            pltpu.make_async_remote_copy(
                src_ref=src.at[rows, :],
                dst_ref=dst.at[:, lanes],
                send_sem=push_send.at[n, owner],
                recv_sem=push_recv.at[n, k],
                device_id={"seq": owner},
                device_id_type=LAST,
            )
            for n, (src, dst) in enumerate(moved)
        ]

    def keeps(owner):
        rows = pl.ds(owner * frames, frames)
        return [
            pltpu.make_async_copy(src.at[rows, :], dst.at[:, lanes], push_send.at[n, owner])
            for n, (src, dst) in enumerate(moved)
        ]

    per = frames // B
    for owner in reversed(range(seqs)):
        def block(n, x, owner=owner):
            qblock(owner * per + per - 1 - n, (owner + 1) * frames > TAIL)
            return x
        lax.fori_loop(0, per, block, 0)

        @pl.when(s != owner)
        def _():
            start(pushes(owner))

        @pl.when(s == owner)
        def _():
            start(keeps(owner))

        if owner == seqs - 1:
            for one in (gxk, gxv):
                arrive(one.cores())
                one.sum_cores()
                start(one.across())

    loads[0].wait()
    for n, src in enumerate((dq_s, dk_s, dv_s)):
        def product(r, x, src=src):
            rows = pl.ds(pl.multiple_of(r * B, B), B)
            add = dg(n1_buf[rows, :], src[rows, :], TN)
            wacc[...] = jnp.where(r == 0, add, wacc[...] + add)
            return x
        lax.fori_loop(0, T // B, product, 0)
        place_product(2 + n, gq.rb)
        start((gq, gk, gv)[n].cores())

    for one in (gxk, gxv):
        arrive(one.across())
        one.sum_across()
        start(one.gather())
        one.keep().start()
    for one in (gq, gk, gv):
        arrive(one.cores())
        one.sum_cores()
        start(one.across())
    arrive(up.seq())
    up.sum_seq()
    start(up.across())
    for one in (go, gcq, gco):
        arrive(one.seq())
        one.sum_seq()
        start(one.across())

    for k in range(1, seqs):
        for n in range(3):
            dst = dqkv.at[n, :, pl.ds(pl.multiple_of(lax.rem(s - k + seqs, seqs) * W, 128), W)]
            pltpu.make_async_copy(dst, dst, push_recv.at[n, k]).wait()
    for owner in range(seqs):
        @pl.when(s != owner)
        def _():
            finish(pushes(owner))

        @pl.when(s == owner)
        def _():
            for one in keeps(owner):
                one.wait()
    for n in range(3):
        loads[1 + n].wait()

        def f(t, n=n):
            add = dg(dqkv[n], w_buf[n, tile_of(t), :], NT)
            if n == 0:
                dn1[:, tile_of(t)] = add
            else:
                dn1[:, tile_of(t)] += add

        each(d // 256, f)

    def f(i):
        r = tile_of(i, 64)
        wide_x[r, :] = x_ref[r, :].astype(f32)

    wide_x = frames_grad
    each(frames // 64, f)
    vec[...] = vec_in[...]
    sums = norm_back_rows(dn1, wide_x, g1, dx1, frames_grad, low_buf, frames)
    vec[4:5, :], vec[5:6, :] = sums
    swap = [remote(vec, vec_rv.at[0], vec_sem.at[0, 0, 0], vec_sem.at[1, 0, 0], clip=2 * z + 1 - c)]
    start(swap)

    arrive(down.across())
    down.sum_across()
    start(down.seq())
    arrive(swap)
    finish(swap)
    vec[...] = vec[...] + vec_rv[0]
    base = 1
    vec_rv[base + s] = vec[...]
    round_seq = [
        remote(vec, vec_rv.at[base + s], vec_sem.at[0, 1, k], vec_sem.at[1, 1, k], seq=lax.rem(s + k, seqs))
        for k in range(1, seqs)
    ]
    start(round_seq)
    for one in (gq, gk, gv, up, go, gcq, gco):
        arrive(one.across())
        one.sum_across()
        start(one.gather())
        one.keep().start()
    arrive(round_seq)
    finish(round_seq)
    total = vec_rv[base]
    for k in range(1, seqs):
        total = total + vec_rv[base + k]
    vec[...] = total
    base = 1 + seqs
    round_z = [
        remote(
            vec, vec_rv.at[base + k - 1], vec_sem.at[0, 2, k], vec_sem.at[1, 2, k],
            clip=2 * lax.rem(z + k, pairs) + c,
        )
        for k in range(1, pairs)
    ]
    start(round_z)
    arrive(down.seq())
    down.sum_seq()
    start(down.gather())
    down.keep().start()
    arrive(round_z)
    finish(round_z)
    total = vec[...]
    for k in range(1, pairs):
        total = total + vec_rv[base + k - 1]
    vec[...] = total

    for one in kv_out + kv_own:
        one.wait()
    for one in jobs:
        if one.order == "own":
            finish(one.cores())
        else:
            finish(one.seq())
        finish(one.across())
        finish(one.gather())
        one.keep().wait()
        arrive(one.gather())


ORDERS = ("xy", "z", "xy", "xy", "xy", "own", "own", "own", "own", "own")
TAIL = 1536


def kc(seqs, clips, heads, lse, first, kq, vq, text, x, dx1, g1, vec, n1_all, weights, parts):
    pairs = clips // 2
    rows, d = x.shape
    rb = d // clips
    shapes = [p.shape for p in parts] + [(pairs, 2, rb, W)] * 5
    bufs = []
    for order, shape in zip(ORDERS, shapes):
        bufs += job_bufs(order, pairs, shape[-2], shape[-1], seqs)
    outs = [
        jax.ShapeDtypeStruct((rows, d), f32),
        jax.ShapeDtypeStruct((8, d), f32),
        jax.ShapeDtypeStruct((text.shape[0], d), bf),
        jax.ShapeDtypeStruct((text.shape[0], d), bf),
    ]
    for order, shape in zip(ORDERS, shapes):
        outs.append(jax.ShapeDtypeStruct((shape[-2], shape[-1] * (seqs if order == "own" else 1)), bf))
    hbm = pl.BlockSpec(memory_space=pl.ANY)
    vmem = pl.BlockSpec(memory_space=pltpu.VMEM)
    most = max(seqs, pairs)
    dma = pltpu.SemaphoreType.DMA
    return pl.pallas_call(
        functools.partial(kc_kernel, seqs, pairs),
        out_shape=outs,
        in_specs=[vmem] * 14 + [hbm] * 9,
        out_specs=[vmem] * 2 + [hbm] * 12,
        scratch_shapes=[pltpu.VMEM((T, W), bf)] * 3
        + [pltpu.VMEM((T, W), f32)] * 2
        + [
            pltpu.VMEM((T, d), bf),
            pltpu.VMEM((d, W), f32),
            pltpu.VMEM((5, pairs, 2, rb, W), bf),
            pltpu.VMEM((3, rows, d), bf),
            pltpu.VMEM((3, d, d), bf),
            pltpu.VMEM((rows, d), f32),
            pltpu.VMEM((1 + seqs + pairs - 1, 8, d), f32),
            pltpu.VMEM((rows, d), bf),
        ]
        + bufs
        + [
            dma((10, 2, 5, most)),
            dma((3, seqs)),
            dma((3, seqs)),
            dma((4,)),
            dma((2, 2, seqs)),
            dma((2, 3, most)),
        ],
        compiler_params=pltpu.CompilerParams(
            collective_id=1, has_side_effects=True, vmem_limit_bytes=60 * 2**20
        ),
    )(*heads, lse, first, kq, vq, text, x, dx1, g1[None], vec, n1_all, *weights, *parts)


def matmul(left, right):
    return jnp.dot(left, right, preferred_element_type=jnp.float32)


def left_times(left, right):
    return lax.dot_general(
        left, right, (((0,), (0,)), ((), ())), preferred_element_type=jnp.float32
    )


def right_times(left, right):
    return lax.dot_general(
        left, right, (((1,), (1,)), ((), ())), preferred_element_type=jnp.float32
    )


def norm_forward(values, gain, bias):
    center = values - jnp.mean(values, axis=-1, keepdims=True)
    scaled = lax.rsqrt(jnp.mean(center * center, axis=-1, keepdims=True) + EPS)
    unit = center * scaled
    return (unit * gain + bias, unit, scaled)


def norm_backward(upstream, unit, scaled, gain):
    along = upstream * gain
    inner = (
        along
        - jnp.mean(along, axis=-1, keepdims=True)
        - unit * jnp.mean(along * unit, axis=-1, keepdims=True)
    )
    return (inner * scaled, jnp.sum(upstream * unit, axis=0), jnp.sum(upstream, axis=0))


def gelu_slope(values):
    return (
        0.5 * (1.0 + lax.erf(values * SQRT_HALF))
        + values * jnp.exp(-0.5 * values * values) * INV_ROOT_TWO_PI
    )


def softmax_rows(scores):
    top = jnp.max(scores, axis=-1, keepdims=True)
    expo = jnp.exp(scores - top)
    total = jnp.sum(expo, axis=-1, keepdims=True)
    return (expo / total, top[..., 0] + jnp.log(total[..., 0]))


def shards(
    frames_in,
    text_states,
    clip_lengths,
    self_gain,
    self_bias,
    query_weight,
    key_weight,
    value_weight,
    output_weight,
    cross_gain,
    cross_bias,
    cross_query,
    cross_key,
    cross_value,
    cross_output,
    feed_gain,
    feed_bias,
    feed_upward,
    feed_downward,
    grad_out,
):
    count = lax.axis_size("seq")
    place = lax.axis_index("seq")
    local = frames_in.shape[1]
    total_frames = local * count
    block = min(512, total_frames)
    blocks = total_frames // block
    scale = HD ** (-0.5)
    lengths = clip_lengths[0]
    slot = jnp.arange(CLIPS, dtype=jnp.int32)
    ends = jnp.sum(jnp.where(slot[None, :] <= slot[:, None], lengths[None, :], 0), axis=1)
    begins = ends - lengths
    slots = jnp.arange(CLIPS, dtype=jnp.int32)
    positions = jnp.arange(total_frames, dtype=jnp.int32)
    owner_all = jnp.sum((ends[None, :] <= positions[:, None]).astype(jnp.int32), axis=1)
    first_all = jnp.sum(jnp.where(owner_all[:, None] == slots[None, :], begins[None, :], 0), axis=1)
    owner_mine = lax.dynamic_slice_in_dim(owner_all, place * local, local, 0)
    frames = frames_in[0].astype(jnp.float32)
    text = text_states[0]
    text_rows = text.shape[0]
    normed, _, _ = norm_forward(frames, self_gain, self_bias)
    normed_low = normed.astype(bf)
    query = matmul(normed_low, query_weight).astype(bf)
    keys = matmul(normed_low, key_weight).astype(bf)
    values = matmul(normed_low, value_weight).astype(bf)
    query_heads, key_heads, value_heads = (
        lax.all_to_all(query, "seq", split_axis=1, concat_axis=0, tiled=True),
        lax.all_to_all(keys, "seq", split_axis=1, concat_axis=0, tiled=True),
        lax.all_to_all(values, "seq", split_axis=1, concat_axis=0, tiled=True),
    )
    attended, log_totals = fwd(query_heads, key_heads, value_heads, first_all[:, None])
    attended_frames = lax.all_to_all(attended, "seq", split_axis=0, concat_axis=1, tiled=True)
    cross_k = matmul(text, cross_key).astype(bf)
    cross_v = matmul(text, cross_value).astype(bf)
    clips = lax.axis_size("clip")
    dx1, output, vec, c_up, c_dn, c_o, c_cq, c_co, grad_heads, normed_all, key_own, value_own = kb(
        count,
        clips,
        attended_frames,
        frames_in[0],
        grad_out[0],
        cross_k,
        cross_v,
        owner_mine,
        cross_gain,
        cross_bias,
        feed_gain,
        feed_bias,
        output_weight,
        cross_query,
        cross_output,
        feed_upward,
        feed_downward,
        normed_low,
    )
    frames_grad, vec, key_low, value_low, *mats = kc(
        count,
        clips,
        (query_heads, key_heads, value_heads, attended, grad_heads),
        log_totals,
        first_all[None],
        key_own,
        value_own,
        text,
        frames_in[0],
        dx1,
        self_gain,
        vec,
        normed_all,
        (query_weight, key_weight, value_weight),
        (c_up, c_dn, c_o, c_cq, c_co),
    )
    text_grad = right_times(key_low, cross_key) + right_times(value_low, cross_value)
    w_up, w_dn, w_o, w_cq, w_co, w_xk, w_xv, w_q, w_k, w_v = [one.astype(f32) for one in mats]
    width_out = D // clips
    vec = lax.dynamic_slice_in_dim(vec, lax.axis_index("clip") * width_out, width_out, 1)
    return (
        output[None],
        frames_grad[None],
        text_grad[None],
        vec[4],
        vec[5],
        w_q,
        w_k,
        w_v,
        w_o,
        vec[0],
        vec[1],
        w_cq,
        w_xk,
        w_xv,
        w_co,
        vec[2],
        vec[3],
        w_up,
        w_dn,
    )


def solution(mesh):
    return jax.shard_map(
        shards,
        mesh=mesh,
        in_specs=(
            P("clip", "seq", None),
            P("clip", None, None),
            P("clip", None),
            P(),
            P(),
            P(),
            P(),
            P(),
            P(),
            P(),
            P(),
            P(),
            P(),
            P(),
            P(),
            P(),
            P(),
            P(),
            P(),
            P("clip", "seq", None),
        ),
        out_specs=(
            P("clip", "seq", None),
            P("clip", "seq", None),
            P("clip", None, None),
            P("clip"),
            P("clip"),
            P("clip", None),
            P("clip", None),
            P("clip", None),
            P("clip", None),
            P("clip"),
            P("clip"),
            P("clip", None),
            P("clip", None),
            P("clip", None),
            P("clip", None),
            P("clip"),
            P("clip"),
            P("clip", None),
            P("clip", None),
        ),
        check_vma=False,
    )
```

```python
import functools
import math

import jax
import jax.numpy as jnp
from jax import lax
from jax.experimental import pallas as pl
from jax.experimental.pallas import tpu as pltpu
from jax.sharding import PartitionSpec as P

D = 1024
HEADS = 16
HD = 64
TEXT = 64
CLIPS = 4


EPS = 1e-05
NEG = -1e30
SQRT_HALF = 0.7071067811865476
INV_ROOT_TWO_PI = 0.3989422804014327

bf = jnp.bfloat16
f32 = jnp.float32
T, W, H, B = 2048, 256, 4, 256
LOG2E = math.log2(math.e)
C2 = LOG2E / 8.0
NT = (((1,), (1,)), ((), ()))
NN = (((1,), (0,)), ((), ()))
TN = (((0,), (0,)), ((), ()))


def dg(a, b, d):
    return lax.dot_general(a, b, d, preferred_element_type=f32)


def lanemask(rows,h):
    l=lax.broadcasted_iota(jnp.int32,(rows,W),1)
    return (l//HD)==h
def add_blocks(out, ins, rows, cols):
    step = max(16, min(rows, 65536 // cols))

    def body(i, carry):
        r = pl.ds(pl.multiple_of(i * step, 16), step)
        total = ins[0][r, :].astype(f32)
        for one in ins[1:]:
            total = total + one[r, :].astype(f32)
        out[r, :] = total.astype(bf)
        return carry

    lax.fori_loop(0, rows // step, body, 0)


def each(count, fn):
    def body(i, x):
        fn(i)
        return x

    lax.fori_loop(0, count, body, 0)


def tile_of(i, size=256):
    return pl.ds(pl.multiple_of(i * size, size), size)


def unit_rows(v):
    center = v - jnp.mean(v, axis=-1, keepdims=True)
    scaled = lax.rsqrt(jnp.mean(center * center, axis=-1, keepdims=True) + EPS)
    return center * scaled, scaled


def norm_rows(src, gain, bias, dst, rows):
    def chunk(i):
        r = tile_of(i, 64)
        unit, _ = unit_rows(src[r, :])
        dst[r, :] = (unit * gain[...] + bias[...]).astype(bf)

    each(rows // 64, chunk)


def norm_back_rows(up, src, gain, add, dst, dst_low, rows):
    def chunk(i, sums):
        r = tile_of(i, 64)
        unit, scaled = unit_rows(src[r, :])
        u = up[r, :]
        along = u * gain[...]
        inner = (
            along
            - jnp.mean(along, axis=-1, keepdims=True)
            - unit * jnp.mean(along * unit, axis=-1, keepdims=True)
        )
        total = add[r, :].astype(f32) + inner * scaled
        dst[r, :] = total
        dst_low[r, :] = total.astype(bf)
        fold = lambda v: jnp.sum(v.reshape(8, 8, v.shape[1]), axis=0)
        return sums[0] + fold(u * unit), sums[1] + fold(u)

    zero = jnp.zeros((8, src.shape[1]), f32)
    a, b = lax.fori_loop(0, rows // 64, chunk, (zero, zero))
    return jnp.sum(a, axis=0, keepdims=True), jnp.sum(b, axis=0, keepdims=True)


def remote(src, dst, send, recv, **where):
    return pltpu.make_async_remote_copy(
        src_ref=src, dst_ref=dst, send_sem=send, recv_sem=recv, device_id=where,
        device_id_type=pl.DeviceIdType.MESH,
    )


def greet(env, pairs):
    s, c, z, seqs = env["s"], env["c"], env["z"], env["seqs"]
    barrier = pltpu.get_barrier_semaphore()
    count = 1
    pl.semaphore_signal(
        barrier, inc=1, device_id={"clip": 2 * z + 1 - c}, device_id_type=pl.DeviceIdType.MESH
    )
    for k in range(1, seqs):
        pl.semaphore_signal(
            barrier, inc=1, device_id={"seq": lax.rem(s + k, seqs)}, device_id_type=pl.DeviceIdType.MESH
        )
        count += 1
    for k in range(1, pairs):
        pl.semaphore_signal(
            barrier, inc=1, device_id={"clip": 2 * lax.rem(z + k, pairs) + c},
            device_id_type=pl.DeviceIdType.MESH,
        )
        count += 1
    pl.semaphore_wait(barrier, count)


def place(seqs):
    b = lax.axis_index("clip")
    return dict(seqs=seqs, s=lax.axis_index("seq"), c=lax.rem(b, 2), z=lax.div(b, 2))


def kb_kernel(seqs, *refs):
    (
        att, x_ref, gb, ck, cv, owner, g2, b2, g3, b3,
        w_o, w_cq, w_co, w_up, w_dn, n1_hbm,
    ) = refs[:16]
    (x1, fo, vec, c_up, c_dn, c_o, c_cq, c_co, heads, n1_all, kq, vq) = refs[16:28]
    (
        ring, up_st, dn_st, up_rv, dn_rv, sq_rv, x2, n2, n3, n3t, cq, co, probs, u, ut, dh,
        acc, dn3, dck, dcv, kv_low, kv_rv, ring_sem, st_send, st_recv, out_sem, n1_sem, head_sem, kv_sem,
        own_sem,
    ) = refs[28:]
    env = place(seqs)
    s, c, z = env["s"], env["c"], env["z"]
    rows, d = x_ref.shape
    pairs, rb = up_rv.shape[0], up_rv.shape[1]
    ppc, rbd = dn_st.shape[0], dn_st.shape[2]
    steps = w_up.shape[1] // d
    width = d // seqs
    texts = ck.shape[0]
    depth = ring.shape[0]

    items = [w_o, w_cq, w_co]
    for t in range(steps):
        items += [w_up.at[:, pl.ds(t * d, d)], w_dn.at[pl.ds(t * d, d), :]]
    items += [w_co, w_cq, w_o]

    def load(i):
        return pltpu.make_async_copy(items[i], ring.at[i % depth], ring_sem.at[i % depth])

    def take(i):
        load(i).wait()
        return ring.at[i % depth]

    def drop(i):
        if i + depth < len(items):
            load(i + depth).start()

    for i in range(depth):
        load(i).start()
    greet(env, 1)

    peers = [(k, lax.rem(s + k, seqs)) for k in range(1, seqs)]
    spots = pl.ds(pl.multiple_of(s * rows, rows), rows)
    n1_out = [
        remote(n1_hbm, n1_all.at[spots, :], n1_sem.at[0, k], n1_sem.at[1, k], seq=to) for k, to in peers
    ]
    n1_own = pltpu.make_async_copy(n1_hbm, n1_all.at[spots, :], n1_sem.at[0, 0])
    start(n1_out)
    n1_own.start()

    w = take(0)

    def f(t):
        x1[:, tile_of(t)] = x_ref[:, tile_of(t)].astype(f32) + dg(att[...], w[:, tile_of(t)], NN)

    each(d // 256, f)
    drop(0)
    norm_rows(x1, g2, b2, n2, rows)
    w = take(1)

    def f(t):
        cq[:, tile_of(t)] = dg(n2[...], w[:, tile_of(t)], NN).astype(bf)

    each(d // 256, f)
    drop(1)
    half = 256
    key_clip = lax.broadcasted_iota(jnp.int32, (half, texts), 1) // TEXT

    def masked(v, h):
        lane = lax.broadcasted_iota(jnp.int32, v.shape, 1)
        return jnp.where(lane // HD == h, v, jnp.zeros_like(v))

    def f(n):
        t, r = lax.div(n, rows // half), tile_of(lax.rem(n, rows // half), half)
        allowed = owner[r, :] == key_clip
        q, k, v = cq[r, tile_of(t)], ck[:, tile_of(t)], cv[:, tile_of(t)]
        total = jnp.zeros((half, 256), f32)
        for h in range(256 // HD):
            sc = jnp.where(allowed, dg(masked(q, h), k, NT), NEG)
            p = jnp.exp2((sc - jnp.max(sc, axis=-1, keepdims=True)) * C2)
            p = (p / jnp.sum(p, axis=-1, keepdims=True)).astype(bf)
            probs[t * (256 // HD) + h, r, :] = p
            total = total + dg(p, masked(v, h), NN)
        co[r, tile_of(t)] = total.astype(bf)

    each(d // 256 * (rows // half), f)
    w = take(2)

    def f(t):
        x2[:, tile_of(t)] = x1[:, tile_of(t)] + dg(co[...], w[:, tile_of(t)], NN)

    each(d // 256, f)
    drop(2)
    norm_rows(x2, g3, b3, n3, rows)

    def turn(src, dst):
        def f(t):
            dst[tile_of(t), :] = src[:, tile_of(t)].T

        each(d // 256, f)

    turn(n3, n3t)

    def swap(n, src, dst):
        return remote(src, dst, st_send.at[n], st_recv.at[n], clip=2 * z + 1 - c)

    def up_swap(t):
        return swap(2 * t, up_st.at[0, :, 1 - c], up_rv.at[:, :, pl.ds(t * d, d)])

    def dn_swap(t):
        return swap(2 * t + 1, dn_st.at[:, 1 - c], dn_rv.at[pl.ds(t * ppc, ppc)])

    def up_out(t):
        cols = pl.ds(t * d, d)
        return pltpu.make_async_copy(up_rv.at[:, :, cols], c_up.at[:, :, cols], out_sem.at[2 * t])

    def dn_out(t):
        blocks = pl.ds(t * ppc, ppc)
        return pltpu.make_async_copy(dn_rv.at[blocks], c_dn.at[blocks], out_sem.at[2 * t + 1])

    def settle(t):
        one = up_swap(t)
        one.wait_recv()
        for p in range(pairs):
            dst = up_rv.at[p, :, pl.ds(t * d, d)]
            add_blocks(dst, [dst, up_st.at[0, p, c]], rb, d)
        one.wait_send()
        up_out(t).start()
        one = dn_swap(t)
        one.wait_recv()
        for p in range(ppc):
            dst = dn_rv.at[t * ppc + p]
            add_blocks(dst, [dst, dn_st.at[p, c]], rbd, d)
        one.wait_send()
        dn_out(t).start()

    for t in range(steps):
        wu, wd = take(3 + 2 * t), take(4 + 2 * t)

        def f(i):
            h = dg(n3[...], wu[:, tile_of(i)], NN)
            du = dg(gb[...], wd[tile_of(i), :], NT)
            part = 0.5 * (1.0 + lax.erf(h * SQRT_HALF))
            slope = part + h * jnp.exp2(h * h * (-0.5 * LOG2E)) * INV_ROOT_TWO_PI
            dh[:, tile_of(i)] = (du * slope).astype(bf)
            act = (h * part).astype(bf)
            u[:, tile_of(i)] = act
            ut[tile_of(i), :] = act.T

        each(d // 256, f)
        if t > 0:
            settle(t - 1)

        def f(i, t=t):
            a = dg(u[...], wd[:, tile_of(i)], NN)
            b = dg(dh[...], wu[tile_of(i), :], NT)
            if t == 0:
                acc[:, tile_of(i)] = a
                dn3[:, tile_of(i)] = b
            else:
                acc[:, tile_of(i)] += a
                dn3[:, tile_of(i)] += b
            g = dg(n3t[...], dh[:, tile_of(i)], NN).astype(bf)
            up_st[0, :, :, :, tile_of(i)] = g.reshape(pairs, 2, rb, 256)
            g = dg(ut[...], gb[:, tile_of(i)], NN).astype(bf)
            dn_st[:, :, :, tile_of(i)] = g.reshape(ppc, 2, rbd, 256)

        each(d // 256, f)
        drop(3 + 2 * t)
        drop(4 + 2 * t)
        up_swap(t).start()
        dn_swap(t).start()

    def f(i):
        r = tile_of(i, 64)
        fo[r, :] = (x2[r, :] + acc[r, :]).astype(bf)

    each(rows // 64, f)
    base = 3 + 2 * steps
    low = u
    sums = norm_back_rows(dn3, x2, g3, gb, acc, low, rows)
    vec[2:3, :], vec[3:4, :] = sums
    w = take(base)
    dco = dh

    def f(t):
        dco[:, tile_of(t)] = dg(low[...], w[tile_of(t), :], NT).astype(bf)

    each(d // 256, f)
    drop(base)
    settle(steps - 1)

    def grad(n, slot, a, low):
        turn(a, n3t)

        def f(t):
            g = dg(n3t[...], low[:, tile_of(t)], NN).astype(bf)
            up_st[slot, :, :, :, tile_of(t)] = g.reshape(pairs, 2, rb, 256)

        each(d // 256, f)
        grad_swap(n, slot).start()

    def grad_swap(n, slot):
        return swap(2 * steps + n, up_st.at[slot, :, 1 - c], sq_rv.at[n])

    def grad_out(n):
        return pltpu.make_async_copy(sq_rv.at[n], (c_co, c_cq, c_o)[n], out_sem.at[2 * steps + n])

    def grad_settle(n, slot):
        one = grad_swap(n, slot)
        one.wait_recv()
        for p in range(pairs):
            add_blocks(sq_rv.at[n, p], [sq_rv.at[n, p], up_st.at[slot, p, c]], rb, d)
        one.wait_send()
        grad_out(n).start()

    grad(0, 0, co, low)
    dcq = n3

    def f(t):
        k, v = ck[:, tile_of(t)], cv[:, tile_of(t)]
        sum_k = jnp.zeros((texts, 256), f32)
        sum_v = jnp.zeros((texts, 256), f32)
        for n in range(rows // half):
            r = pl.ds(n * half, half)
            q, g = cq[r, tile_of(t)], dco[r, tile_of(t)]
            out = jnp.zeros((half, 256), f32)
            for h in range(256 // HD):
                p_low = probs[t * (256 // HD) + h, r, :]
                p = p_low.astype(f32)
                dp = dg(masked(g, h), v, NT)
                inner = jnp.sum(p * dp, axis=-1, keepdims=True)
                ds = (p * (dp - inner)).astype(bf)
                out = out + dg(ds, masked(k, h), NN)
                sum_k = sum_k + dg(ds, masked(q, h), TN)
                sum_v = sum_v + dg(p_low, masked(g, h), TN)
            dcq[r, tile_of(t)] = (out * 0.125).astype(bf)
        kv_low[0, :, tile_of(t)] = (sum_k * 0.125).astype(bf)
        kv_low[1, :, tile_of(t)] = sum_v.astype(bf)

    each(d // 256, f)
    mine = pl.ds(pl.multiple_of(s * width, 128), width)
    kv_out = [
        remote(
            kv_low.at[:, :, pl.ds(pl.multiple_of(to * width, 128), width)], kv_rv.at[k - 1],
            kv_sem.at[0, k], kv_sem.at[1, k], seq=to,
        )
        for k, to in peers
    ]
    start(kv_out)
    w = take(base + 1)
    dn2 = dn3

    def f(t):
        dn2[:, tile_of(t)] = dg(dcq[...], w[tile_of(t), :], NT)

    each(d // 256, f)
    drop(base + 1)
    sums = norm_back_rows(dn2, x1, g2, acc, x1, low, rows)
    vec[0:1, :], vec[1:2, :] = sums
    vec[4:8, :] = jnp.zeros((4, d), f32)
    w = take(base + 2)
    do = dh

    def f(t):
        do[:, tile_of(t)] = dg(low[...], w[tile_of(t), :], NT).astype(bf)

    each(d // 256, f)
    head_out = [
        remote(
            do.at[:, pl.ds(pl.multiple_of(to * width, 128), width)], heads.at[spots, :],
            head_sem.at[0, k], head_sem.at[1, k], seq=to,
        )
        for k, to in peers
    ]
    head_own = pltpu.make_async_copy(do.at[:, mine], heads.at[spots, :], head_sem.at[0, 0])
    start(head_out)
    head_own.start()
    grad(1, 1, n2, dcq)
    grad_settle(0, 0)
    grad(2, 0, att, low)
    grad_settle(1, 1)
    arrive(kv_out)
    for n, dst in enumerate((kq, vq)):
        total = kv_low[n, :, mine].astype(f32)
        for k in range(1, seqs):
            total = total + kv_rv[k - 1, n].astype(f32)
        dst[...] = total.astype(bf)
    grad_settle(2, 0)
    finish(kv_out)
    head_own.wait()
    n1_own.wait()
    for one in head_out + n1_out:
        one.wait()
    for t in range(steps):
        up_out(t).wait()
        dn_out(t).wait()
    for n in range(3):
        grad_out(n).wait()


def kb(seqs, clips, att, x, gb, ck, cv, owner, g2, b2, g3, b3, w_o, w_cq, w_co, w_up, w_dn, n1):
    rows, d = x.shape
    pairs = clips // 2
    rb, rbd = d // clips, w_dn.shape[0] // clips
    steps = w_up.shape[1] // d
    ppc = pairs // steps
    texts = ck.shape[0]
    width = d // seqs
    hbm = pl.BlockSpec(memory_space=pl.ANY)
    vmem = pl.BlockSpec(memory_space=pltpu.VMEM)
    low = lambda *shape: pltpu.VMEM(shape, bf)
    full = lambda *shape: pltpu.VMEM(shape, f32)
    s_low = lambda *shape: jax.ShapeDtypeStruct(shape, bf)
    dma = pltpu.SemaphoreType.DMA
    return pl.pallas_call(
        functools.partial(kb_kernel, seqs),
        out_shape=[
            jax.ShapeDtypeStruct((rows, d), f32),
            s_low(rows, d),
            jax.ShapeDtypeStruct((8, d), f32),
            s_low(pairs, rb, steps * d),
            s_low(pairs, rbd, d),
            s_low(pairs, rb, d),
            s_low(pairs, rb, d),
            s_low(pairs, rb, d),
            s_low(rows * seqs, width),
            s_low(rows * seqs, d),
            s_low(texts, width),
            s_low(texts, width),
        ],
        in_specs=[vmem] * 10 + [hbm] * 6,
        out_specs=[vmem] * 3 + [hbm] * 7 + [vmem] * 2,
        scratch_shapes=[
            low(4, d, d),
            low(2, pairs, 2, rb, d),
            low(ppc, 2, rbd, d),
            low(pairs, rb, steps * d),
            low(pairs, rbd, d),
            low(3, pairs, rb, d),
            full(rows, d),
            low(rows, d),
            low(rows, d),
            low(d, rows),
            low(rows, d),
            low(rows, d),
            low(d // HD, rows, texts),
            low(rows, d),
            low(d, rows),
            low(rows, d),
            full(rows, d),
            full(rows, d),
            full(8, 128),
            full(8, 128),
            low(2, texts, d),
            low(seqs - 1, 2, texts, width),
            dma((4,)),
            dma((2 * steps + 3,)),
            dma((2 * steps + 3,)),
            dma((2 * steps + 3,)),
            dma((2, seqs)),
            dma((2, seqs)),
            dma((2, seqs)),
            dma((1,)),
        ],
        compiler_params=pltpu.CompilerParams(
            collective_id=2, has_side_effects=True, vmem_limit_bytes=60 * 2**20
        ),
    )(
        att, x, gb, ck, cv, owner[:, None],
        *[v[None] for v in (g2, b2, g3, b3)],
        w_o, w_cq, w_co, w_up, w_dn, n1,
    )


def ka_kernel(seqs, *refs):
    x_ref, g1, b1, first, w_q, w_k, w_v = refs[:7]
    n1, o_ref, lse_ref, q_out, k_out, v_out, att = refs[7:14]
    w_buf, wide, stage, held, vt, w_sem, send, recv, push_send, push_recv, out_sem = refs[14:]
    env = place(seqs)
    s = env["s"]
    rows, d = x_ref.shape
    pair = 2 * HD
    loads = [
        pltpu.make_async_copy(one, w_buf.at[n], w_sem.at[n]) for n, one in enumerate((w_q, w_k, w_v))
    ]
    start(loads)
    greet_seq(env)

    def f(i):
        r = tile_of(i, 64)
        wide[r, :] = x_ref[r, :].astype(f32)

    each(rows // 64, f)
    norm_rows(wide, g1, b1, n1, rows)
    spots = pl.ds(pl.multiple_of(s * rows, rows), rows)
    peers = [(k, lax.rem(s + k, seqs)) for k in range(1, seqs)]

    def sends(g):
        return [
            remote(
                stage.at[:, :, pl.ds(pl.multiple_of(to * W + g * pair, 128), pair)],
                held.at[:, spots, pl.ds(g * pair, pair)],
                send.at[g, k], recv.at[g, k], seq=to,
            )
            for k, to in peers
        ]

    for one in loads:
        one.wait()
    first_sends = sends(0)
    for n, (k, to) in enumerate(peers):
        cols = pl.ds(pl.multiple_of(to * W, 128), W)
        for t in range(3):
            stage[t, :, cols] = dg(n1[...], w_buf[t, :, cols], NN).astype(bf)
        first_sends[n].start()
    cols = pl.ds(pl.multiple_of(s * W, 128), W)
    for t in range(3):
        held[t, spots, :] = dg(n1[...], w_buf[t, :, cols], NN).astype(bf)

    lane = lax.broadcasted_iota(jnp.int32, (1, pair), 1) // HD
    kvi = lax.broadcasted_iota(jnp.int32, (rows, rows), 0)
    qi = lax.broadcasted_iota(jnp.int32, (rows, rows), 1)

    def qblock(g, i, masked):
        ln = pl.ds(g * pair, pair)
        r = tile_of(i, rows)
        q = held[0, r, ln]
        qm = [jnp.where(lane == h, q, jnp.zeros_like(q)) for h in range(2)]
        fst = first[:, r]

        def step(j, carry, diag):
            c = tile_of(j, rows)
            k = held[1, c, ln]
            out = []
            for h in range(2):
                m, l, acc = carry[h]
                sc = dg(k, qm[h], NT)
                if diag:
                    sc = jnp.where(kvi <= qi, sc, NEG)
                if masked:
                    sc = jnp.where(kvi + j * rows >= fst, sc, NEG)
                top = jnp.maximum(m, jnp.max(sc, axis=0, keepdims=True))
                p = jnp.exp2((sc - top) * C2)
                a = jnp.exp2((m - top) * C2)
                l = l * a + jnp.sum(p, axis=0, keepdims=True)
                acc = acc * a + dg(vt[h * HD : (h + 1) * HD, c], p.astype(bf), NN)
                out.append((top, l, acc))
            return tuple(out)

        carry = tuple(
            (jnp.full((1, rows), NEG, f32), jnp.zeros((1, rows), f32), jnp.zeros((HD, rows), f32))
            for _ in range(2)
        )
        carry = lax.fori_loop(0, i, lambda j, x: step(j, x, False), carry)
        carry = step(i, carry, True)
        ot = jnp.concatenate([acc / l for _, l, acc in carry], axis=0)
        o_ref[r, ln] = ot.T.astype(bf)
        for h in range(2):
            lse_ref[2 * g + h : 2 * g + h + 1, r] = carry[h][0] * C2 + jnp.log2(carry[h][1])

    def push(g, owner, away):
        src = o_ref.at[tile_of(owner, rows), pl.ds(g * pair, pair)]
        dst = att.at[:, pl.ds(pl.multiple_of(s * W + g * pair, 128), pair)]
        k = lax.rem(owner - s + seqs, seqs)
        if away:
            return remote(src, dst, push_send.at[g, owner], push_recv.at[g, k], seq=owner)
        return pltpu.make_async_copy(src, dst, push_send.at[g, owner])

    def send_rows(g, owner):
        @pl.when(s != owner)
        def _():
            push(g, owner, True).start()

        @pl.when(s == owner)
        def _():
            push(g, owner, False).start()

    lse_ref[4:8, :] = jnp.zeros((4, lse_ref.shape[1]), f32)
    for g in range(2):
        arrive(sends(g))
        if g == 0:
            start(sends(1))
        else:
            outs = [
                pltpu.make_async_copy(held.at[n], one, out_sem.at[n])
                for n, one in enumerate((q_out, k_out, v_out))
            ]
            start(outs)

        def f(i, g=g):
            r = tile_of(i, rows)
            vt[:, r] = held[2, r, pl.ds(g * pair, pair)].T

        each(seqs, f)

        def f(i, g=g):
            qblock(g, i, False)
            send_rows(g, i)

        plain = TAIL // rows
        each(plain, f)
        for i in range(plain, seqs):
            qblock(g, i, True)
            send_rows(g, i)
    for one in outs:
        one.wait()
    for g in range(2):
        finish(sends(g))
        for owner in range(seqs):
            @pl.when(s != owner)
            def _():
                push(g, owner, True).wait_send()

            @pl.when(s == owner)
            def _():
                push(g, owner, False).wait()
        for k in range(1, seqs):
            back = lax.rem(s - k + seqs, seqs)
            dst = att.at[:, pl.ds(pl.multiple_of(back * W + g * pair, 128), pair)]
            pltpu.make_async_copy(dst, dst, push_recv.at[g, k]).wait()


def greet_seq(env):
    s, seqs = env["s"], env["seqs"]
    barrier = pltpu.get_barrier_semaphore()
    for k in range(1, seqs):
        pl.semaphore_signal(
            barrier, inc=1, device_id={"seq": lax.rem(s + k, seqs)}, device_id_type=pl.DeviceIdType.MESH
        )
    pl.semaphore_wait(barrier, seqs - 1)


def ka(seqs, x, g1, b1, first, weights):
    rows, d = x.shape
    hbm = pl.BlockSpec(memory_space=pl.ANY)
    vmem = pl.BlockSpec(memory_space=pltpu.VMEM)
    dma = pltpu.SemaphoreType.DMA
    s_low = lambda *shape: jax.ShapeDtypeStruct(shape, bf)
    total = rows * seqs
    return pl.pallas_call(
        functools.partial(ka_kernel, seqs),
        out_shape=[
            s_low(rows, d),
            s_low(total, W),
            jax.ShapeDtypeStruct((8, total), f32),
            s_low(total, W),
            s_low(total, W),
            s_low(total, W),
            s_low(rows, d),
        ],
        in_specs=[vmem] * 4 + [hbm] * 3,
        out_specs=[vmem] * 3 + [hbm] * 4,
        scratch_shapes=[
            pltpu.VMEM((3, d, d), bf),
            pltpu.VMEM((rows, d), f32),
            pltpu.VMEM((3, rows, d), bf),
            pltpu.VMEM((3, total, W), bf),
            pltpu.VMEM((2 * HD, total), bf),
            dma((3,)),
            dma((2, seqs)),
            dma((2, seqs)),
            dma((2, seqs)),
            dma((2, seqs)),
            dma((3,)),
        ],
        compiler_params=pltpu.CompilerParams(
            collective_id=3, has_side_effects=True, vmem_limit_bytes=50 * 2**20
        ),
    )(x, g1[None], b1[None], first, *weights)


class Job:
    def __init__(self, order, part, bufs, sems, out, env, pairs):
        self.order, self.part, self.out, self.env, self.pairs = order, part, out, env, pairs
        self.r0, self.r1, self.r2 = bufs
        self.sems = sems
        self.rb, self.n = part.shape[-2:]
        self.q = self.n if order == "own" else self.n // env["seqs"]

    def copy(self, stage, k, src, dst, **where):
        return remote(src, dst, self.sems.at[0, stage, k], self.sems.at[1, stage, k], **where)

    def cores(self):
        e = self.env
        return [
            self.copy(0, 0, self.part.at[:, 1 - e["c"]], self.r0, clip=2 * e["z"] + 1 - e["c"])
        ]

    def mine(self):
        src = self.part.at[:, :, self.columns(self.env["s"])] if self.order == "xy" else self.part.at[self.env["z"]]
        return pltpu.make_async_copy(src, self.r0, self.sems.at[0, 4, 0])

    def columns(self, s):
        return pl.ds(pl.multiple_of(s * self.q, 128), self.q)

    def seq(self):
        e, copies = self.env, []
        for k in range(1, e["seqs"]):
            to = lax.rem(e["s"] + k, e["seqs"])
            if self.order == "xy":
                src, dst = self.part.at[:, :, self.columns(to)], self.r1.at[k - 1]
            else:
                src, dst = self.r1.at[0, :, self.columns(to)], self.r2.at[k - 1]
            copies.append(self.copy(1, k - 1, src, dst, seq=to))
        return copies

    def across(self):
        e, copies = self.env, []
        for k in range(1, self.pairs):
            to = lax.rem(e["z"] + k, self.pairs)
            if self.order == "xy":
                src, dst = self.r1.at[0, to], self.r2.at[k - 1]
            elif self.order == "z":
                src, dst = self.part.at[to], self.r1.at[k - 1]
            else:
                src, dst = self.r0.at[to], self.r2.at[k - 1]
            copies.append(self.copy(2, k - 1, src, dst, clip=2 * to + e["c"]))
        return copies

    def gather(self):
        e, copies = self.env, []
        for k in range(1, e["seqs"]):
            to = lax.rem(e["s"] + k, e["seqs"])
            copies.append(
                self.copy(3, k - 1, self.r2.at[0], self.out.at[:, self.columns(e["s"])], seq=to)
            )
        return copies

    def keep(self):
        return pltpu.make_async_copy(
            self.r2.at[0], self.out.at[:, self.columns(self.env["s"])], self.sems.at[1, 4, 0]
        )

    def sum_cores(self):
        for p in range(self.pairs):
            add_blocks(self.r0.at[p], [self.r0.at[p], self.part.at[p, self.env["c"]]], self.rb, self.n)

    def sum_seq(self):
        others = range(self.env["seqs"] - 1)
        if self.order == "xy":
            self.mine().wait()
            for p in range(self.pairs):
                add_blocks(self.r1.at[0, p], [self.r0.at[p]] + [self.r1.at[k, p] for k in others], self.rb, self.q)
        else:
            mine = self.r1.at[0, :, self.columns(self.env["s"])]
            add_blocks(self.r2.at[0], [mine] + [self.r2.at[k] for k in others], self.rb, self.q)

    def sum_across(self):
        e = self.env
        others = range(self.pairs - 1)
        if self.order == "xy":
            add_blocks(self.r2.at[0], [self.r1.at[0, e["z"]]] + [self.r2.at[k] for k in others], self.rb, self.q)
        elif self.order == "z":
            self.mine().wait()
            add_blocks(self.r1.at[0], [self.r0] + [self.r1.at[k] for k in others], self.rb, self.n)
        else:
            add_blocks(self.r2.at[0], [self.r0.at[e["z"]]] + [self.r2.at[k] for k in others], self.rb, self.q)


def start(copies):
    for one in copies:
        one.start()


def arrive(copies):
    for one in copies:
        one.wait_recv()


def finish(copies):
    for one in copies:
        one.wait_send()


def job_bufs(order, pairs, rb, n, seqs):
    q = n if order == "own" else n // seqs
    low = lambda *shape: pltpu.VMEM(shape, bf)
    if order == "xy":
        return [low(pairs, rb, q), low(seqs - 1, pairs, rb, q), low(pairs - 1, rb, q)]
    if order == "z":
        return [low(rb, n), low(pairs - 1, rb, n), low(seqs - 1, rb, q)]
    return [low(pairs, rb, q), low(16, 128), low(pairs - 1, rb, q)]


LAST = pl.DeviceIdType.MESH


def kc_kernel(seqs, pairs, *refs):
    (q_ref, k_ref, v_ref, o_ref, g_ref, lse_ref, first_ref) = refs[:7]
    (kq, vq, text, x_ref, dx1, g1, vec_in, n1_hbm, w_q, w_k, w_v, *parts) = refs[7:23]
    (frames_grad, vec, k_all, v_all, *outs) = refs[23:37]
    dq_s, dk_s, dv_s, dka, dva, n1_buf, wacc, wparts, dqkv, w_buf, dn1, vec_rv, low_buf, *rest = refs[37:]
    sems, push_send, push_recv, local_sem, kv_sem, vec_sem = rest[-6:]
    bufs = rest[:-6]
    env = place(seqs)
    s, c, z = env["s"], env["c"], env["z"]
    frames = T // seqs
    d = n1_hbm.shape[1]
    greet(env, pairs)

    orders = ORDERS
    jobs = []
    for t, order in enumerate(orders):
        src = parts[t] if t < 5 else wparts.at[t - 5]
        jobs.append(Job(order, src, bufs[3 * t : 3 * t + 3], sems.at[t], outs[t], env, pairs))
    up, down, go, gcq, gco, gxk, gxv, gq, gk, gv = jobs
    start(down.across())
    start(up.seq())
    for one in (go, gcq, gco):
        start(one.seq())
    for one in (up, down, go, gcq, gco):
        one.mine().start()
    width = kq.shape[1]
    spot = pl.ds(pl.multiple_of(s * width, 128), width)
    kv_out, kv_own = [], []
    for n, (src, dst) in enumerate(((kq, k_all), (vq, v_all))):
        for k in range(1, seqs):
            kv_out.append(
                remote(src, dst.at[:, spot], kv_sem.at[0, n, k], kv_sem.at[1, n, k], seq=lax.rem(s + k, seqs))
            )
        kv_own.append(pltpu.make_async_copy(src, dst.at[:, spot], kv_sem.at[0, n, 0]))
    start(kv_out)
    start(kv_own)
    loads = [pltpu.make_async_copy(n1_hbm, n1_buf, local_sem.at[0])]
    for n, one in enumerate((w_q, w_k, w_v)):
        loads.append(pltpu.make_async_copy(one, w_buf.at[n], local_sem.at[1 + n]))
    start(loads)

    def place_product(n, rb):
        for p in range(pairs):
            for cc in range(2):
                wparts[n, p, cc] = wacc[pl.ds((2 * p + cc) * rb, rb), :].astype(bf)

    for n, src in enumerate((kq, vq)):
        wacc[...] = dg(text[...], src[...], TN)
        place_product(n, gxk.rb)
        start((gxk, gxv)[n].cores())

    dka[...] = jnp.zeros_like(dka)
    dva[...] = jnp.zeros_like(dva)

    def qblock(i, masked):
        r0 = pl.multiple_of(i * B, B)
        q = q_ref[pl.ds(r0, B), :]
        g = g_ref[pl.ds(r0, B), :]
        go_ = g.astype(f32) * o_ref[pl.ds(r0, B), :].astype(f32)
        hm = (
            lax.broadcasted_iota(jnp.int32, (8, W), 1) // HD == lax.broadcasted_iota(jnp.int32, (8, W), 0)
        ).astype(f32)
        delta = lax.dot_general(hm, go_, NT, precision=lax.Precision.HIGHEST, preferred_element_type=f32)
        lse = lse_ref[:, pl.ds(r0, B)]
        fst = first_ref[:, pl.ds(r0, B)]
        zero = jnp.zeros_like(q)
        qm = [jnp.where(lanemask(B, h), q, zero) for h in range(H)]
        gm = [jnp.where(lanemask(B, h), g, zero) for h in range(H)]
        kvi = lax.broadcasted_iota(jnp.int32, (B, B), 0)
        qi = lax.broadcasted_iota(jnp.int32, (B, B), 1)

        def tile(j, dq, diag):
            c0 = pl.multiple_of(j * B, B)
            k = k_ref[pl.ds(c0, B), :]
            v = v_ref[pl.ds(c0, B), :]
            dv = jnp.zeros((B, W), f32)
            dk = jnp.zeros((B, W), f32)
            for h in range(H):
                st = dg(k, qm[h], NT)
                p = jnp.exp2(st * C2 - lse[h : h + 1])
                if diag:
                    p = jnp.where(kvi <= qi, p, 0.0)
                if masked:
                    p = jnp.where(kvi + c0 >= fst, p, 0.0)
                dp = dg(v, gm[h], NT)
                ds = (p * (dp - delta[h : h + 1])).astype(bf)
                dv = dv + dg(p.astype(bf), gm[h], NN)
                dk = dk + dg(ds, qm[h], NN)
                km = jnp.where(lanemask(B, h), k, zero)
                dq = dq + dg(ds, km, TN)
            dva[pl.ds(c0, B), :] += dv
            dka[pl.ds(c0, B), :] += dk
            return dq

        dq = jnp.zeros((B, W), f32)
        dq = lax.fori_loop(0, i, lambda j, x: tile(j, x, False), dq)
        dq = tile(i, dq, True)
        dq_s[pl.ds(r0, B), :] = (dq * 0.125).astype(bf)
        dk_s[pl.ds(r0, B), :] = (dka[pl.ds(r0, B), :] * 0.125).astype(bf)
        dv_s[pl.ds(r0, B), :] = dva[pl.ds(r0, B), :].astype(bf)

    lanes = pl.ds(pl.multiple_of(s * W, 128), W)
    moved = [(src, dqkv.at[n]) for n, src in enumerate((dq_s, dk_s, dv_s))]

    def pushes(owner):
        k = lax.rem(owner - s + seqs, seqs)
        rows = pl.ds(owner * frames, frames)
        return [
            pltpu.make_async_remote_copy(
                src_ref=src.at[rows, :],
                dst_ref=dst.at[:, lanes],
                send_sem=push_send.at[n, owner],
                recv_sem=push_recv.at[n, k],
                device_id={"seq": owner},
                device_id_type=LAST,
            )
            for n, (src, dst) in enumerate(moved)
        ]

    def keeps(owner):
        rows = pl.ds(owner * frames, frames)
        return [
            pltpu.make_async_copy(src.at[rows, :], dst.at[:, lanes], push_send.at[n, owner])
            for n, (src, dst) in enumerate(moved)
        ]

    per = frames // B
    for owner in reversed(range(seqs)):
        def block(n, x, owner=owner):
            qblock(owner * per + per - 1 - n, (owner + 1) * frames > TAIL)
            return x
        lax.fori_loop(0, per, block, 0)

        @pl.when(s != owner)
        def _():
            start(pushes(owner))

        @pl.when(s == owner)
        def _():
            start(keeps(owner))

        if owner == seqs - 1:
            for one in (gxk, gxv):
                arrive(one.cores())
                one.sum_cores()
                start(one.across())

    loads[0].wait()
    for n, src in enumerate((dq_s, dk_s, dv_s)):
        def product(r, x, src=src):
            rows = pl.ds(pl.multiple_of(r * B, B), B)
            add = dg(n1_buf[rows, :], src[rows, :], TN)
            wacc[...] = jnp.where(r == 0, add, wacc[...] + add)
            return x
        lax.fori_loop(0, T // B, product, 0)
        place_product(2 + n, gq.rb)
        start((gq, gk, gv)[n].cores())

    for one in (gxk, gxv):
        arrive(one.across())
        one.sum_across()
        start(one.gather())
        one.keep().start()
    for one in (gq, gk, gv):
        arrive(one.cores())
        one.sum_cores()
        start(one.across())
    arrive(up.seq())
    up.sum_seq()
    start(up.across())
    for one in (go, gcq, gco):
        arrive(one.seq())
        one.sum_seq()
        start(one.across())

    for k in range(1, seqs):
        for n in range(3):
            dst = dqkv.at[n, :, pl.ds(pl.multiple_of(lax.rem(s - k + seqs, seqs) * W, 128), W)]
            pltpu.make_async_copy(dst, dst, push_recv.at[n, k]).wait()
    for owner in range(seqs):
        @pl.when(s != owner)
        def _():
            finish(pushes(owner))

        @pl.when(s == owner)
        def _():
            for one in keeps(owner):
                one.wait()
    for n in range(3):
        loads[1 + n].wait()

        def f(t, n=n):
            add = dg(dqkv[n], w_buf[n, tile_of(t), :], NT)
            if n == 0:
                dn1[:, tile_of(t)] = add
            else:
                dn1[:, tile_of(t)] += add

        each(d // 256, f)

    def f(i):
        r = tile_of(i, 64)
        wide_x[r, :] = x_ref[r, :].astype(f32)

    wide_x = frames_grad
    each(frames // 64, f)
    vec[...] = vec_in[...]
    sums = norm_back_rows(dn1, wide_x, g1, dx1, frames_grad, low_buf, frames)
    vec[4:5, :], vec[5:6, :] = sums
    swap = [remote(vec, vec_rv.at[0], vec_sem.at[0, 0, 0], vec_sem.at[1, 0, 0], clip=2 * z + 1 - c)]
    start(swap)

    arrive(down.across())
    down.sum_across()
    start(down.seq())
    arrive(swap)
    finish(swap)
    vec[...] = vec[...] + vec_rv[0]
    base = 1
    vec_rv[base + s] = vec[...]
    round_seq = [
        remote(vec, vec_rv.at[base + s], vec_sem.at[0, 1, k], vec_sem.at[1, 1, k], seq=lax.rem(s + k, seqs))
        for k in range(1, seqs)
    ]
    start(round_seq)
    for one in (gq, gk, gv, up, go, gcq, gco):
        arrive(one.across())
        one.sum_across()
        start(one.gather())
        one.keep().start()
    arrive(round_seq)
    finish(round_seq)
    total = vec_rv[base]
    for k in range(1, seqs):
        total = total + vec_rv[base + k]
    vec[...] = total
    base = 1 + seqs
    round_z = [
        remote(
            vec, vec_rv.at[base + k - 1], vec_sem.at[0, 2, k], vec_sem.at[1, 2, k],
            clip=2 * lax.rem(z + k, pairs) + c,
        )
        for k in range(1, pairs)
    ]
    start(round_z)
    arrive(down.seq())
    down.sum_seq()
    start(down.gather())
    down.keep().start()
    arrive(round_z)
    finish(round_z)
    total = vec[...]
    for k in range(1, pairs):
        total = total + vec_rv[base + k - 1]
    vec[...] = total

    for one in kv_out + kv_own:
        one.wait()
    for one in jobs:
        if one.order == "own":
            finish(one.cores())
        else:
            finish(one.seq())
        finish(one.across())
        finish(one.gather())
        one.keep().wait()
        arrive(one.gather())


ORDERS = ("xy", "z", "xy", "xy", "xy", "own", "own", "own", "own", "own")
TAIL = 1536


def kc(seqs, clips, heads, lse, first, kq, vq, text, x, dx1, g1, vec, n1_all, weights, parts):
    pairs = clips // 2
    rows, d = x.shape
    rb = d // clips
    shapes = [p.shape for p in parts] + [(pairs, 2, rb, W)] * 5
    bufs = []
    for order, shape in zip(ORDERS, shapes):
        bufs += job_bufs(order, pairs, shape[-2], shape[-1], seqs)
    outs = [
        jax.ShapeDtypeStruct((rows, d), f32),
        jax.ShapeDtypeStruct((8, d), f32),
        jax.ShapeDtypeStruct((text.shape[0], d), bf),
        jax.ShapeDtypeStruct((text.shape[0], d), bf),
    ]
    for order, shape in zip(ORDERS, shapes):
        outs.append(jax.ShapeDtypeStruct((shape[-2], shape[-1] * (seqs if order == "own" else 1)), bf))
    hbm = pl.BlockSpec(memory_space=pl.ANY)
    vmem = pl.BlockSpec(memory_space=pltpu.VMEM)
    most = max(seqs, pairs)
    dma = pltpu.SemaphoreType.DMA
    return pl.pallas_call(
        functools.partial(kc_kernel, seqs, pairs),
        out_shape=outs,
        in_specs=[vmem] * 14 + [hbm] * 9,
        out_specs=[vmem] * 2 + [hbm] * 12,
        scratch_shapes=[pltpu.VMEM((T, W), bf)] * 3
        + [pltpu.VMEM((T, W), f32)] * 2
        + [
            pltpu.VMEM((T, d), bf),
            pltpu.VMEM((d, W), f32),
            pltpu.VMEM((5, pairs, 2, rb, W), bf),
            pltpu.VMEM((3, rows, d), bf),
            pltpu.VMEM((3, d, d), bf),
            pltpu.VMEM((rows, d), f32),
            pltpu.VMEM((1 + seqs + pairs - 1, 8, d), f32),
            pltpu.VMEM((rows, d), bf),
        ]
        + bufs
        + [
            dma((10, 2, 5, most)),
            dma((3, seqs)),
            dma((3, seqs)),
            dma((4,)),
            dma((2, 2, seqs)),
            dma((2, 3, most)),
        ],
        compiler_params=pltpu.CompilerParams(
            collective_id=1, has_side_effects=True, vmem_limit_bytes=60 * 2**20
        ),
    )(*heads, lse, first, kq, vq, text, x, dx1, g1[None], vec, n1_all, *weights, *parts)


def matmul(left, right):
    return jnp.dot(left, right, preferred_element_type=jnp.float32)


def left_times(left, right):
    return lax.dot_general(
        left, right, (((0,), (0,)), ((), ())), preferred_element_type=jnp.float32
    )


def right_times(left, right):
    return lax.dot_general(
        left, right, (((1,), (1,)), ((), ())), preferred_element_type=jnp.float32
    )


def norm_forward(values, gain, bias):
    center = values - jnp.mean(values, axis=-1, keepdims=True)
    scaled = lax.rsqrt(jnp.mean(center * center, axis=-1, keepdims=True) + EPS)
    unit = center * scaled
    return (unit * gain + bias, unit, scaled)


def norm_backward(upstream, unit, scaled, gain):
    along = upstream * gain
    inner = (
        along
        - jnp.mean(along, axis=-1, keepdims=True)
        - unit * jnp.mean(along * unit, axis=-1, keepdims=True)
    )
    return (inner * scaled, jnp.sum(upstream * unit, axis=0), jnp.sum(upstream, axis=0))


def gelu_slope(values):
    return (
        0.5 * (1.0 + lax.erf(values * SQRT_HALF))
        + values * jnp.exp(-0.5 * values * values) * INV_ROOT_TWO_PI
    )


def softmax_rows(scores):
    top = jnp.max(scores, axis=-1, keepdims=True)
    expo = jnp.exp(scores - top)
    total = jnp.sum(expo, axis=-1, keepdims=True)
    return (expo / total, top[..., 0] + jnp.log(total[..., 0]))


def shards(
    frames_in,
    text_states,
    clip_lengths,
    self_gain,
    self_bias,
    query_weight,
    key_weight,
    value_weight,
    output_weight,
    cross_gain,
    cross_bias,
    cross_query,
    cross_key,
    cross_value,
    cross_output,
    feed_gain,
    feed_bias,
    feed_upward,
    feed_downward,
    grad_out,
):
    count = lax.axis_size("seq")
    place = lax.axis_index("seq")
    local = frames_in.shape[1]
    total_frames = local * count
    block = min(512, total_frames)
    blocks = total_frames // block
    scale = HD ** (-0.5)
    lengths = clip_lengths[0]
    slot = jnp.arange(CLIPS, dtype=jnp.int32)
    ends = jnp.sum(jnp.where(slot[None, :] <= slot[:, None], lengths[None, :], 0), axis=1)
    begins = ends - lengths
    slots = jnp.arange(CLIPS, dtype=jnp.int32)
    positions = jnp.arange(total_frames, dtype=jnp.int32)
    owner_all = jnp.sum((ends[None, :] <= positions[:, None]).astype(jnp.int32), axis=1)
    first_all = jnp.sum(jnp.where(owner_all[:, None] == slots[None, :], begins[None, :], 0), axis=1)
    owner_mine = lax.dynamic_slice_in_dim(owner_all, place * local, local, 0)
    frames = frames_in[0].astype(jnp.float32)
    text = text_states[0]
    text_rows = text.shape[0]
    weights = (query_weight, key_weight, value_weight)
    normed_low, attended, log_totals, query_heads, key_heads, value_heads, attended_frames = ka(
        count, frames_in[0], self_gain, self_bias, first_all[None], weights
    )
    cross_k = matmul(text, cross_key).astype(bf)
    cross_v = matmul(text, cross_value).astype(bf)
    clips = lax.axis_size("clip")
    dx1, output, vec, c_up, c_dn, c_o, c_cq, c_co, grad_heads, normed_all, key_own, value_own = kb(
        count,
        clips,
        attended_frames,
        frames_in[0],
        grad_out[0],
        cross_k,
        cross_v,
        owner_mine,
        cross_gain,
        cross_bias,
        feed_gain,
        feed_bias,
        output_weight,
        cross_query,
        cross_output,
        feed_upward,
        feed_downward,
        normed_low,
    )
    frames_grad, vec, key_low, value_low, *mats = kc(
        count,
        clips,
        (query_heads, key_heads, value_heads, attended, grad_heads),
        log_totals,
        first_all[None],
        key_own,
        value_own,
        text,
        frames_in[0],
        dx1,
        self_gain,
        vec,
        normed_all,
        weights,
        (c_up, c_dn, c_o, c_cq, c_co),
    )
    text_grad = right_times(key_low, cross_key) + right_times(value_low, cross_value)
    w_up, w_dn, w_o, w_cq, w_co, w_xk, w_xv, w_q, w_k, w_v = [one.astype(f32) for one in mats]
    width_out = D // clips
    vec = lax.dynamic_slice_in_dim(vec, lax.axis_index("clip") * width_out, width_out, 1)
    return (
        output[None],
        frames_grad[None],
        text_grad[None],
        vec[4],
        vec[5],
        w_q,
        w_k,
        w_v,
        w_o,
        vec[0],
        vec[1],
        w_cq,
        w_xk,
        w_xv,
        w_co,
        vec[2],
        vec[3],
        w_up,
        w_dn,
    )


def solution(mesh):
    return jax.shard_map(
        shards,
        mesh=mesh,
        in_specs=(
            P("clip", "seq", None),
            P("clip", None, None),
            P("clip", None),
            P(),
            P(),
            P(),
            P(),
            P(),
            P(),
            P(),
            P(),
            P(),
            P(),
            P(),
            P(),
            P(),
            P(),
            P(),
            P(),
            P("clip", "seq", None),
        ),
        out_specs=(
            P("clip", "seq", None),
            P("clip", "seq", None),
            P("clip", None, None),
            P("clip"),
            P("clip"),
            P("clip", None),
            P("clip", None),
            P("clip", None),
            P("clip", None),
            P("clip"),
            P("clip"),
            P("clip", None),
            P("clip", None),
            P("clip", None),
            P("clip", None),
            P("clip"),
            P("clip"),
            P("clip", None),
            P("clip", None),
        ),
        check_vma=False,
    )
```

```python
import functools
import math

import jax
import jax.numpy as jnp
from jax import lax
from jax.experimental import pallas as pl
from jax.experimental.pallas import tpu as pltpu
from jax.sharding import PartitionSpec as P

D = 1024
HEADS = 16
HD = 64
TEXT = 64
CLIPS = 4


EPS = 1e-05
NEG = -1e30
SQRT_HALF = 0.7071067811865476
INV_ROOT_TWO_PI = 0.3989422804014327

bf = jnp.bfloat16
f32 = jnp.float32
T, W, H, B = 2048, 256, 4, 256
LOG2E = math.log2(math.e)
C2 = LOG2E / 8.0
NT = (((1,), (1,)), ((), ()))
NN = (((1,), (0,)), ((), ()))
TN = (((0,), (0,)), ((), ()))


def dg(a, b, d):
    return lax.dot_general(a, b, d, preferred_element_type=f32)


def lanemask(rows,h):
    l=lax.broadcasted_iota(jnp.int32,(rows,W),1)
    return (l//HD)==h
def add_blocks(out, ins, rows, cols):
    step = max(16, min(rows, 65536 // cols))

    def body(i, carry):
        r = pl.ds(pl.multiple_of(i * step, 16), step)
        total = ins[0][r, :].astype(f32)
        for one in ins[1:]:
            total = total + one[r, :].astype(f32)
        out[r, :] = total.astype(bf)
        return carry

    lax.fori_loop(0, rows // step, body, 0)


def each(count, fn):
    def body(i, x):
        fn(i)
        return x

    lax.fori_loop(0, count, body, 0)


def tile_of(i, size=256):
    return pl.ds(pl.multiple_of(i * size, size), size)


def unit_rows(v):
    center = v - jnp.mean(v, axis=-1, keepdims=True)
    scaled = lax.rsqrt(jnp.mean(center * center, axis=-1, keepdims=True) + EPS)
    return center * scaled, scaled


def norm_rows(src, gain, bias, dst, rows):
    def chunk(i):
        r = tile_of(i, 128)
        unit, _ = unit_rows(src[r, :])
        dst[r, :] = (unit * gain[...] + bias[...]).astype(bf)

    each(rows // 128, chunk)


def norm_back_rows(up, src, gain, add, dst, dst_low, rows):
    def chunk(i, sums):
        r = tile_of(i, 64)
        unit, scaled = unit_rows(src[r, :])
        u = up[r, :]
        along = u * gain[...]
        inner = (
            along
            - jnp.mean(along, axis=-1, keepdims=True)
            - unit * jnp.mean(along * unit, axis=-1, keepdims=True)
        )
        total = add[r, :].astype(f32) + inner * scaled
        dst[r, :] = total
        dst_low[r, :] = total.astype(bf)
        fold = lambda v: jnp.sum(v.reshape(8, 8, v.shape[1]), axis=0)
        return sums[0] + fold(u * unit), sums[1] + fold(u)

    zero = jnp.zeros((8, src.shape[1]), f32)
    a, b = lax.fori_loop(0, rows // 64, chunk, (zero, zero))
    return jnp.sum(a, axis=0, keepdims=True), jnp.sum(b, axis=0, keepdims=True)


def remote(src, dst, send, recv, **where):
    return pltpu.make_async_remote_copy(
        src_ref=src, dst_ref=dst, send_sem=send, recv_sem=recv, device_id=where,
        device_id_type=pl.DeviceIdType.MESH,
    )


def greet(env, halves):
    s, c, z, seqs = env["s"], env["c"], env["z"], env["seqs"]
    whom = [{"clip": 2 * z + 1 - c}, {"clip": beside(env)}]
    whom += [{"seq": lax.rem(s + k, seqs)} for k in range(1, seqs)]
    whom += [
        {"clip": 2 * (2 * lax.rem(env["zh"] + k, halves) + env["zl"]) + c} for k in range(1, halves)
    ]
    barrier = pltpu.get_barrier_semaphore()
    for one in whom:
        pl.semaphore_signal(barrier, inc=1, device_id=one, device_id_type=pl.DeviceIdType.MESH)
    pl.semaphore_wait(barrier, len(whom))


def greet_all(env, clips):
    s, seqs = env["s"], env["seqs"]
    b = 2 * env["z"] + env["c"]
    whom = [{"seq": lax.rem(s + k, seqs)} for k in range(1, seqs)]
    whom += [{"clip": lax.rem(b + k, clips)} for k in range(1, clips)]
    barrier = pltpu.get_barrier_semaphore()
    for one in whom:
        pl.semaphore_signal(barrier, inc=1, device_id=one, device_id_type=pl.DeviceIdType.MESH)
    pl.semaphore_wait(barrier, len(whom))


def place(seqs):
    b = lax.axis_index("clip")
    z = lax.div(b, 2)
    return dict(
        seqs=seqs, s=lax.axis_index("seq"), c=lax.rem(b, 2), z=z, zh=lax.div(z, 2), zl=lax.rem(z, 2)
    )


def beside(env):
    return 2 * (2 * env["zh"] + 1 - env["zl"]) + env["c"]


def kb_kernel(seqs, *refs):
    (
        att, x_ref, gb, ck, cv, owner, g2, b2, g3, b3,
        w_o, w_cq, w_co, w_up, w_dn, n1_hbm,
    ) = refs[:16]
    (x1, fo, vec, c_up, c_dn, c_o, c_cq, c_co, heads, n1_all, kq, vq) = refs[16:28]
    (
        ring, up_st, dn_st, up_rv, dn_rv, sq_rv, x2, n2, n3, n3t, cq, co, probs, u, ut, dh,
        acc, dn3, up_nr, up_fr, dn_sr, kv_low, kv_rv, ring_sem, st_send, st_recv, out_sem, n1_sem, head_sem, kv_sem,
        near_sem, far_sem, seq_sem,
    ) = refs[28:]
    env = place(seqs)
    s, c, z = env["s"], env["c"], env["z"]
    rows, d = x_ref.shape
    halves, rb = up_rv.shape[0], up_rv.shape[2]
    pairs, zl = 2 * halves, env["zl"]
    ppc, rbd = dn_st.shape[0], dn_st.shape[2]
    steps = w_up.shape[1] // d
    width = d // seqs
    texts = ck.shape[0]
    depth = ring.shape[0]

    items = [w_o, w_cq, w_co]
    for t in range(steps):
        items += [w_up.at[:, pl.ds(t * d, d)], w_dn.at[pl.ds(t * d, d), :]]
    items += [w_co, w_cq, w_o]

    def load(i):
        return pltpu.make_async_copy(items[i], ring.at[i % depth], ring_sem.at[i % depth])

    def take(i):
        load(i).wait()
        return ring.at[i % depth]

    def drop(i):
        if i + depth < len(items):
            load(i + depth).start()

    for i in range(depth):
        load(i).start()
    greet(env, halves)

    peers = [(k, lax.rem(s + k, seqs)) for k in range(1, seqs)]
    spots = pl.ds(pl.multiple_of(s * rows, rows), rows)
    by_x, by_y = s + 1 - 2 * lax.rem(s, 2), lax.rem(s + 2, 4)
    here = lambda who, part: n1_all.at[
        pl.ds(pl.multiple_of(who * rows + part * (rows // 2), rows // 2), rows // 2), :
    ]
    n1_out = [
        remote(n1_hbm, n1_all.at[spots, :], n1_sem.at[0, k], n1_sem.at[1, k], seq=to)
        for k, to in ((1, by_x), (2, by_y))
    ]
    n1_on = [
        remote(here(by_y, 0), here(by_y, 0), n1_sem.at[0, 3], n1_sem.at[1, 3], seq=by_x),
        remote(here(by_x, 1), here(by_x, 1), n1_sem.at[0, 4], n1_sem.at[1, 4], seq=by_y),
    ]
    n1_own = pltpu.make_async_copy(n1_hbm, n1_all.at[spots, :], n1_sem.at[0, 0])
    start(n1_out)
    n1_own.start()

    w = take(0)

    def f(t):
        x1[:, tile_of(t)] = x_ref[:, tile_of(t)].astype(f32) + dg(att[...], w[:, tile_of(t)], NN)

    each(d // 256, f)
    drop(0)
    norm_rows(x1, g2, b2, n2, rows)
    w = take(1)

    def f(t):
        cq[:, tile_of(t)] = dg(n2[...], w[:, tile_of(t)], NN).astype(bf)

    each(d // 256, f)
    drop(1)
    half = 256
    key_clip = lax.broadcasted_iota(jnp.int32, (half, texts), 1) // TEXT

    def masked(v, h):
        lane = lax.broadcasted_iota(jnp.int32, v.shape, 1)
        return jnp.where(lane // HD == h, v, jnp.zeros_like(v))

    def f(n):
        t, r = lax.div(n, rows // half), tile_of(lax.rem(n, rows // half), half)
        allowed = owner[r, :] == key_clip
        q, k, v = cq[r, tile_of(t)], ck[:, tile_of(t)], cv[:, tile_of(t)]
        total = jnp.zeros((half, 256), f32)
        for h in range(256 // HD):
            sc = jnp.where(allowed, dg(masked(q, h), k, NT), NEG)
            p = jnp.exp2((sc - jnp.max(sc, axis=-1, keepdims=True)) * C2)
            p = (p / jnp.sum(p, axis=-1, keepdims=True)).astype(bf)
            probs[t * (256 // HD) + h, r, :] = p
            total = total + dg(p, masked(v, h), NN)
        co[r, tile_of(t)] = total.astype(bf)

    each(d // 256 * (rows // half), f)
    w = take(2)

    def f(t):
        x2[:, tile_of(t)] = x1[:, tile_of(t)] + dg(co[...], w[:, tile_of(t)], NN)

    each(d // 256, f)
    drop(2)
    norm_rows(x2, g3, b3, n3, rows)

    def turn(src, dst):
        def f(t):
            dst[tile_of(t), :] = src[:, tile_of(t)].T

        each(d // 256, f)

    turn(n3, n3t)
    arrive(n1_out)
    start(n1_on)

    def swap(n, src, dst):
        return remote(src, dst, st_send.at[n], st_recv.at[n], clip=2 * z + 1 - c)

    def up_swap(t):
        return swap(2 * t, up_st.at[0, :, :, 1 - c], up_rv.at[:, :, :, pl.ds(t * d, d)])

    def dn_swap(t):
        return swap(2 * t + 1, dn_st.at[:, 1 - c], dn_rv.at[pl.ds(t * ppc, ppc)])

    def up_near(t):
        cols = pl.ds(t * d, d)
        return remote(
            up_rv.at[:, 1 - zl, :, cols], up_nr.at[:, :, cols], near_sem.at[0, t], near_sem.at[1, t],
            clip=beside(env),
        )

    def dn_seq(t):
        blocks = pl.ds(t * ppc, ppc)
        return [
            remote(
                dn_rv.at[blocks, :, pl.ds(pl.multiple_of(to * width, 128), width)], dn_sr.at[k - 1, blocks],
                seq_sem.at[0, t, k], seq_sem.at[1, t, k], seq=to,
            )
            for k, to in peers
        ]

    def up_out(t):
        cols = pl.ds(t * d, d)
        return pltpu.make_async_copy(up_fr.at[0, :, cols], c_up.at[:, cols], out_sem.at[2 * t])

    def up_far(t):
        cols = pl.ds(t * d, d)
        copies = []
        for k in range(1, halves):
            to = lax.rem(env["zh"] + k, halves)
            copies.append(
                remote(
                    up_nr.at[to, :, cols], up_fr.at[k - 1, :, cols], far_sem.at[0, t, k], far_sem.at[1, t, k],
                    clip=2 * (2 * to + zl) + c,
                )
            )
        return copies

    def dn_out(t):
        blocks = pl.ds(t * ppc, ppc)
        return pltpu.make_async_copy(dn_sr.at[0, blocks], c_dn.at[blocks], out_sem.at[2 * t + 1])

    def settle(t):
        cols = pl.ds(t * d, d)
        one = up_swap(t)
        one.wait_recv()
        for p in range(halves):
            for l in range(2):
                dst = up_rv.at[p, l, :, cols]
                add_blocks(dst, [dst, up_st.at[0, p, l, c]], rb, d)
        one.wait_send()
        up_near(t).start()
        one = dn_swap(t)
        one.wait_recv()
        for p in range(ppc):
            dst = dn_rv.at[t * ppc + p]
            add_blocks(dst, [dst, dn_st.at[p, c]], rbd, d)
        one.wait_send()
        start(dn_seq(t))

    mine = pl.ds(pl.multiple_of(s * width, 128), width)

    def settle_far(t):
        cols = pl.ds(t * d, d)
        one = up_near(t)
        one.wait_recv()
        for p in range(halves):
            dst = up_nr.at[p, :, cols]
            add_blocks(dst, [dst, up_rv.at[p, zl, :, cols]], rb, d)
        start(up_far(t))
        arrive(dn_seq(t))
        for p in range(t * ppc, (t + 1) * ppc):
            add_blocks(
                dn_sr.at[0, p],
                [dn_rv.at[p, :, mine]] + [dn_sr.at[k - 1, p] for k, _ in peers],
                rbd,
                width,
            )
        dn_out(t).start()

    def settle_last(t):
        cols = pl.ds(t * d, d)
        arrive(up_far(t))
        others = [up_fr.at[k - 1, :, cols] for k in range(1, halves)]
        add_blocks(up_fr.at[0, :, cols], [up_nr.at[env["zh"], :, cols]] + others, rb, d)
        up_out(t).start()

    for t in range(steps):
        wu, wd = take(3 + 2 * t), take(4 + 2 * t)

        def f(i):
            h = dg(n3[...], wu[:, tile_of(i)], NN)
            du = dg(gb[...], wd[tile_of(i), :], NT)
            part = 0.5 * (1.0 + lax.erf(h * SQRT_HALF))
            slope = part + h * jnp.exp2(h * h * (-0.5 * LOG2E)) * INV_ROOT_TWO_PI
            dh[:, tile_of(i)] = (du * slope).astype(bf)
            act = (h * part).astype(bf)
            u[:, tile_of(i)] = act
            ut[tile_of(i), :] = act.T

        each(d // 256, f)
        if t > 0:
            settle(t - 1)

        def f(i, t=t):
            a = dg(u[...], wd[:, tile_of(i)], NN)
            b = dg(dh[...], wu[tile_of(i), :], NT)
            if t == 0:
                acc[:, tile_of(i)] = a
                dn3[:, tile_of(i)] = b
            else:
                acc[:, tile_of(i)] += a
                dn3[:, tile_of(i)] += b
            g = dg(n3t[...], dh[:, tile_of(i)], NN).astype(bf)
            up_st[0, :, :, :, :, tile_of(i)] = g.reshape(halves, 2, 2, rb, 256)
            g = dg(ut[...], gb[:, tile_of(i)], NN).astype(bf)
            dn_st[:, :, :, tile_of(i)] = g.reshape(ppc, 2, rbd, 256)

        each(d // 256, f)
        drop(3 + 2 * t)
        drop(4 + 2 * t)
        up_swap(t).start()
        dn_swap(t).start()

    def f(i):
        r = tile_of(i, 64)
        fo[r, :] = (x2[r, :] + acc[r, :]).astype(bf)

    each(rows // 64, f)
    base = 3 + 2 * steps
    low = u
    sums = norm_back_rows(dn3, x2, g3, gb, acc, low, rows)
    vec[2:3, :], vec[3:4, :] = sums
    w = take(base)
    dco = dh

    def f(t):
        dco[:, tile_of(t)] = dg(low[...], w[tile_of(t), :], NT).astype(bf)

    each(d // 256, f)
    drop(base)
    settle(steps - 1)
    settle_far(0)
    settle_far(1)

    def grad(n, slot, a, low):
        turn(a, n3t)

        def f(t):
            g = dg(n3t[...], low[:, tile_of(t)], NN).astype(bf)
            up_st[slot, :, :, :, :, tile_of(t)] = g.reshape(halves, 2, 2, rb, 256)

        each(d // 256, f)
        grad_swap(n, slot).start()

    def grad_swap(n, slot):
        return swap(2 * steps + n, up_st.at[slot, :, :, 1 - c], sq_rv.at[n])

    def grad_out(n):
        return pltpu.make_async_copy(sq_rv.at[n], (c_co, c_cq, c_o)[n], out_sem.at[2 * steps + n])

    def grad_settle(n, slot):
        one = grad_swap(n, slot)
        one.wait_recv()
        for p in range(halves):
            for l in range(2):
                add_blocks(sq_rv.at[n, p, l], [sq_rv.at[n, p, l], up_st.at[slot, p, l, c]], rb, d)
        one.wait_send()
        grad_out(n).start()

    grad(0, 0, co, low)
    dcq = n3

    def f(t):
        k, v = ck[:, tile_of(t)], cv[:, tile_of(t)]
        sum_k = jnp.zeros((texts, 256), f32)
        sum_v = jnp.zeros((texts, 256), f32)
        for n in range(rows // half):
            r = pl.ds(n * half, half)
            q, g = cq[r, tile_of(t)], dco[r, tile_of(t)]
            out = jnp.zeros((half, 256), f32)
            for h in range(256 // HD):
                p_low = probs[t * (256 // HD) + h, r, :]
                p = p_low.astype(f32)
                dp = dg(masked(g, h), v, NT)
                inner = jnp.sum(p * dp, axis=-1, keepdims=True)
                ds = (p * (dp - inner)).astype(bf)
                out = out + dg(ds, masked(k, h), NN)
                sum_k = sum_k + dg(ds, masked(q, h), TN)
                sum_v = sum_v + dg(p_low, masked(g, h), TN)
            dcq[r, tile_of(t)] = (out * 0.125).astype(bf)
        kv_low[0, :, tile_of(t)] = (sum_k * 0.125).astype(bf)
        kv_low[1, :, tile_of(t)] = sum_v.astype(bf)

    each(d // 256, f)
    for t in range(2, steps - 1):
        settle_far(t)
    settle_last(0)
    kv_out = [
        remote(
            kv_low.at[:, :, pl.ds(pl.multiple_of(to * width, 128), width)], kv_rv.at[k - 1],
            kv_sem.at[0, k], kv_sem.at[1, k], seq=to,
        )
        for k, to in peers
    ]
    start(kv_out)
    w = take(base + 1)
    dn2 = dn3

    def f(t):
        dn2[:, tile_of(t)] = dg(dcq[...], w[tile_of(t), :], NT)

    each(d // 256, f)
    drop(base + 1)
    sums = norm_back_rows(dn2, x1, g2, acc, x1, low, rows)
    vec[0:1, :], vec[1:2, :] = sums
    vec[4:8, :] = jnp.zeros((4, d), f32)
    w = take(base + 2)
    do = dh

    def f(t):
        do[:, tile_of(t)] = dg(low[...], w[tile_of(t), :], NT).astype(bf)

    each(d // 256, f)
    head_out = [
        remote(
            do.at[:, pl.ds(pl.multiple_of(to * width, 128), width)], heads.at[spots, :],
            head_sem.at[0, k], head_sem.at[1, k], seq=to,
        )
        for k, to in peers
    ]
    head_own = pltpu.make_async_copy(do.at[:, mine], heads.at[spots, :], head_sem.at[0, 0])
    start(head_out)
    head_own.start()
    grad_settle(0, 0)
    grad(1, 0, n2, dcq)
    settle_far(steps - 1)
    for t in range(1, steps - 1):
        settle_last(t)
    grad_settle(1, 0)
    grad(2, 0, att, low)
    arrive(kv_out)
    for n, dst in enumerate((kq, vq)):
        total = kv_low[n, :, mine].astype(f32)
        for k in range(1, seqs):
            total = total + kv_rv[k - 1, n].astype(f32)
        dst[...] = total.astype(bf)
    settle_last(steps - 1)
    grad_settle(2, 0)
    finish(kv_out)
    head_own.wait()
    n1_own.wait()
    for one in head_out + n1_on:
        one.wait()
    finish(n1_out)
    for t in range(steps):
        up_near(t).wait_send()
        finish(up_far(t))
        finish(dn_seq(t))
        up_out(t).wait()
        dn_out(t).wait()
    for n in range(3):
        grad_out(n).wait()


def kb(seqs, clips, att, x, gb, ck, cv, owner, g2, b2, g3, b3, w_o, w_cq, w_co, w_up, w_dn, n1):
    rows, d = x.shape
    pairs = clips // 2
    halves = pairs // 2
    rb, rbd = d // clips, w_dn.shape[0] // clips
    steps = w_up.shape[1] // d
    ppc = pairs // steps
    texts = ck.shape[0]
    width = d // seqs
    hbm = pl.BlockSpec(memory_space=pl.ANY)
    vmem = pl.BlockSpec(memory_space=pltpu.VMEM)
    low = lambda *shape: pltpu.VMEM(shape, bf)
    full = lambda *shape: pltpu.VMEM(shape, f32)
    s_low = lambda *shape: jax.ShapeDtypeStruct(shape, bf)
    dma = pltpu.SemaphoreType.DMA
    return pl.pallas_call(
        functools.partial(kb_kernel, seqs),
        out_shape=[
            jax.ShapeDtypeStruct((rows, d), f32),
            s_low(rows, d),
            jax.ShapeDtypeStruct((8, d), f32),
            s_low(rb, steps * d),
            s_low(pairs, rbd, width),
            s_low(halves, 2, rb, d),
            s_low(halves, 2, rb, d),
            s_low(halves, 2, rb, d),
            s_low(rows * seqs, width),
            s_low(rows * seqs, d),
            s_low(texts, width),
            s_low(texts, width),
        ],
        in_specs=[vmem] * 10 + [hbm] * 6,
        out_specs=[vmem] * 3 + [hbm] * 7 + [vmem] * 2,
        scratch_shapes=[
            low(4, d, d),
            low(1, halves, 2, 2, rb, d),
            low(ppc, 2, rbd, d),
            low(halves, 2, rb, steps * d),
            low(pairs, rbd, d),
            low(3, halves, 2, rb, d),
            full(rows, d),
            low(rows, d),
            low(rows, d),
            low(d, rows),
            low(rows, d),
            low(rows, d),
            low(d // HD, rows, texts),
            low(rows, d),
            low(d, rows),
            low(rows, d),
            full(rows, d),
            full(rows, d),
            low(halves, rb, steps * d),
            low(max(1, halves - 1), rb, steps * d),
            low(seqs - 1, pairs, rbd, width),
            low(2, texts, d),
            low(seqs - 1, 2, texts, width),
            dma((4,)),
            dma((2 * steps + 3,)),
            dma((2 * steps + 3,)),
            dma((2 * steps + 3,)),
            dma((2, 5)),
            dma((2, seqs)),
            dma((2, seqs)),
            dma((2, steps)),
            dma((2, steps, halves)),
            dma((2, steps, seqs)),
        ],
        compiler_params=pltpu.CompilerParams(
            collective_id=2, has_side_effects=True, vmem_limit_bytes=60 * 2**20
        ),
    )(
        att, x, gb, ck, cv, owner[:, None],
        *[v[None] for v in (g2, b2, g3, b3)],
        w_o, w_cq, w_co, w_up, w_dn, n1,
    )


def ka_kernel(seqs, *refs):
    x_ref, g1, b1, first, w_q, w_k, w_v = refs[:7]
    n1, o_ref, lse_ref, q_out, k_out, v_out, att = refs[7:14]
    w_buf, wide, stage, held, vt, w_sem, send, recv, push_send, push_recv, out_sem = refs[14:]
    env = place(seqs)
    s = env["s"]
    rows, d = x_ref.shape
    pair = 2 * HD
    loads = [
        pltpu.make_async_copy(one, w_buf.at[n], w_sem.at[n]) for n, one in enumerate((w_q, w_k, w_v))
    ]
    start(loads)
    greet_seq(env)

    def f(i):
        r = tile_of(i, 64)
        wide[r, :] = x_ref[r, :].astype(f32)

    each(rows // 64, f)
    norm_rows(wide, g1, b1, n1, rows)
    spots = pl.ds(pl.multiple_of(s * rows, rows), rows)
    peers = [(k, lax.rem(s + k, seqs)) for k in range(1, seqs)]

    def sends(g):
        return [
            remote(
                stage.at[:, :, pl.ds(pl.multiple_of(to * W + g * pair, 128), pair)],
                held.at[:, spots, pl.ds(g * pair, pair)],
                send.at[g, k], recv.at[g, k], seq=to,
            )
            for k, to in peers
        ]

    for one in loads:
        one.wait()
    first_sends = sends(0)
    for n, (k, to) in enumerate(peers):
        cols = pl.ds(pl.multiple_of(to * W, 128), W)
        for t in range(3):
            stage[t, :, cols] = dg(n1[...], w_buf[t, :, cols], NN).astype(bf)
        first_sends[n].start()
    cols = pl.ds(pl.multiple_of(s * W, 128), W)
    for t in range(3):
        held[t, spots, :] = dg(n1[...], w_buf[t, :, cols], NN).astype(bf)

    lane = lax.broadcasted_iota(jnp.int32, (1, pair), 1) // HD
    kvi = lax.broadcasted_iota(jnp.int32, (rows, rows), 0)
    qi = lax.broadcasted_iota(jnp.int32, (rows, rows), 1)

    def qblock(g, i, masked):
        ln = pl.ds(g * pair, pair)
        r = tile_of(i, rows)
        q = held[0, r, ln]
        qm = [jnp.where(lane == h, q, jnp.zeros_like(q)) for h in range(2)]
        fst = first[:, r]

        def step(j, carry, diag):
            c = tile_of(j, rows)
            k = held[1, c, ln]
            out = []
            for h in range(2):
                m, l, acc = carry[h]
                sc = dg(k, qm[h], NT)
                if diag:
                    sc = jnp.where(kvi <= qi, sc, NEG)
                if masked:
                    sc = jnp.where(kvi + j * rows >= fst, sc, NEG)
                top = jnp.maximum(m, jnp.max(sc, axis=0, keepdims=True))
                p = jnp.exp2((sc - top) * C2)
                a = jnp.exp2((m - top) * C2)
                l = l * a + jnp.sum(p, axis=0, keepdims=True)
                acc = acc * a + dg(vt[h * HD : (h + 1) * HD, c], p.astype(bf), NN)
                out.append((top, l, acc))
            return tuple(out)

        carry = tuple(
            (jnp.full((1, rows), NEG, f32), jnp.zeros((1, rows), f32), jnp.zeros((HD, rows), f32))
            for _ in range(2)
        )
        carry = lax.fori_loop(0, i, lambda j, x: step(j, x, False), carry)
        carry = step(i, carry, True)
        ot = jnp.concatenate([acc / l for _, l, acc in carry], axis=0)
        o_ref[r, ln] = ot.T.astype(bf)
        for h in range(2):
            lse_ref[2 * g + h : 2 * g + h + 1, r] = carry[h][0] * C2 + jnp.log2(carry[h][1])

    def push(g, owner, away):
        src = o_ref.at[tile_of(owner, rows), pl.ds(g * pair, pair)]
        dst = att.at[:, pl.ds(pl.multiple_of(s * W + g * pair, 128), pair)]
        k = lax.rem(owner - s + seqs, seqs)
        if away:
            return remote(src, dst, push_send.at[g, owner], push_recv.at[g, k], seq=owner)
        return pltpu.make_async_copy(src, dst, push_send.at[g, owner])

    def send_rows(g, owner):
        @pl.when(s != owner)
        def _():
            push(g, owner, True).start()

        @pl.when(s == owner)
        def _():
            push(g, owner, False).start()

    lse_ref[4:8, :] = jnp.zeros((4, lse_ref.shape[1]), f32)
    for g in range(2):
        arrive(sends(g))
        if g == 0:
            start(sends(1))
        else:
            outs = [
                pltpu.make_async_copy(held.at[n], one, out_sem.at[n])
                for n, one in enumerate((q_out, k_out, v_out))
            ]
            start(outs)

        def f(i, g=g):
            r = tile_of(i, rows)
            vt[:, r] = held[2, r, pl.ds(g * pair, pair)].T

        each(seqs, f)

        def f(i, g=g):
            qblock(g, i, False)
            send_rows(g, i)

        plain = TAIL // rows
        each(plain, f)
        for i in range(plain, seqs):
            qblock(g, i, True)
            send_rows(g, i)
    for one in outs:
        one.wait()
    for g in range(2):
        finish(sends(g))
        for owner in range(seqs):
            @pl.when(s != owner)
            def _():
                push(g, owner, True).wait_send()

            @pl.when(s == owner)
            def _():
                push(g, owner, False).wait()
        for k in range(1, seqs):
            back = lax.rem(s - k + seqs, seqs)
            dst = att.at[:, pl.ds(pl.multiple_of(back * W + g * pair, 128), pair)]
            pltpu.make_async_copy(dst, dst, push_recv.at[g, k]).wait()


def greet_seq(env):
    s, seqs = env["s"], env["seqs"]
    barrier = pltpu.get_barrier_semaphore()
    for k in range(1, seqs):
        pl.semaphore_signal(
            barrier, inc=1, device_id={"seq": lax.rem(s + k, seqs)}, device_id_type=pl.DeviceIdType.MESH
        )
    pl.semaphore_wait(barrier, seqs - 1)


def ka(seqs, x, g1, b1, first, weights):
    rows, d = x.shape
    hbm = pl.BlockSpec(memory_space=pl.ANY)
    vmem = pl.BlockSpec(memory_space=pltpu.VMEM)
    dma = pltpu.SemaphoreType.DMA
    s_low = lambda *shape: jax.ShapeDtypeStruct(shape, bf)
    total = rows * seqs
    return pl.pallas_call(
        functools.partial(ka_kernel, seqs),
        out_shape=[
            s_low(rows, d),
            s_low(total, W),
            jax.ShapeDtypeStruct((8, total), f32),
            s_low(total, W),
            s_low(total, W),
            s_low(total, W),
            s_low(rows, d),
        ],
        in_specs=[vmem] * 4 + [hbm] * 3,
        out_specs=[vmem] * 3 + [hbm] * 4,
        scratch_shapes=[
            pltpu.VMEM((3, d, d), bf),
            pltpu.VMEM((rows, d), f32),
            pltpu.VMEM((3, rows, d), bf),
            pltpu.VMEM((3, total, W), bf),
            pltpu.VMEM((2 * HD, total), bf),
            dma((3,)),
            dma((2, seqs)),
            dma((2, seqs)),
            dma((2, seqs)),
            dma((2, seqs)),
            dma((3,)),
        ],
        compiler_params=pltpu.CompilerParams(
            collective_id=3, has_side_effects=True, vmem_limit_bytes=50 * 2**20
        ),
    )(x, g1[None], b1[None], first, *weights)


class Job:
    def __init__(self, steps, part, bufs, sems, out, env, halves):
        self.steps, self.part, self.out, self.env, self.halves = steps, part, out, env, halves
        self.r0, self.rm, self.rn, self.rf, self.rs = bufs
        self.sems = sems
        self.rb, self.n = part.shape[-2:]
        self.first = "split" in steps
        self.q = self.n // env["seqs"] if "seq" in steps or self.first else self.n
        self.done = self.rs if "seq" in steps else self.rf
        self.bare = steps == ("seq",)
        self.cored = self.r0 if "cores" in steps else (self.rs.at[0] if self.first else part)
        self.w = self.q if self.first else self.n

    def copy(self, stage, k, src, dst, **where):
        return remote(src, dst, self.sems.at[0, stage, k], self.sems.at[1, stage, k], **where)

    def cores(self):
        e = self.env
        return [
            self.copy(0, 0, self.part.at[:, :, 1 - e["c"]], self.r0, clip=2 * e["z"] + 1 - e["c"])
        ]

    def sum_cores(self):
        for p in range(self.halves):
            for l in range(2):
                one = self.r0.at[p, l]
                add_blocks(one, [one, self.part.at[p, l, self.env["c"]]], self.rb, self.n)

    def split(self):
        e, copies = self.env, []
        for k in range(1, e["seqs"]):
            to = lax.rem(e["s"] + k, e["seqs"])
            copies.append(
                self.copy(3, k - 1, self.part.at[:, :, :, self.columns(to)], self.rs.at[k - 1], seq=to)
            )
        return copies

    def sum_split(self):
        self.load().wait()
        for p in range(self.halves):
            for l in range(2):
                others = [self.rs.at[k, p, l] for k in range(self.env["seqs"] - 1)]
                add_blocks(self.rs.at[0, p, l], [self.rm.at[p, l]] + others, self.rb, self.q)

    def load(self):
        if self.first or self.bare:
            at = (slice(None),) * (len(self.part.shape) - 1) + (self.columns(self.env["s"]),)
            src = self.part.at[at]
            return pltpu.make_async_copy(src, self.rm, self.sems.at[0, 5, 0])
        src = self.part.at[:, self.env["zl"]] if "near" in self.steps else self.part.at[self.env["zh"]]
        return pltpu.make_async_copy(src, self.rm, self.sems.at[0, 5, 0])

    def near(self):
        return [self.copy(1, 0, self.cored.at[:, 1 - self.env["zl"]], self.rn, clip=beside(self.env))]

    def sum_near(self):
        loaded = "cores" not in self.steps and not self.first
        if loaded:
            self.load().wait()
        for p in range(self.halves):
            mine = self.rm.at[p] if loaded else self.cored.at[p, self.env["zl"]]
            add_blocks(self.rn.at[p], [self.rn.at[p], mine], self.rb, self.w)

    def far(self):
        e, copies = self.env, []
        src = self.rn if "near" in self.steps else self.part
        for k in range(1, self.halves):
            to = lax.rem(e["zh"] + k, self.halves)
            copies.append(
                self.copy(2, k - 1, src.at[to], self.rf.at[k - 1], clip=2 * (2 * to + e["zl"]) + e["c"])
            )
        return copies

    def sum_far(self):
        if "near" in self.steps:
            mine = self.rn.at[self.env["zh"]]
        else:
            self.load().wait()
            mine = self.rm
        add_blocks(self.rf.at[0], [mine] + [self.rf.at[k] for k in range(self.halves - 1)], self.rb, self.w)

    def columns(self, s):
        return pl.ds(pl.multiple_of(s * self.q, 128), self.q)

    def seq(self):
        e, copies = self.env, []
        for k in range(1, e["seqs"]):
            to = lax.rem(e["s"] + k, e["seqs"])
            src = self.part.at[:, self.columns(to)] if self.bare else self.rf.at[0, :, self.columns(to)]
            copies.append(self.copy(3, k - 1, src, self.rs.at[k - 1], seq=to))
        return copies

    def sum_seq(self):
        if self.bare:
            self.load().wait()
            mine = self.rm
        else:
            mine = self.rf.at[0, :, self.columns(self.env["s"])]
        others = [self.rs.at[k] for k in range(self.env["seqs"] - 1)]
        add_blocks(self.rs.at[0], [mine] + others, self.rb, self.q)

    def gather(self):
        e, copies = self.env, []
        for k in range(1, e["seqs"]):
            to = lax.rem(e["s"] + k, e["seqs"])
            copies.append(
                self.copy(4, k - 1, self.done.at[0], self.out.at[:, self.columns(e["s"])], seq=to)
            )
        return copies

    def keep(self):
        return pltpu.make_async_copy(
            self.done.at[0], self.out.at[:, self.columns(self.env["s"])], self.sems.at[1, 5, 0]
        )

    def spread(self):
        start(self.gather())
        self.keep().start()

    def close(self):
        for name in self.steps:
            finish(getattr(self, name)())
        finish(self.gather())
        self.keep().wait()
        arrive(self.gather())


def start(copies):
    for one in copies:
        one.start()


def arrive(copies):
    for one in copies:
        one.wait_recv()


def finish(copies):
    for one in copies:
        one.wait_send()


def job_bufs(steps, shape, seqs, halves):
    rb, n = shape[-2:]
    low = lambda use, *dims: pltpu.VMEM(dims if use else (16, 128), bf)
    cores, near, split = ("cores" in steps), ("near" in steps), ("split" in steps)
    q = n // seqs
    w = q if split else n
    mine = (halves, 2, rb, q) if split else ((halves, rb, n) if near else (rb, q))
    return [
        low(cores, halves, 2, rb, n),
        low(not cores, *mine),
        low(near, halves, rb, w),
        low("far" in steps, max(1, halves - 1), rb, w),
        pltpu.VMEM((seqs - 1, halves, 2, rb, q), bf) if split else low("seq" in steps, seqs - 1, rb, q),
    ]


LAST = pl.DeviceIdType.MESH


def kc_kernel(seqs, halves, *refs):
    (q_ref, k_ref, v_ref, o_ref, g_ref, lse_ref, first_ref) = refs[:7]
    (kq, vq, text, x_ref, dx1, g1, vec_in, n1_hbm, w_q, w_k, w_v, *parts) = refs[7:23]
    (frames_grad, vec, k_all, v_all, *outs) = refs[23:37]
    dq_s, dk_s, dv_s, dka, dva, n1_buf, wacc, wsum, wparts, dqkv, w_buf, dn1, vec_rv, low_buf, *rest = refs[37:]
    sems, push_send, push_recv, local_sem, kv_sem, vec_sem = rest[-6:]
    bufs = rest[:-6]
    env = place(seqs)
    s, c, z = env["s"], env["c"], env["z"]
    frames = T // seqs
    d = n1_hbm.shape[1]
    greet_all(env, 4 * halves)

    jobs = []
    for t, steps in enumerate(STEPS):
        src = parts[t] if t < 5 else wparts.at[t - 5]
        jobs.append(Job(steps, src, bufs[5 * t : 5 * t + 5], sems.at[t], outs[t], env, halves))
    up, down, go, gcq, gco, gxk, gxv, gq, gk, gv = jobs
    start(up.seq())
    start(down.near())
    start(gco.near())
    for one in (up, down, go, gcq, gco):
        one.load().start()
    width = kq.shape[1]
    spot = pl.ds(pl.multiple_of(s * width, 128), width)
    kv_out, kv_own = [], []
    for n, (src, dst) in enumerate(((kq, k_all), (vq, v_all))):
        for k in range(1, seqs):
            kv_out.append(
                remote(src, dst.at[:, spot], kv_sem.at[0, n, k], kv_sem.at[1, n, k], seq=lax.rem(s + k, seqs))
            )
        kv_own.append(pltpu.make_async_copy(src, dst.at[:, spot], kv_sem.at[0, n, 0]))
    start(kv_out)
    start(kv_own)
    loads = [pltpu.make_async_copy(n1_hbm, n1_buf, local_sem.at[0])]
    for n, one in enumerate((w_q, w_k, w_v)):
        loads.append(pltpu.make_async_copy(one, w_buf.at[n], local_sem.at[1 + n]))
    start(loads)

    def place_product(n, rb):
        wparts[n] = wacc[...].astype(bf).reshape(halves, 2, 2, rb, W)

    for n, src in enumerate((kq, vq)):
        wacc[...] = dg(text[...], src[...], TN)
        place_product(n, gxk.rb)
        start((gxk, gxv)[n].cores())

    dka[...] = jnp.zeros_like(dka)
    dva[...] = jnp.zeros_like(dva)

    lane = lax.broadcasted_iota(jnp.int32, (1, W), 1) // HD
    kvi = lax.broadcasted_iota(jnp.int32, (frames, frames), 0)
    qi = lax.broadcasted_iota(jnp.int32, (frames, frames), 1)

    def qblock(i, masked):
        r = pl.ds(i * frames, frames)
        q = q_ref[r, :]
        g = g_ref[r, :]
        both = g.astype(f32) * o_ref[r, :].astype(f32)
        hm = (
            lax.broadcasted_iota(jnp.int32, (8, W), 1) // HD == lax.broadcasted_iota(jnp.int32, (8, W), 0)
        ).astype(f32)
        delta = lax.dot_general(hm, both, NT, precision=lax.Precision.HIGHEST, preferred_element_type=f32)
        lse = lse_ref[:, r]
        fst = first_ref[:, r]
        zero = jnp.zeros_like(q)
        qm = [jnp.where(lane == h, q, zero) for h in range(H)]
        gm = [jnp.where(lane == h, g, zero) for h in range(H)]

        def tile(j, dq, diag):
            at = tile_of(j, frames)
            k = k_ref[at, :]
            v = v_ref[at, :]
            dv = jnp.zeros((frames, W), f32)
            dk = jnp.zeros((frames, W), f32)
            for h in range(H):
                p = jnp.exp2(dg(k, qm[h], NT) * C2 - lse[h : h + 1])
                if diag:
                    p = jnp.where(kvi <= qi, p, 0.0)
                if masked:
                    p = jnp.where(kvi + j * frames >= fst, p, 0.0)
                dp = dg(v, gm[h], NT)
                ds = (p * (dp - delta[h : h + 1])).astype(bf)
                dv = dv + dg(p.astype(bf), gm[h], NN)
                dk = dk + dg(ds, qm[h], NN)
                dq = dq + dg(ds, jnp.where(lane == h, k, jnp.zeros_like(k)), TN)
            dva[at, :] += dv
            dka[at, :] += dk
            return dq

        dq = jnp.zeros((frames, W), f32)
        dq = lax.fori_loop(0, i, lambda j, x: tile(j, x, False), dq)
        dq = tile(i, dq, True)
        dq_s[r, :] = (dq * 0.125).astype(bf)
        dk_s[r, :] = (dka[r, :] * 0.125).astype(bf)
        dv_s[r, :] = dva[r, :].astype(bf)

    lanes = pl.ds(pl.multiple_of(s * W, 128), W)
    moved = [(src, dqkv.at[n]) for n, src in enumerate((dq_s, dk_s, dv_s))]

    def pushes(owner):
        k = lax.rem(owner - s + seqs, seqs)
        rows = pl.ds(owner * frames, frames)
        return [
            pltpu.make_async_remote_copy(
                src_ref=src.at[rows, :],
                dst_ref=dst.at[:, lanes],
                send_sem=push_send.at[n, owner],
                recv_sem=push_recv.at[n, k],
                device_id={"seq": owner},
                device_id_type=LAST,
            )
            for n, (src, dst) in enumerate(moved)
        ]

    def keeps(owner):
        rows = pl.ds(owner * frames, frames)
        return [
            pltpu.make_async_copy(src.at[rows, :], dst.at[:, lanes], push_send.at[n, owner])
            for n, (src, dst) in enumerate(moved)
        ]

    for owner in reversed(range(seqs)):
        qblock(owner, (owner + 1) * frames > TAIL)

        @pl.when(s != owner)
        def _():
            start(pushes(owner))

        @pl.when(s == owner)
        def _():
            start(keeps(owner))

        if owner == seqs - 1:
            for one in (gcq, go):
                start(one.near())
            for one in (gxk, gxv):
                arrive(one.cores())
                one.sum_cores()
                start(one.near())
            arrive(up.seq())
            up.sum_seq()
            up.spread()
        if owner == seqs - 2:
            for one in (down, gco):
                arrive(one.near())
                one.sum_near()
                start(one.far())

    loads[0].wait()
    for one in (gxk, gxv, gcq, go):
        arrive(one.near())
        one.sum_near()
        start(one.far())

    def product(r, x):
        rows = tile_of(r, 512)
        left = n1_buf[rows, :]
        for n, src in enumerate((dq_s, dk_s, dv_s)):
            cols = pl.ds(n * W, W)
            add = dg(left, src[rows, :], TN)
            wsum[:, cols] = jnp.where(r == 0, add, wsum[:, cols] + add)
        return x

    lax.fori_loop(0, T // 512, product, 0)
    for n, one in enumerate((gq, gk, gv)):
        wparts[2 + n] = wsum[:, n * W : (n + 1) * W].astype(bf).reshape(halves, 2, 2, gq.rb, W)
        start(one.cores())
    arrive(down.far())
    down.sum_far()
    down.spread()
    for one in (gq, gk, gv):
        arrive(one.cores())
        one.sum_cores()
        start(one.near())
    arrive(gco.far())
    gco.sum_far()
    start(gco.seq())
    for one in (gxk, gxv):
        arrive(one.far())
        one.sum_far()
        one.spread()
    for one in (gcq, go):
        arrive(one.far())
        one.sum_far()
        start(one.seq())
    for one in (gq, gk, gv):
        arrive(one.near())
        one.sum_near()
        start(one.far())

    for k in range(1, seqs):
        for n in range(3):
            dst = dqkv.at[n, :, pl.ds(pl.multiple_of(lax.rem(s - k + seqs, seqs) * W, 128), W)]
            pltpu.make_async_copy(dst, dst, push_recv.at[n, k]).wait()
    for owner in range(seqs):
        @pl.when(s != owner)
        def _():
            finish(pushes(owner))

        @pl.when(s == owner)
        def _():
            for one in keeps(owner):
                one.wait()
    for n in range(3):
        loads[1 + n].wait()

        def f(t, n=n):
            add = dg(dqkv[n], w_buf[n, tile_of(t), :], NT)
            if n == 0:
                dn1[:, tile_of(t)] = add
            else:
                dn1[:, tile_of(t)] += add

        each(d // 256, f)

    def f(i):
        r = tile_of(i, 64)
        wide_x[r, :] = x_ref[r, :].astype(f32)

    wide_x = frames_grad
    each(frames // 64, f)
    vec[...] = vec_in[...]
    sums = norm_back_rows(dn1, wide_x, g1, dx1, frames_grad, low_buf, frames)
    vec[4:5, :], vec[5:6, :] = sums
    clips = 4 * halves
    b = 2 * z + c
    vec_rv[b] = vec[...]
    around = [
        remote(vec, vec_rv.at[b], vec_sem.at[0, k], vec_sem.at[1, k], clip=lax.rem(b + k, clips))
        for k in range(1, clips)
    ]
    start(around)
    for one in (gco, gcq, go):
        arrive(one.seq())
        one.sum_seq()
        one.spread()
    for one in (gq, gk, gv):
        arrive(one.far())
        one.sum_far()
        one.spread()
    arrive(around)
    finish(around)
    total = vec_rv[0]
    for k in range(1, clips):
        total = total + vec_rv[k]
    vec[...] = total
    vec_rv[clips + s] = total
    along = [
        remote(
            vec, vec_rv.at[clips + s], vec_sem.at[0, clips + k], vec_sem.at[1, clips + k],
            seq=lax.rem(s + k, seqs),
        )
        for k in range(1, seqs)
    ]
    start(along)
    arrive(along)
    finish(along)
    total = vec_rv[clips]
    for k in range(1, seqs):
        total = total + vec_rv[clips + k]
    vec[...] = total

    for one in kv_out + kv_own:
        one.wait()
    for one in jobs:
        one.close()


OWN = ("cores", "near", "far")
STEPS = (("seq",), ("near", "far")) + (("near", "far", "seq"),) * 3 + (OWN,) * 5
TAIL = 1536


def kc(seqs, clips, heads, lse, first, kq, vq, text, x, dx1, g1, vec, n1_all, weights, parts):
    halves = clips // 4
    rows, d = x.shape
    rb = d // clips
    shapes = [p.shape for p in parts] + [(halves, 2, 2, rb, W)] * 5
    bufs = []
    for steps, shape in zip(STEPS, shapes):
        bufs += job_bufs(steps, shape, seqs, halves)
    outs = [
        jax.ShapeDtypeStruct((rows, d), f32),
        jax.ShapeDtypeStruct((8, d), f32),
        jax.ShapeDtypeStruct((text.shape[0], d), bf),
        jax.ShapeDtypeStruct((text.shape[0], d), bf),
    ]
    for steps, shape in zip(STEPS, shapes):
        wide = 1 if "seq" in steps or "split" in steps else seqs
        outs.append(jax.ShapeDtypeStruct((shape[-2], shape[-1] * wide), bf))
    hbm = pl.BlockSpec(memory_space=pl.ANY)
    vmem = pl.BlockSpec(memory_space=pltpu.VMEM)
    most = max(seqs, halves)
    dma = pltpu.SemaphoreType.DMA
    return pl.pallas_call(
        functools.partial(kc_kernel, seqs, halves),
        out_shape=outs,
        in_specs=[vmem] * 14 + [hbm] * 9,
        out_specs=[vmem] * 2 + [hbm] * 12,
        scratch_shapes=[pltpu.VMEM((T, W), bf)] * 3
        + [pltpu.VMEM((T, W), f32)] * 2
        + [
            pltpu.VMEM((T, d), bf),
            pltpu.VMEM((d, W), f32),
            pltpu.VMEM((d, 3 * W), f32),
            pltpu.VMEM((5, halves, 2, 2, rb, W), bf),
            pltpu.VMEM((3, rows, d), bf),
            pltpu.VMEM((3, d, d), bf),
            pltpu.VMEM((rows, d), f32),
            pltpu.VMEM((4 * halves + seqs, 8, d), f32),
            pltpu.VMEM((rows, d), bf),
        ]
        + bufs
        + [
            dma((10, 2, 6, most)),
            dma((3, seqs)),
            dma((3, seqs)),
            dma((4,)),
            dma((2, 2, seqs)),
            dma((2, 4 * halves + seqs)),
        ],
        compiler_params=pltpu.CompilerParams(
            collective_id=1, has_side_effects=True, vmem_limit_bytes=60 * 2**20
        ),
    )(*heads, lse, first, kq, vq, text, x, dx1, g1[None], vec, n1_all, *weights, *parts)


def matmul(left, right):
    return jnp.dot(left, right, preferred_element_type=jnp.float32)


def left_times(left, right):
    return lax.dot_general(
        left, right, (((0,), (0,)), ((), ())), preferred_element_type=jnp.float32
    )


def right_times(left, right):
    return lax.dot_general(
        left, right, (((1,), (1,)), ((), ())), preferred_element_type=jnp.float32
    )


def norm_forward(values, gain, bias):
    center = values - jnp.mean(values, axis=-1, keepdims=True)
    scaled = lax.rsqrt(jnp.mean(center * center, axis=-1, keepdims=True) + EPS)
    unit = center * scaled
    return (unit * gain + bias, unit, scaled)


def norm_backward(upstream, unit, scaled, gain):
    along = upstream * gain
    inner = (
        along
        - jnp.mean(along, axis=-1, keepdims=True)
        - unit * jnp.mean(along * unit, axis=-1, keepdims=True)
    )
    return (inner * scaled, jnp.sum(upstream * unit, axis=0), jnp.sum(upstream, axis=0))


def gelu_slope(values):
    return (
        0.5 * (1.0 + lax.erf(values * SQRT_HALF))
        + values * jnp.exp(-0.5 * values * values) * INV_ROOT_TWO_PI
    )


def softmax_rows(scores):
    top = jnp.max(scores, axis=-1, keepdims=True)
    expo = jnp.exp(scores - top)
    total = jnp.sum(expo, axis=-1, keepdims=True)
    return (expo / total, top[..., 0] + jnp.log(total[..., 0]))


def shards(
    frames_in,
    text_states,
    clip_lengths,
    self_gain,
    self_bias,
    query_weight,
    key_weight,
    value_weight,
    output_weight,
    cross_gain,
    cross_bias,
    cross_query,
    cross_key,
    cross_value,
    cross_output,
    feed_gain,
    feed_bias,
    feed_upward,
    feed_downward,
    grad_out,
):
    count = lax.axis_size("seq")
    place = lax.axis_index("seq")
    local = frames_in.shape[1]
    total_frames = local * count
    block = min(512, total_frames)
    blocks = total_frames // block
    scale = HD ** (-0.5)
    lengths = clip_lengths[0]
    slot = jnp.arange(CLIPS, dtype=jnp.int32)
    ends = jnp.sum(jnp.where(slot[None, :] <= slot[:, None], lengths[None, :], 0), axis=1)
    begins = ends - lengths
    slots = jnp.arange(CLIPS, dtype=jnp.int32)
    positions = jnp.arange(total_frames, dtype=jnp.int32)
    owner_all = jnp.sum((ends[None, :] <= positions[:, None]).astype(jnp.int32), axis=1)
    first_all = jnp.sum(jnp.where(owner_all[:, None] == slots[None, :], begins[None, :], 0), axis=1)
    owner_mine = lax.dynamic_slice_in_dim(owner_all, place * local, local, 0)
    frames = frames_in[0].astype(jnp.float32)
    text = text_states[0]
    text_rows = text.shape[0]
    weights = (query_weight, key_weight, value_weight)
    normed_low, attended, log_totals, query_heads, key_heads, value_heads, attended_frames = ka(
        count, frames_in[0], self_gain, self_bias, first_all[None], weights
    )
    cross_k = matmul(text, cross_key).astype(bf)
    cross_v = matmul(text, cross_value).astype(bf)
    clips = lax.axis_size("clip")
    dx1, output, vec, c_up, c_dn, c_o, c_cq, c_co, grad_heads, normed_all, key_own, value_own = kb(
        count,
        clips,
        attended_frames,
        frames_in[0],
        grad_out[0],
        cross_k,
        cross_v,
        owner_mine,
        cross_gain,
        cross_bias,
        feed_gain,
        feed_bias,
        output_weight,
        cross_query,
        cross_output,
        feed_upward,
        feed_downward,
        normed_low,
    )
    frames_grad, vec, key_low, value_low, *mats = kc(
        count,
        clips,
        (query_heads, key_heads, value_heads, attended, grad_heads),
        log_totals,
        first_all[None],
        key_own,
        value_own,
        text,
        frames_in[0],
        dx1,
        self_gain,
        vec,
        normed_all,
        weights,
        (c_up, c_dn.reshape((-1, 2) + c_dn.shape[1:]), c_o, c_cq, c_co),
    )
    text_grad = right_times(key_low, cross_key) + right_times(value_low, cross_value)
    w_up, w_dn, w_o, w_cq, w_co, w_xk, w_xv, w_q, w_k, w_v = [one.astype(f32) for one in mats]
    width_out = D // clips
    vec = lax.dynamic_slice_in_dim(vec, lax.axis_index("clip") * width_out, width_out, 1)
    return (
        output[None],
        frames_grad[None],
        text_grad[None],
        vec[4],
        vec[5],
        w_q,
        w_k,
        w_v,
        w_o,
        vec[0],
        vec[1],
        w_cq,
        w_xk,
        w_xv,
        w_co,
        vec[2],
        vec[3],
        w_up,
        w_dn,
    )


def solution(mesh):
    return jax.shard_map(
        shards,
        mesh=mesh,
        in_specs=(
            P("clip", "seq", None),
            P("clip", None, None),
            P("clip", None),
            P(),
            P(),
            P(),
            P(),
            P(),
            P(),
            P(),
            P(),
            P(),
            P(),
            P(),
            P(),
            P(),
            P(),
            P(),
            P(),
            P("clip", "seq", None),
        ),
        out_specs=(
            P("clip", "seq", None),
            P("clip", "seq", None),
            P("clip", None, None),
            P("clip"),
            P("clip"),
            P("clip", None),
            P("clip", None),
            P("clip", None),
            P("clip", None),
            P("clip"),
            P("clip"),
            P("clip", None),
            P("clip", None),
            P("clip", None),
            P("clip", None),
            P("clip"),
            P("clip"),
            P("clip", None),
            P("clip", None),
        ),
        check_vma=False,
    )
```

```python
import functools
import math

import jax
import jax.numpy as jnp
from jax import lax
from jax.experimental import pallas as pl
from jax.experimental.pallas import tpu as pltpu
from jax.sharding import PartitionSpec as P

D = 1024
HEADS = 16
HD = 64
TEXT = 64
CLIPS = 4


EPS = 1e-05
NEG = -1e30
SQRT_HALF = 0.7071067811865476
INV_ROOT_TWO_PI = 0.3989422804014327

bf = jnp.bfloat16
f32 = jnp.float32
T, W, H, B = 2048, 256, 4, 256
LOG2E = math.log2(math.e)
C2 = LOG2E / 8.0
NT = (((1,), (1,)), ((), ()))
NN = (((1,), (0,)), ((), ()))
TN = (((0,), (0,)), ((), ()))


def dg(a, b, d):
    return lax.dot_general(a, b, d, preferred_element_type=f32)


def lanemask(rows,h):
    l=lax.broadcasted_iota(jnp.int32,(rows,W),1)
    return (l//HD)==h
def add_blocks(out, ins, rows, cols):
    step = max(16, min(rows, 65536 // cols))

    def body(i, carry):
        r = pl.ds(pl.multiple_of(i * step, 16), step)
        total = ins[0][r, :].astype(f32)
        for one in ins[1:]:
            total = total + one[r, :].astype(f32)
        out[r, :] = total.astype(bf)
        return carry

    lax.fori_loop(0, rows // step, body, 0)


def each(count, fn):
    def body(i, x):
        fn(i)
        return x

    lax.fori_loop(0, count, body, 0)


def tile_of(i, size=256):
    return pl.ds(pl.multiple_of(i * size, size), size)


def unit_rows(v):
    center = v - jnp.mean(v, axis=-1, keepdims=True)
    scaled = lax.rsqrt(jnp.mean(center * center, axis=-1, keepdims=True) + EPS)
    return center * scaled, scaled


def norm_rows(src, gain, bias, dst, rows):
    def chunk(i):
        r = tile_of(i, 128)
        unit, _ = unit_rows(src[r, :])
        dst[r, :] = (unit * gain[...] + bias[...]).astype(bf)

    each(rows // 128, chunk)


def norm_back_rows(up, src, gain, add, dst, dst_low, rows):
    def chunk(i, sums):
        r = tile_of(i, 64)
        unit, scaled = unit_rows(src[r, :])
        u = up[r, :]
        along = u * gain[...]
        inner = (
            along
            - jnp.mean(along, axis=-1, keepdims=True)
            - unit * jnp.mean(along * unit, axis=-1, keepdims=True)
        )
        total = add[r, :].astype(f32) + inner * scaled
        dst[r, :] = total
        dst_low[r, :] = total.astype(bf)
        fold = lambda v: jnp.sum(v.reshape(8, 8, v.shape[1]), axis=0)
        return sums[0] + fold(u * unit), sums[1] + fold(u)

    zero = jnp.zeros((8, src.shape[1]), f32)
    a, b = lax.fori_loop(0, rows // 64, chunk, (zero, zero))
    return jnp.sum(a, axis=0, keepdims=True), jnp.sum(b, axis=0, keepdims=True)


def remote(src, dst, send, recv, **where):
    return pltpu.make_async_remote_copy(
        src_ref=src, dst_ref=dst, send_sem=send, recv_sem=recv, device_id=where,
        device_id_type=pl.DeviceIdType.MESH,
    )


def greet(env, halves):
    s, c, z, seqs = env["s"], env["c"], env["z"], env["seqs"]
    whom = [{"clip": 2 * z + 1 - c}, {"clip": beside(env)}]
    whom += [{"seq": lax.rem(s + k, seqs)} for k in range(1, seqs)]
    whom += [
        {"clip": 2 * (2 * lax.rem(env["zh"] + k, halves) + env["zl"]) + c} for k in range(1, halves)
    ]
    barrier = pltpu.get_barrier_semaphore()
    for one in whom:
        pl.semaphore_signal(barrier, inc=1, device_id=one, device_id_type=pl.DeviceIdType.MESH)
    pl.semaphore_wait(barrier, len(whom))


def greet_all(env, clips):
    s, seqs = env["s"], env["seqs"]
    b = 2 * env["z"] + env["c"]
    whom = [{"seq": lax.rem(s + k, seqs)} for k in range(1, seqs)]
    whom += [{"clip": lax.rem(b + k, clips)} for k in range(1, clips)]
    barrier = pltpu.get_barrier_semaphore()
    for one in whom:
        pl.semaphore_signal(barrier, inc=1, device_id=one, device_id_type=pl.DeviceIdType.MESH)
    pl.semaphore_wait(barrier, len(whom))


def place(seqs):
    b = lax.axis_index("clip")
    z = lax.div(b, 2)
    return dict(
        seqs=seqs, s=lax.axis_index("seq"), c=lax.rem(b, 2), z=z, zh=lax.div(z, 2), zl=lax.rem(z, 2)
    )


def beside(env):
    return 2 * (2 * env["zh"] + 1 - env["zl"]) + env["c"]


def kb_kernel(seqs, *refs):
    (
        att, x_ref, gb, ck, cv, owner, g2, b2, g3, b3,
        w_o, w_cq, w_co, w_up, w_dn, n1_hbm,
    ) = refs[:16]
    (x1, fo, vec, c_up, c_dn, c_o, c_cq, c_co, heads, n1_all, kq, vq) = refs[16:28]
    (
        ring, up_st, dn_st, up_rv, dn_rv, sq_rv, x2, n2, n3, n3t, cq, co, probs, u, ut, dh,
        acc, dn3, up_nr, up_fr, dn_sr, kv_low, kv_rv, ring_sem, st_send, st_recv, out_sem, n1_sem, head_sem, kv_sem,
        near_sem, far_sem, seq_sem,
    ) = refs[28:]
    env = place(seqs)
    s, c, z = env["s"], env["c"], env["z"]
    rows, d = x_ref.shape
    halves, rb = up_rv.shape[0], up_rv.shape[2]
    pairs, zl = 2 * halves, env["zl"]
    ppc, rbd = dn_st.shape[0], dn_st.shape[2]
    steps = w_up.shape[1] // d
    width = d // seqs
    texts = ck.shape[0]
    depth = ring.shape[0]

    items = [w_o, w_cq, w_co]
    for t in range(steps):
        items += [w_up.at[:, pl.ds(t * d, d)], w_dn.at[pl.ds(t * d, d), :]]
    items += [w_co, w_cq, w_o]

    def load(i):
        return pltpu.make_async_copy(items[i], ring.at[i % depth], ring_sem.at[i % depth])

    def take(i):
        load(i).wait()
        return ring.at[i % depth]

    def drop(i):
        if i + depth < len(items):
            load(i + depth).start()

    for i in range(depth):
        load(i).start()
    greet(env, halves)

    peers = [(k, lax.rem(s + k, seqs)) for k in range(1, seqs)]
    spots = pl.ds(pl.multiple_of(s * rows, rows), rows)
    by_x, by_y = s + 1 - 2 * lax.rem(s, 2), lax.rem(s + 2, 4)
    here = lambda who, part: n1_all.at[
        pl.ds(pl.multiple_of(who * rows + part * (rows // 2), rows // 2), rows // 2), :
    ]
    n1_out = [
        remote(n1_hbm, n1_all.at[spots, :], n1_sem.at[0, k], n1_sem.at[1, k], seq=to)
        for k, to in ((1, by_x), (2, by_y))
    ]
    n1_on = [
        remote(here(by_y, 0), here(by_y, 0), n1_sem.at[0, 3], n1_sem.at[1, 3], seq=by_x),
        remote(here(by_x, 1), here(by_x, 1), n1_sem.at[0, 4], n1_sem.at[1, 4], seq=by_y),
    ]
    n1_own = pltpu.make_async_copy(n1_hbm, n1_all.at[spots, :], n1_sem.at[0, 0])
    start(n1_out)
    n1_own.start()

    w = take(0)

    def f(t):
        x1[:, tile_of(t)] = x_ref[:, tile_of(t)].astype(f32) + dg(att[...], w[:, tile_of(t)], NN)

    each(d // 256, f)
    drop(0)
    norm_rows(x1, g2, b2, n2, rows)
    w = take(1)

    def f(t):
        cq[:, tile_of(t)] = dg(n2[...], w[:, tile_of(t)], NN).astype(bf)

    each(d // 256, f)
    drop(1)
    half = 256
    key_clip = lax.broadcasted_iota(jnp.int32, (half, texts), 1) // TEXT

    def masked(v, h):
        lane = lax.broadcasted_iota(jnp.int32, v.shape, 1)
        return jnp.where(lane // HD == h, v, jnp.zeros_like(v))

    def f(n):
        t, r = lax.div(n, rows // half), tile_of(lax.rem(n, rows // half), half)
        allowed = owner[r, :] == key_clip
        q, k, v = cq[r, tile_of(t)], ck[:, tile_of(t)], cv[:, tile_of(t)]
        total = jnp.zeros((half, 256), f32)
        for h in range(256 // HD):
            sc = jnp.where(allowed, dg(masked(q, h), k, NT), NEG)
            p = jnp.exp2((sc - jnp.max(sc, axis=-1, keepdims=True)) * C2)
            p = (p / jnp.sum(p, axis=-1, keepdims=True)).astype(bf)
            probs[t * (256 // HD) + h, r, :] = p
            total = total + dg(p, masked(v, h), NN)
        co[r, tile_of(t)] = total.astype(bf)

    each(d // 256 * (rows // half), f)
    w = take(2)

    def f(t):
        x2[:, tile_of(t)] = x1[:, tile_of(t)] + dg(co[...], w[:, tile_of(t)], NN)

    each(d // 256, f)
    drop(2)
    norm_rows(x2, g3, b3, n3, rows)

    def turn(src, dst):
        def f(t):
            dst[tile_of(t), :] = src[:, tile_of(t)].T

        each(d // 256, f)

    turn(n3, n3t)

    def swap(n, src, dst):
        return remote(src, dst, st_send.at[n], st_recv.at[n], clip=2 * z + 1 - c)

    def up_swap(t):
        return swap(2 * t, up_st.at[0, :, :, 1 - c], up_rv.at[:, :, :, pl.ds(t * d, d)])

    def dn_swap(t):
        return swap(2 * t + 1, dn_st.at[:, 1 - c], dn_rv.at[pl.ds(t * ppc, ppc)])

    def up_near(t):
        cols = pl.ds(t * d, d)
        return remote(
            up_rv.at[:, 1 - zl, :, cols], up_nr.at[:, :, cols], near_sem.at[0, t], near_sem.at[1, t],
            clip=beside(env),
        )

    def dn_seq(t):
        blocks = pl.ds(t * ppc, ppc)
        return [
            remote(
                dn_rv.at[blocks, :, pl.ds(pl.multiple_of(to * width, 128), width)], dn_sr.at[k - 1, blocks],
                seq_sem.at[0, t, k], seq_sem.at[1, t, k], seq=to,
            )
            for k, to in peers
        ]

    def up_out(t):
        cols = pl.ds(t * d, d)
        return pltpu.make_async_copy(up_fr.at[0, :, cols], c_up.at[:, cols], out_sem.at[2 * t])

    def up_far(t):
        cols = pl.ds(t * d, d)
        copies = []
        for k in range(1, halves):
            to = lax.rem(env["zh"] + k, halves)
            copies.append(
                remote(
                    up_nr.at[to, :, cols], up_fr.at[k - 1, :, cols], far_sem.at[0, t, k], far_sem.at[1, t, k],
                    clip=2 * (2 * to + zl) + c,
                )
            )
        return copies

    def dn_out(t):
        blocks = pl.ds(t * ppc, ppc)
        return pltpu.make_async_copy(dn_sr.at[0, blocks], c_dn.at[blocks], out_sem.at[2 * t + 1])

    def settle(t):
        cols = pl.ds(t * d, d)
        one = up_swap(t)
        one.wait_recv()
        for p in range(halves):
            for l in range(2):
                dst = up_rv.at[p, l, :, cols]
                add_blocks(dst, [dst, up_st.at[0, p, l, c]], rb, d)
        one.wait_send()
        up_near(t).start()
        one = dn_swap(t)
        one.wait_recv()
        for p in range(ppc):
            dst = dn_rv.at[t * ppc + p]
            add_blocks(dst, [dst, dn_st.at[p, c]], rbd, d)
        one.wait_send()
        start(dn_seq(t))

    mine = pl.ds(pl.multiple_of(s * width, 128), width)

    def settle_near(t):
        cols = pl.ds(t * d, d)
        one = up_near(t)
        one.wait_recv()
        for p in range(halves):
            dst = up_nr.at[p, :, cols]
            add_blocks(dst, [dst, up_rv.at[p, zl, :, cols]], rb, d)
        start(up_far(t))

    def settle_dn(t):
        arrive(dn_seq(t))
        for p in range(t * ppc, (t + 1) * ppc):
            add_blocks(
                dn_sr.at[0, p],
                [dn_rv.at[p, :, mine]] + [dn_sr.at[k - 1, p] for k, _ in peers],
                rbd,
                width,
            )
        dn_out(t).start()

    def settle_last(t):
        cols = pl.ds(t * d, d)
        arrive(up_far(t))
        others = [up_fr.at[k - 1, :, cols] for k in range(1, halves)]
        add_blocks(up_fr.at[0, :, cols], [up_nr.at[env["zh"], :, cols]] + others, rb, d)
        up_out(t).start()

    for t in range(steps):
        wu, wd = take(3 + 2 * t), take(4 + 2 * t)

        def f(i):
            h = dg(n3[...], wu[:, tile_of(i)], NN)
            du = dg(gb[...], wd[tile_of(i), :], NT)
            part = 0.5 * (1.0 + lax.erf(h * SQRT_HALF))
            slope = part + h * jnp.exp2(h * h * (-0.5 * LOG2E)) * INV_ROOT_TWO_PI
            dh[:, tile_of(i)] = (du * slope).astype(bf)
            act = (h * part).astype(bf)
            u[:, tile_of(i)] = act
            ut[tile_of(i), :] = act.T

        each(d // 256, f)
        if t > 0:
            settle(t - 1)
        if t > 2:
            settle_near(t - 3)

        def f(i, t=t):
            a = dg(u[...], wd[:, tile_of(i)], NN)
            b = dg(dh[...], wu[tile_of(i), :], NT)
            if t == 0:
                acc[:, tile_of(i)] = a
                dn3[:, tile_of(i)] = b
            else:
                acc[:, tile_of(i)] += a
                dn3[:, tile_of(i)] += b
            g = dg(n3t[...], dh[:, tile_of(i)], NN).astype(bf)
            up_st[0, :, :, :, :, tile_of(i)] = g.reshape(halves, 2, 2, rb, 256)
            g = dg(ut[...], gb[:, tile_of(i)], NN).astype(bf)
            dn_st[:, :, :, tile_of(i)] = g.reshape(ppc, 2, rbd, 256)

        each(d // 256, f)
        drop(3 + 2 * t)
        drop(4 + 2 * t)
        up_swap(t).start()
        dn_swap(t).start()

    def f(i):
        r = tile_of(i, 64)
        fo[r, :] = (x2[r, :] + acc[r, :]).astype(bf)

    each(rows // 64, f)
    base = 3 + 2 * steps
    settle(steps - 1)
    settle_near(steps - 3)
    arrive(n1_out)
    start(n1_on)
    low = u
    sums = norm_back_rows(dn3, x2, g3, gb, acc, low, rows)
    vec[2:3, :], vec[3:4, :] = sums
    w = take(base)
    dco = dh

    def f(t):
        dco[:, tile_of(t)] = dg(low[...], w[tile_of(t), :], NT).astype(bf)

    each(d // 256, f)
    drop(base)
    settle_near(steps - 2)

    def grad(n, slot, a, low):
        turn(a, n3t)

        def f(t):
            g = dg(n3t[...], low[:, tile_of(t)], NN).astype(bf)
            up_st[slot, :, :, :, :, tile_of(t)] = g.reshape(halves, 2, 2, rb, 256)

        each(d // 256, f)
        grad_swap(n, slot).start()

    def grad_swap(n, slot):
        return swap(2 * steps + n, up_st.at[slot, :, :, 1 - c], sq_rv.at[n])

    def grad_out(n):
        return pltpu.make_async_copy(sq_rv.at[n], (c_co, c_cq, c_o)[n], out_sem.at[2 * steps + n])

    def grad_settle(n, slot):
        one = grad_swap(n, slot)
        one.wait_recv()
        for p in range(halves):
            for l in range(2):
                add_blocks(sq_rv.at[n, p, l], [sq_rv.at[n, p, l], up_st.at[slot, p, l, c]], rb, d)
        one.wait_send()
        grad_out(n).start()

    grad(0, 0, co, low)
    dcq = n3

    def f(t):
        k, v = ck[:, tile_of(t)], cv[:, tile_of(t)]
        sum_k = jnp.zeros((texts, 256), f32)
        sum_v = jnp.zeros((texts, 256), f32)
        for n in range(rows // half):
            r = pl.ds(n * half, half)
            q, g = cq[r, tile_of(t)], dco[r, tile_of(t)]
            out = jnp.zeros((half, 256), f32)
            for h in range(256 // HD):
                p_low = probs[t * (256 // HD) + h, r, :]
                p = p_low.astype(f32)
                dp = dg(masked(g, h), v, NT)
                inner = jnp.sum(p * dp, axis=-1, keepdims=True)
                ds = (p * (dp - inner)).astype(bf)
                out = out + dg(ds, masked(k, h), NN)
                sum_k = sum_k + dg(ds, masked(q, h), TN)
                sum_v = sum_v + dg(p_low, masked(g, h), TN)
            dcq[r, tile_of(t)] = (out * 0.125).astype(bf)
        kv_low[0, :, tile_of(t)] = (sum_k * 0.125).astype(bf)
        kv_low[1, :, tile_of(t)] = sum_v.astype(bf)

    each(d // 256, f)
    kv_out = [
        remote(
            kv_low.at[:, :, pl.ds(pl.multiple_of(to * width, 128), width)], kv_rv.at[k - 1],
            kv_sem.at[0, k], kv_sem.at[1, k], seq=to,
        )
        for k, to in peers
    ]
    start(kv_out)
    settle_near(steps - 1)
    w = take(base + 1)
    dn2 = dn3

    def f(t):
        dn2[:, tile_of(t)] = dg(dcq[...], w[tile_of(t), :], NT)

    each(d // 256, f)
    drop(base + 1)
    sums = norm_back_rows(dn2, x1, g2, acc, x1, low, rows)
    vec[0:1, :], vec[1:2, :] = sums
    vec[4:8, :] = jnp.zeros((4, d), f32)
    w = take(base + 2)
    do = dh

    def f(t):
        do[:, tile_of(t)] = dg(low[...], w[tile_of(t), :], NT).astype(bf)

    each(d // 256, f)
    head_out = [
        remote(
            do.at[:, pl.ds(pl.multiple_of(to * width, 128), width)], heads.at[spots, :],
            head_sem.at[0, k], head_sem.at[1, k], seq=to,
        )
        for k, to in peers
    ]
    head_own = pltpu.make_async_copy(do.at[:, mine], heads.at[spots, :], head_sem.at[0, 0])
    start(head_out)
    head_own.start()
    grad_settle(0, 0)
    grad(1, 0, n2, dcq)
    for t in range(steps - 2):
        settle_dn(t)
        settle_last(t)
    grad_settle(1, 0)
    grad(2, 0, att, low)
    settle_dn(steps - 2)
    settle_last(steps - 2)
    grad_settle(2, 0)
    arrive(kv_out)
    for n, dst in enumerate((kq, vq)):
        total = kv_low[n, :, mine].astype(f32)
        for k in range(1, seqs):
            total = total + kv_rv[k - 1, n].astype(f32)
        dst[...] = total.astype(bf)
    settle_dn(steps - 1)
    settle_last(steps - 1)
    finish(kv_out)
    head_own.wait()
    n1_own.wait()
    for one in head_out + n1_on:
        one.wait()
    finish(n1_out)
    for t in range(steps):
        up_near(t).wait_send()
        finish(up_far(t))
        finish(dn_seq(t))
        up_out(t).wait()
        dn_out(t).wait()
    for n in range(3):
        grad_out(n).wait()


def kb(seqs, clips, att, x, gb, ck, cv, owner, g2, b2, g3, b3, w_o, w_cq, w_co, w_up, w_dn, n1):
    rows, d = x.shape
    pairs = clips // 2
    halves = pairs // 2
    rb, rbd = d // clips, w_dn.shape[0] // clips
    steps = w_up.shape[1] // d
    ppc = pairs // steps
    texts = ck.shape[0]
    width = d // seqs
    hbm = pl.BlockSpec(memory_space=pl.ANY)
    vmem = pl.BlockSpec(memory_space=pltpu.VMEM)
    low = lambda *shape: pltpu.VMEM(shape, bf)
    full = lambda *shape: pltpu.VMEM(shape, f32)
    s_low = lambda *shape: jax.ShapeDtypeStruct(shape, bf)
    dma = pltpu.SemaphoreType.DMA
    return pl.pallas_call(
        functools.partial(kb_kernel, seqs),
        out_shape=[
            jax.ShapeDtypeStruct((rows, d), f32),
            s_low(rows, d),
            jax.ShapeDtypeStruct((8, d), f32),
            s_low(rb, steps * d),
            s_low(pairs, rbd, width),
            s_low(halves, 2, rb, d),
            s_low(halves, 2, rb, d),
            s_low(halves, 2, rb, d),
            s_low(rows * seqs, width),
            s_low(rows * seqs, d),
            s_low(texts, width),
            s_low(texts, width),
        ],
        in_specs=[vmem] * 10 + [hbm] * 6,
        out_specs=[vmem] * 3 + [hbm] * 7 + [vmem] * 2,
        scratch_shapes=[
            low(4, d, d),
            low(1, halves, 2, 2, rb, d),
            low(ppc, 2, rbd, d),
            low(halves, 2, rb, steps * d),
            low(pairs, rbd, d),
            low(3, halves, 2, rb, d),
            full(rows, d),
            low(rows, d),
            low(rows, d),
            low(d, rows),
            low(rows, d),
            low(rows, d),
            low(d // HD, rows, texts),
            low(rows, d),
            low(d, rows),
            low(rows, d),
            full(rows, d),
            full(rows, d),
            low(halves, rb, steps * d),
            low(max(1, halves - 1), rb, steps * d),
            low(seqs - 1, pairs, rbd, width),
            low(2, texts, d),
            low(seqs - 1, 2, texts, width),
            dma((4,)),
            dma((2 * steps + 3,)),
            dma((2 * steps + 3,)),
            dma((2 * steps + 3,)),
            dma((2, 5)),
            dma((2, seqs)),
            dma((2, seqs)),
            dma((2, steps)),
            dma((2, steps, halves)),
            dma((2, steps, seqs)),
        ],
        compiler_params=pltpu.CompilerParams(
            collective_id=2, has_side_effects=True, vmem_limit_bytes=60 * 2**20
        ),
    )(
        att, x, gb, ck, cv, owner[:, None],
        *[v[None] for v in (g2, b2, g3, b3)],
        w_o, w_cq, w_co, w_up, w_dn, n1,
    )


def ka_kernel(seqs, *refs):
    x_ref, g1, b1, first, text, w_q, w_k, w_v, w_xk, w_xv = refs[:10]
    n1_out, o_out, lse_out, q_out, k_out, v_out, att, ck_out, cv_out = refs[10:19]
    (
        w_buf, wide, stage, held, vt, n1, o_ref, lse_ref, c_buf, w_sem, send, recv, push_send, push_recv, out_sem,
    ) = refs[19:]
    env = place(seqs)
    s = env["s"]
    rows, d = x_ref.shape
    pair = 2 * HD
    loads = [
        pltpu.make_async_copy(one, w_buf.at[n], w_sem.at[n]) for n, one in enumerate((w_q, w_k, w_v, w_xk, w_xv))
    ]
    start(loads)
    greet_seq(env)

    def f(i):
        r = tile_of(i, 64)
        wide[r, :] = x_ref[r, :].astype(f32)

    each(rows // 64, f)
    norm_rows(wide, g1, b1, n1, rows)
    outs = [pltpu.make_async_copy(n1, n1_out, out_sem.at[3])]
    start(outs)
    spots = pl.ds(pl.multiple_of(s * rows, rows), rows)
    peers = [(k, lax.rem(s + k, seqs)) for k in range(1, seqs)]

    def sends(g):
        return [
            remote(
                stage.at[:, :, pl.ds(pl.multiple_of(to * W + g * pair, 128), pair)],
                held.at[:, spots, pl.ds(g * pair, pair)],
                send.at[g, k], recv.at[g, k], seq=to,
            )
            for k, to in peers
        ]

    for one in loads[:3]:
        one.wait()
    first_sends = sends(0)
    for n, (k, to) in enumerate(peers):
        cols = pl.ds(pl.multiple_of(to * W, 128), W)
        for t in range(3):
            stage[t, :, cols] = dg(n1[...], w_buf[t, :, cols], NN).astype(bf)
        first_sends[n].start()
    cols = pl.ds(pl.multiple_of(s * W, 128), W)
    for t in range(3):
        held[t, spots, :] = dg(n1[...], w_buf[t, :, cols], NN).astype(bf)

    for n, one in enumerate((ck_out, cv_out)):
        loads[3 + n].wait()

        def f(t, n=n):
            c_buf[n, :, tile_of(t)] = dg(text[...], w_buf[3 + n, :, tile_of(t)], NN).astype(bf)

        each(d // 256, f)
        outs.append(pltpu.make_async_copy(c_buf.at[n], one, out_sem.at[4 + n]))
        outs[-1].start()

    lane = lax.broadcasted_iota(jnp.int32, (1, pair), 1) // HD
    kvi = lax.broadcasted_iota(jnp.int32, (rows, rows), 0)
    qi = lax.broadcasted_iota(jnp.int32, (rows, rows), 1)

    def qblock(g, i, masked):
        ln = pl.ds(g * pair, pair)
        r = tile_of(i, rows)
        q = held[0, r, ln]
        qm = [jnp.where(lane == h, q, jnp.zeros_like(q)) for h in range(2)]
        fst = first[:, r]

        def step(j, carry, diag):
            c = tile_of(j, rows)
            k = held[1, c, ln]
            out = []
            for h in range(2):
                m, l, acc = carry[h]
                sc = dg(k, qm[h], NT)
                if diag:
                    sc = jnp.where(kvi <= qi, sc, NEG)
                if masked:
                    sc = jnp.where(kvi + j * rows >= fst, sc, NEG)
                top = jnp.maximum(m, jnp.max(sc, axis=0, keepdims=True))
                p = jnp.exp2((sc - top) * C2)
                a = jnp.exp2((m - top) * C2)
                l = l * a + jnp.sum(p, axis=0, keepdims=True)
                acc = acc * a + dg(vt[h * HD : (h + 1) * HD, c], p.astype(bf), NN)
                out.append((top, l, acc))
            return tuple(out)

        carry = tuple(
            (jnp.full((1, rows), NEG, f32), jnp.zeros((1, rows), f32), jnp.zeros((HD, rows), f32))
            for _ in range(2)
        )
        carry = lax.fori_loop(0, i, lambda j, x: step(j, x, False), carry)
        carry = step(i, carry, True)
        ot = jnp.concatenate([acc / l for _, l, acc in carry], axis=0)
        o_ref[r, ln] = ot.T.astype(bf)
        for h in range(2):
            lse_ref[2 * g + h : 2 * g + h + 1, r] = carry[h][0] * C2 + jnp.log2(carry[h][1])

    def push(g, owner, away):
        src = o_ref.at[tile_of(owner, rows), pl.ds(g * pair, pair)]
        dst = att.at[:, pl.ds(pl.multiple_of(s * W + g * pair, 128), pair)]
        k = lax.rem(owner - s + seqs, seqs)
        if away:
            return remote(src, dst, push_send.at[g, owner], push_recv.at[g, k], seq=owner)
        return pltpu.make_async_copy(src, dst, push_send.at[g, owner])

    def send_rows(g, owner):
        @pl.when(s != owner)
        def _():
            push(g, owner, True).start()

        @pl.when(s == owner)
        def _():
            push(g, owner, False).start()

    lse_ref[4:8, :] = jnp.zeros((4, lse_ref.shape[1]), f32)
    for g in range(2):
        arrive(sends(g))
        if g == 0:
            start(sends(1))
        else:
            heads = [
                pltpu.make_async_copy(held.at[n], one, out_sem.at[n])
                for n, one in enumerate((q_out, k_out, v_out))
            ]
            start(heads)
            outs += heads

        def f(i, g=g):
            r = tile_of(i, rows)
            vt[:, r] = held[2, r, pl.ds(g * pair, pair)].T

        each(seqs, f)

        def f(i, g=g):
            qblock(g, i, False)
            send_rows(g, i)

        plain = TAIL // rows
        each(plain, f)
        for i in range(plain, seqs):
            qblock(g, i, True)
            send_rows(g, i)
    last = [pltpu.make_async_copy(o_ref, o_out, out_sem.at[6]), pltpu.make_async_copy(lse_ref, lse_out, out_sem.at[7])]
    start(last)
    for one in outs + last:
        one.wait()
    for g in range(2):
        finish(sends(g))
        for owner in range(seqs):
            @pl.when(s != owner)
            def _():
                push(g, owner, True).wait_send()

            @pl.when(s == owner)
            def _():
                push(g, owner, False).wait()
        for k in range(1, seqs):
            back = lax.rem(s - k + seqs, seqs)
            dst = att.at[:, pl.ds(pl.multiple_of(back * W + g * pair, 128), pair)]
            pltpu.make_async_copy(dst, dst, push_recv.at[g, k]).wait()


def greet_seq(env):
    s, seqs = env["s"], env["seqs"]
    barrier = pltpu.get_barrier_semaphore()
    for k in range(1, seqs):
        pl.semaphore_signal(
            barrier, inc=1, device_id={"seq": lax.rem(s + k, seqs)}, device_id_type=pl.DeviceIdType.MESH
        )
    pl.semaphore_wait(barrier, seqs - 1)


def ka(seqs, x, g1, b1, first, text, weights):
    rows, d = x.shape
    hbm = pl.BlockSpec(memory_space=pl.ANY)
    vmem = pl.BlockSpec(memory_space=pltpu.VMEM)
    dma = pltpu.SemaphoreType.DMA
    s_low = lambda *shape: jax.ShapeDtypeStruct(shape, bf)
    total = rows * seqs
    return pl.pallas_call(
        functools.partial(ka_kernel, seqs),
        out_shape=[
            s_low(rows, d),
            s_low(total, W),
            jax.ShapeDtypeStruct((8, total), f32),
            s_low(total, W),
            s_low(total, W),
            s_low(total, W),
            s_low(rows, d),
            s_low(text.shape[0], d),
            s_low(text.shape[0], d),
        ],
        in_specs=[vmem] * 5 + [hbm] * 5,
        out_specs=[hbm] * 9,
        scratch_shapes=[
            pltpu.VMEM((5, d, d), bf),
            pltpu.VMEM((rows, d), f32),
            pltpu.VMEM((3, rows, d), bf),
            pltpu.VMEM((3, total, W), bf),
            pltpu.VMEM((2 * HD, total), bf),
            pltpu.VMEM((rows, d), bf),
            pltpu.VMEM((total, W), bf),
            pltpu.VMEM((8, total), f32),
            pltpu.VMEM((2, text.shape[0], d), bf),
            dma((5,)),
            dma((2, seqs)),
            dma((2, seqs)),
            dma((2, seqs)),
            dma((2, seqs)),
            dma((8,)),
        ],
        compiler_params=pltpu.CompilerParams(
            collective_id=3, has_side_effects=True, vmem_limit_bytes=60 * 2**20
        ),
    )(x, g1[None], b1[None], first, text, *weights)


class Job:
    def __init__(self, steps, part, bufs, sems, out, env, halves):
        self.steps, self.part, self.out, self.env, self.halves = steps, part, out, env, halves
        self.r0, self.rm, self.rn, self.rf, self.rs = bufs
        self.sems = sems
        self.rb, self.n = part.shape[-2:]
        self.first = "split" in steps
        self.q = self.n // env["seqs"] if "seq" in steps or self.first else self.n
        self.done = self.rs if "seq" in steps else self.rf
        self.bare = steps == ("seq",)
        self.cored = self.r0 if "cores" in steps else (self.rs.at[0] if self.first else part)
        self.w = self.q if self.first else self.n

    def copy(self, stage, k, src, dst, **where):
        return remote(src, dst, self.sems.at[0, stage, k], self.sems.at[1, stage, k], **where)

    def cores(self):
        e = self.env
        return [
            self.copy(0, 0, self.part.at[:, :, 1 - e["c"]], self.r0, clip=2 * e["z"] + 1 - e["c"])
        ]

    def sum_cores(self):
        for p in range(self.halves):
            for l in range(2):
                one = self.r0.at[p, l]
                add_blocks(one, [one, self.part.at[p, l, self.env["c"]]], self.rb, self.n)

    def split(self):
        e, copies = self.env, []
        for k in range(1, e["seqs"]):
            to = lax.rem(e["s"] + k, e["seqs"])
            copies.append(
                self.copy(3, k - 1, self.part.at[:, :, :, self.columns(to)], self.rs.at[k - 1], seq=to)
            )
        return copies

    def sum_split(self):
        self.load().wait()
        for p in range(self.halves):
            for l in range(2):
                others = [self.rs.at[k, p, l] for k in range(self.env["seqs"] - 1)]
                add_blocks(self.rs.at[0, p, l], [self.rm.at[p, l]] + others, self.rb, self.q)

    def load(self):
        if self.first or self.bare:
            at = (slice(None),) * (len(self.part.shape) - 1) + (self.columns(self.env["s"]),)
            src = self.part.at[at]
            return pltpu.make_async_copy(src, self.rm, self.sems.at[0, 5, 0])
        src = self.part.at[:, self.env["zl"]] if "near" in self.steps else self.part.at[self.env["zh"]]
        return pltpu.make_async_copy(src, self.rm, self.sems.at[0, 5, 0])

    def near(self):
        return [self.copy(1, 0, self.cored.at[:, 1 - self.env["zl"]], self.rn, clip=beside(self.env))]

    def sum_near(self):
        loaded = "cores" not in self.steps and not self.first
        if loaded:
            self.load().wait()
        for p in range(self.halves):
            mine = self.rm.at[p] if loaded else self.cored.at[p, self.env["zl"]]
            add_blocks(self.rn.at[p], [self.rn.at[p], mine], self.rb, self.w)

    def far(self):
        e, copies = self.env, []
        src = self.rn if "near" in self.steps else self.part
        for k in range(1, self.halves):
            to = lax.rem(e["zh"] + k, self.halves)
            copies.append(
                self.copy(2, k - 1, src.at[to], self.rf.at[k - 1], clip=2 * (2 * to + e["zl"]) + e["c"])
            )
        return copies

    def sum_far(self):
        if "near" in self.steps:
            mine = self.rn.at[self.env["zh"]]
        else:
            self.load().wait()
            mine = self.rm
        add_blocks(self.rf.at[0], [mine] + [self.rf.at[k] for k in range(self.halves - 1)], self.rb, self.w)

    def columns(self, s):
        return pl.ds(pl.multiple_of(s * self.q, 128), self.q)

    def seq(self):
        e, copies = self.env, []
        for k in range(1, e["seqs"]):
            to = lax.rem(e["s"] + k, e["seqs"])
            src = self.part.at[:, self.columns(to)] if self.bare else self.rf.at[0, :, self.columns(to)]
            copies.append(self.copy(3, k - 1, src, self.rs.at[k - 1], seq=to))
        return copies

    def sum_seq(self):
        if self.bare:
            self.load().wait()
            mine = self.rm
        else:
            mine = self.rf.at[0, :, self.columns(self.env["s"])]
        others = [self.rs.at[k] for k in range(self.env["seqs"] - 1)]
        add_blocks(self.rs.at[0], [mine] + others, self.rb, self.q)

    def gather(self):
        e, copies = self.env, []
        for k in range(1, e["seqs"]):
            to = lax.rem(e["s"] + k, e["seqs"])
            copies.append(
                self.copy(4, k - 1, self.done.at[0], self.out.at[:, self.columns(e["s"])], seq=to)
            )
        return copies

    def keep(self):
        return pltpu.make_async_copy(
            self.done.at[0], self.out.at[:, self.columns(self.env["s"])], self.sems.at[1, 5, 0]
        )

    def spread(self):
        start(self.gather())
        self.keep().start()

    def close(self):
        for name in self.steps:
            finish(getattr(self, name)())
        finish(self.gather())
        self.keep().wait()
        arrive(self.gather())


def start(copies):
    for one in copies:
        one.start()


def arrive(copies):
    for one in copies:
        one.wait_recv()


def finish(copies):
    for one in copies:
        one.wait_send()


def job_bufs(steps, shape, seqs, halves):
    rb, n = shape[-2:]
    low = lambda use, *dims: pltpu.VMEM(dims if use else (16, 128), bf)
    cores, near, split = ("cores" in steps), ("near" in steps), ("split" in steps)
    q = n // seqs
    w = q if split else n
    mine = (halves, 2, rb, q) if split else ((halves, rb, n) if near else (rb, q))
    return [
        low(cores, halves, 2, rb, n),
        low(not cores, *mine),
        low(near, halves, rb, w),
        low("far" in steps, max(1, halves - 1), rb, w),
        pltpu.VMEM((seqs - 1, halves, 2, rb, q), bf) if split else low("seq" in steps, seqs - 1, rb, q),
    ]


LAST = pl.DeviceIdType.MESH


def kc_kernel(seqs, halves, *refs):
    (q_ref, k_ref, v_ref, o_ref, g_ref, lse_ref, first_ref) = refs[:7]
    (kq, vq, text, x_ref, dx1, g1, vec_in, n1_hbm, w_q, w_k, w_v, *parts) = refs[7:23]
    (frames_grad, vec, k_all, v_all, *outs) = refs[23:37]
    dq_s, dk_s, dv_s, dka, dva, n1_buf, wacc, wsum, wparts, dqkv, w_buf, dn1, vec_rv, low_buf, *rest = refs[37:]
    sems, push_send, push_recv, local_sem, kv_sem, vec_sem = rest[-6:]
    bufs = rest[:-6]
    env = place(seqs)
    s, c, z = env["s"], env["c"], env["z"]
    frames = T // seqs
    d = n1_hbm.shape[1]
    greet_all(env, 4 * halves)

    jobs = []
    for t, steps in enumerate(STEPS):
        src = parts[t] if t < 5 else wparts.at[t - 5]
        jobs.append(Job(steps, src, bufs[5 * t : 5 * t + 5], sems.at[t], outs[t], env, halves))
    up, down, go, gcq, gco, gxk, gxv, gq, gk, gv = jobs
    start(up.seq())
    start(down.near())
    start(gco.near())
    for one in (up, down, go, gcq, gco):
        one.load().start()
    width = kq.shape[1]
    spot = pl.ds(pl.multiple_of(s * width, 128), width)
    kv_out, kv_own = [], []
    for n, (src, dst) in enumerate(((kq, k_all), (vq, v_all))):
        for k in range(1, seqs):
            kv_out.append(
                remote(src, dst.at[:, spot], kv_sem.at[0, n, k], kv_sem.at[1, n, k], seq=lax.rem(s + k, seqs))
            )
        kv_own.append(pltpu.make_async_copy(src, dst.at[:, spot], kv_sem.at[0, n, 0]))
    start(kv_out)
    start(kv_own)
    loads = [pltpu.make_async_copy(n1_hbm, n1_buf, local_sem.at[0])]
    for n, one in enumerate((w_q, w_k, w_v)):
        loads.append(pltpu.make_async_copy(one, w_buf.at[n], local_sem.at[1 + n]))
    start(loads)

    def place_product(n, rb):
        wparts[n] = wacc[...].astype(bf).reshape(halves, 2, 2, rb, W)

    for n, src in enumerate((kq, vq)):
        wacc[...] = dg(text[...], src[...], TN)
        place_product(n, gxk.rb)
        start((gxk, gxv)[n].cores())

    dka[...] = jnp.zeros_like(dka)
    dva[...] = jnp.zeros_like(dva)

    lane = lax.broadcasted_iota(jnp.int32, (1, W), 1) // HD
    kvi = lax.broadcasted_iota(jnp.int32, (frames, frames), 0)
    qi = lax.broadcasted_iota(jnp.int32, (frames, frames), 1)

    def qblock(i, masked):
        r = pl.ds(i * frames, frames)
        q = q_ref[r, :]
        g = g_ref[r, :]
        both = g.astype(f32) * o_ref[r, :].astype(f32)
        hm = (
            lax.broadcasted_iota(jnp.int32, (8, W), 1) // HD == lax.broadcasted_iota(jnp.int32, (8, W), 0)
        ).astype(f32)
        delta = lax.dot_general(hm, both, NT, precision=lax.Precision.HIGHEST, preferred_element_type=f32)
        lse = lse_ref[:, r]
        fst = first_ref[:, r]
        zero = jnp.zeros_like(q)
        qm = [jnp.where(lane == h, q, zero) for h in range(H)]
        gm = [jnp.where(lane == h, g, zero) for h in range(H)]

        def tile(j, dq, diag):
            at = tile_of(j, frames)
            k = k_ref[at, :]
            v = v_ref[at, :]
            dv = jnp.zeros((frames, W), f32)
            dk = jnp.zeros((frames, W), f32)
            for h in range(H):
                p = jnp.exp2(dg(k, qm[h], NT) * C2 - lse[h : h + 1])
                if diag:
                    p = jnp.where(kvi <= qi, p, 0.0)
                if masked:
                    p = jnp.where(kvi + j * frames >= fst, p, 0.0)
                dp = dg(v, gm[h], NT)
                ds = (p * (dp - delta[h : h + 1])).astype(bf)
                dv = dv + dg(p.astype(bf), gm[h], NN)
                dk = dk + dg(ds, qm[h], NN)
                dq = dq + dg(ds, jnp.where(lane == h, k, jnp.zeros_like(k)), TN)
            dva[at, :] += dv
            dka[at, :] += dk
            return dq

        dq = jnp.zeros((frames, W), f32)
        dq = lax.fori_loop(0, i, lambda j, x: tile(j, x, False), dq)
        dq = tile(i, dq, True)
        dq_s[r, :] = (dq * 0.125).astype(bf)
        dk_s[r, :] = (dka[r, :] * 0.125).astype(bf)
        dv_s[r, :] = dva[r, :].astype(bf)

    lanes = pl.ds(pl.multiple_of(s * W, 128), W)
    moved = [(src, dqkv.at[n]) for n, src in enumerate((dq_s, dk_s, dv_s))]

    def pushes(owner):
        k = lax.rem(owner - s + seqs, seqs)
        rows = pl.ds(owner * frames, frames)
        return [
            pltpu.make_async_remote_copy(
                src_ref=src.at[rows, :],
                dst_ref=dst.at[:, lanes],
                send_sem=push_send.at[n, owner],
                recv_sem=push_recv.at[n, k],
                device_id={"seq": owner},
                device_id_type=LAST,
            )
            for n, (src, dst) in enumerate(moved)
        ]

    def keeps(owner):
        rows = pl.ds(owner * frames, frames)
        return [
            pltpu.make_async_copy(src.at[rows, :], dst.at[:, lanes], push_send.at[n, owner])
            for n, (src, dst) in enumerate(moved)
        ]

    for owner in reversed(range(seqs)):
        qblock(owner, (owner + 1) * frames > TAIL)

        @pl.when(s != owner)
        def _():
            start(pushes(owner))

        @pl.when(s == owner)
        def _():
            start(keeps(owner))

        if owner == seqs - 1:
            for one in (gcq, go):
                start(one.near())
            for one in (gxk, gxv):
                arrive(one.cores())
                one.sum_cores()
                start(one.near())
            arrive(up.seq())
            up.sum_seq()
            up.spread()
        if owner == seqs - 2:
            for one in (down, gco):
                arrive(one.near())
                one.sum_near()
                start(one.far())

    loads[0].wait()
    for one in (gxk, gxv, gcq, go):
        arrive(one.near())
        one.sum_near()
        start(one.far())

    def product(r, x):
        rows = tile_of(r, 512)
        left = n1_buf[rows, :]
        for n, src in enumerate((dq_s, dk_s, dv_s)):
            cols = pl.ds(n * W, W)
            add = dg(left, src[rows, :], TN)
            wsum[:, cols] = jnp.where(r == 0, add, wsum[:, cols] + add)
        return x

    lax.fori_loop(0, T // 512, product, 0)
    for n, one in enumerate((gq, gk, gv)):
        wparts[2 + n] = wsum[:, n * W : (n + 1) * W].astype(bf).reshape(halves, 2, 2, gq.rb, W)
        start(one.cores())
    arrive(down.far())
    down.sum_far()
    down.spread()
    for one in (gq, gk, gv):
        arrive(one.cores())
        one.sum_cores()
        start(one.near())
    arrive(gco.far())
    gco.sum_far()
    start(gco.seq())
    for one in (gxk, gxv):
        arrive(one.far())
        one.sum_far()
        one.spread()
    for one in (gcq, go):
        arrive(one.far())
        one.sum_far()
        start(one.seq())
    for one in (gq, gk, gv):
        arrive(one.near())
        one.sum_near()
        start(one.far())

    for k in range(1, seqs):
        for n in range(3):
            dst = dqkv.at[n, :, pl.ds(pl.multiple_of(lax.rem(s - k + seqs, seqs) * W, 128), W)]
            pltpu.make_async_copy(dst, dst, push_recv.at[n, k]).wait()
    for owner in range(seqs):
        @pl.when(s != owner)
        def _():
            finish(pushes(owner))

        @pl.when(s == owner)
        def _():
            for one in keeps(owner):
                one.wait()
    for n in range(3):
        loads[1 + n].wait()

        def f(t, n=n):
            add = dg(dqkv[n], w_buf[n, tile_of(t), :], NT)
            if n == 0:
                dn1[:, tile_of(t)] = add
            else:
                dn1[:, tile_of(t)] += add

        each(d // 256, f)

    def f(i):
        r = tile_of(i, 64)
        wide_x[r, :] = x_ref[r, :].astype(f32)

    wide_x = frames_grad
    each(frames // 64, f)
    vec[...] = vec_in[...]
    sums = norm_back_rows(dn1, wide_x, g1, dx1, frames_grad, low_buf, frames)
    vec[4:5, :], vec[5:6, :] = sums
    clips = 4 * halves
    b = 2 * z + c
    vec_rv[b] = vec[...]
    around = [
        remote(vec, vec_rv.at[b], vec_sem.at[0, k], vec_sem.at[1, k], clip=lax.rem(b + k, clips))
        for k in range(1, clips)
    ]
    start(around)
    for one in (gco, gcq, go):
        arrive(one.seq())
        one.sum_seq()
        one.spread()
    for one in (gq, gk, gv):
        arrive(one.far())
        one.sum_far()
        one.spread()
    arrive(around)
    finish(around)
    total = vec_rv[0]
    for k in range(1, clips):
        total = total + vec_rv[k]
    vec[...] = total
    vec_rv[clips + s] = total
    along = [
        remote(
            vec, vec_rv.at[clips + s], vec_sem.at[0, clips + k], vec_sem.at[1, clips + k],
            seq=lax.rem(s + k, seqs),
        )
        for k in range(1, seqs)
    ]
    start(along)
    arrive(along)
    finish(along)
    total = vec_rv[clips]
    for k in range(1, seqs):
        total = total + vec_rv[clips + k]
    vec[...] = total

    for one in kv_out + kv_own:
        one.wait()
    for one in jobs:
        one.close()


OWN = ("cores", "near", "far")
STEPS = (("seq",), ("near", "far")) + (("near", "far", "seq"),) * 3 + (OWN,) * 5
TAIL = 1536


def last_kernel(count, *refs):
    mats, (k_low, v_low, w_k, w_v, fo, fg) = refs[:count], refs[count : count + 6]
    outs, (text_out, fo_out, fg_out) = refs[count + 6 : 2 * count + 6], refs[2 * count + 6 : 2 * count + 9]
    rest = refs[2 * count + 9 :]
    low, full = rest[:count], rest[count : 2 * count]
    kv, w, text_grad, fo_buf, fg_buf, load_sem, save_sem, move_sem = rest[2 * count :]
    moves = [pltpu.make_async_copy(fo, fo_buf, move_sem.at[0]), pltpu.make_async_copy(fg, fg_buf, move_sem.at[1])]
    loads = [pltpu.make_async_copy(a, b, load_sem.at[n]) for n, (a, b) in enumerate(zip(mats, low))]
    for n, (src, dst) in enumerate(((k_low, kv.at[0]), (v_low, kv.at[1]), (w_k, w.at[0]), (w_v, w.at[1]))):
        loads.append(pltpu.make_async_copy(src, dst, load_sem.at[count + n]))
    saves = [pltpu.make_async_copy(a, b, save_sem.at[n]) for n, (a, b) in enumerate(zip(full, outs))]
    start(moves)
    start(loads)
    for one in moves:
        one.wait()
    moves = [pltpu.make_async_copy(fo_buf, fo_out, move_sem.at[0]), pltpu.make_async_copy(fg_buf, fg_out, move_sem.at[1])]
    start(moves)
    for n in range(count):
        loads[n].wait()
        rows, cols = low[n].shape
        step = max(16, min(rows, 65536 // cols))

        def f(i, n=n, step=step):
            r = tile_of(i, step)
            full[n][r, :] = low[n][r, :].astype(f32)

        each(rows // step, f)
        saves[n].start()
    for n in range(4):
        loads[count + n].wait()

    def f(t):
        rows = tile_of(t)
        text_grad[:, rows] = dg(kv[0], w[0, rows, :], NT) + dg(kv[1], w[1, rows, :], NT)

    each(w.shape[1] // 256, f)
    saves.append(pltpu.make_async_copy(text_grad, text_out, save_sem.at[count]))
    saves[-1].start()
    for one in saves + moves:
        one.wait()


def last(mats, k_low, v_low, w_k, w_v, fo, fg):
    hbm = pl.BlockSpec(memory_space=pl.ANY)
    count = len(mats)
    dma = pltpu.SemaphoreType.DMA
    shape = jax.ShapeDtypeStruct
    return pl.pallas_call(
        functools.partial(last_kernel, count),
        out_shape=[shape(one.shape, f32) for one in mats]
        + [shape(k_low.shape, f32), shape(fo.shape, bf), shape(fg.shape, f32)],
        in_specs=[hbm] * (count + 6),
        out_specs=[hbm] * (count + 3),
        scratch_shapes=[pltpu.VMEM(one.shape, bf) for one in mats]
        + [pltpu.VMEM(one.shape, f32) for one in mats]
        + [
            pltpu.VMEM((2,) + k_low.shape, bf),
            pltpu.VMEM((2,) + w_k.shape, bf),
            pltpu.VMEM(k_low.shape, f32),
            pltpu.VMEM(fo.shape, bf),
            pltpu.VMEM(fg.shape, f32),
            dma((count + 4,)),
            dma((count + 1,)),
            dma((2,)),
        ],
        compiler_params=pltpu.CompilerParams(vmem_limit_bytes=60 * 2**20),
    )(*mats, k_low, v_low, w_k, w_v, fo, fg)


def kc(seqs, clips, heads, lse, first, kq, vq, text, x, dx1, g1, vec, n1_all, weights, parts):
    halves = clips // 4
    rows, d = x.shape
    rb = d // clips
    shapes = [p.shape for p in parts] + [(halves, 2, 2, rb, W)] * 5
    bufs = []
    for steps, shape in zip(STEPS, shapes):
        bufs += job_bufs(steps, shape, seqs, halves)
    outs = [
        jax.ShapeDtypeStruct((rows, d), f32),
        jax.ShapeDtypeStruct((8, d), f32),
        jax.ShapeDtypeStruct((text.shape[0], d), bf),
        jax.ShapeDtypeStruct((text.shape[0], d), bf),
    ]
    for steps, shape in zip(STEPS, shapes):
        wide = 1 if "seq" in steps or "split" in steps else seqs
        outs.append(jax.ShapeDtypeStruct((shape[-2], shape[-1] * wide), bf))
    hbm = pl.BlockSpec(memory_space=pl.ANY)
    vmem = pl.BlockSpec(memory_space=pltpu.VMEM)
    most = max(seqs, halves)
    dma = pltpu.SemaphoreType.DMA
    return pl.pallas_call(
        functools.partial(kc_kernel, seqs, halves),
        out_shape=outs,
        in_specs=[vmem] * 14 + [hbm] * 9,
        out_specs=[vmem] * 2 + [hbm] * 12,
        scratch_shapes=[pltpu.VMEM((T, W), bf)] * 3
        + [pltpu.VMEM((T, W), f32)] * 2
        + [
            pltpu.VMEM((T, d), bf),
            pltpu.VMEM((d, W), f32),
            pltpu.VMEM((d, 3 * W), f32),
            pltpu.VMEM((5, halves, 2, 2, rb, W), bf),
            pltpu.VMEM((3, rows, d), bf),
            pltpu.VMEM((3, d, d), bf),
            pltpu.VMEM((rows, d), f32),
            pltpu.VMEM((4 * halves + seqs, 8, d), f32),
            pltpu.VMEM((rows, d), bf),
        ]
        + bufs
        + [
            dma((10, 2, 6, most)),
            dma((3, seqs)),
            dma((3, seqs)),
            dma((4,)),
            dma((2, 2, seqs)),
            dma((2, 4 * halves + seqs)),
        ],
        compiler_params=pltpu.CompilerParams(
            collective_id=1, has_side_effects=True, vmem_limit_bytes=60 * 2**20
        ),
    )(*heads, lse, first, kq, vq, text, x, dx1, g1[None], vec, n1_all, *weights, *parts)


def matmul(left, right):
    return jnp.dot(left, right, preferred_element_type=jnp.float32)


def left_times(left, right):
    return lax.dot_general(
        left, right, (((0,), (0,)), ((), ())), preferred_element_type=jnp.float32
    )


def right_times(left, right):
    return lax.dot_general(
        left, right, (((1,), (1,)), ((), ())), preferred_element_type=jnp.float32
    )


def norm_forward(values, gain, bias):
    center = values - jnp.mean(values, axis=-1, keepdims=True)
    scaled = lax.rsqrt(jnp.mean(center * center, axis=-1, keepdims=True) + EPS)
    unit = center * scaled
    return (unit * gain + bias, unit, scaled)


def norm_backward(upstream, unit, scaled, gain):
    along = upstream * gain
    inner = (
        along
        - jnp.mean(along, axis=-1, keepdims=True)
        - unit * jnp.mean(along * unit, axis=-1, keepdims=True)
    )
    return (inner * scaled, jnp.sum(upstream * unit, axis=0), jnp.sum(upstream, axis=0))


def gelu_slope(values):
    return (
        0.5 * (1.0 + lax.erf(values * SQRT_HALF))
        + values * jnp.exp(-0.5 * values * values) * INV_ROOT_TWO_PI
    )


def softmax_rows(scores):
    top = jnp.max(scores, axis=-1, keepdims=True)
    expo = jnp.exp(scores - top)
    total = jnp.sum(expo, axis=-1, keepdims=True)
    return (expo / total, top[..., 0] + jnp.log(total[..., 0]))


def shards(
    frames_in,
    text_states,
    clip_lengths,
    self_gain,
    self_bias,
    query_weight,
    key_weight,
    value_weight,
    output_weight,
    cross_gain,
    cross_bias,
    cross_query,
    cross_key,
    cross_value,
    cross_output,
    feed_gain,
    feed_bias,
    feed_upward,
    feed_downward,
    grad_out,
):
    count = lax.axis_size("seq")
    place = lax.axis_index("seq")
    local = frames_in.shape[1]
    total_frames = local * count
    block = min(512, total_frames)
    blocks = total_frames // block
    scale = HD ** (-0.5)
    lengths = clip_lengths[0]
    slot = jnp.arange(CLIPS, dtype=jnp.int32)
    ends = jnp.sum(jnp.where(slot[None, :] <= slot[:, None], lengths[None, :], 0), axis=1)
    begins = ends - lengths
    slots = jnp.arange(CLIPS, dtype=jnp.int32)
    positions = jnp.arange(total_frames, dtype=jnp.int32)
    owner_all = jnp.sum((ends[None, :] <= positions[:, None]).astype(jnp.int32), axis=1)
    first_all = jnp.sum(jnp.where(owner_all[:, None] == slots[None, :], begins[None, :], 0), axis=1)
    owner_mine = lax.dynamic_slice_in_dim(owner_all, place * local, local, 0)
    frames = frames_in[0].astype(jnp.float32)
    text = text_states[0]
    text_rows = text.shape[0]
    weights = (query_weight, key_weight, value_weight)
    normed_low, attended, log_totals, query_heads, key_heads, value_heads, attended_frames, cross_k, cross_v = ka(
        count, frames_in[0], self_gain, self_bias, first_all[None], text, weights + (cross_key, cross_value)
    )
    clips = lax.axis_size("clip")
    dx1, output, vec, c_up, c_dn, c_o, c_cq, c_co, grad_heads, normed_all, key_own, value_own = kb(
        count,
        clips,
        attended_frames,
        frames_in[0],
        grad_out[0],
        cross_k,
        cross_v,
        owner_mine,
        cross_gain,
        cross_bias,
        feed_gain,
        feed_bias,
        output_weight,
        cross_query,
        cross_output,
        feed_upward,
        feed_downward,
        normed_low,
    )
    frames_grad, vec, key_low, value_low, *mats = kc(
        count,
        clips,
        (query_heads, key_heads, value_heads, attended, grad_heads),
        log_totals,
        first_all[None],
        key_own,
        value_own,
        text,
        frames_in[0],
        dx1,
        self_gain,
        vec,
        normed_all,
        weights,
        (c_up, c_dn.reshape((-1, 2) + c_dn.shape[1:]), c_o, c_cq, c_co),
    )
    *mats, text_grad, output, frames_grad = last(
        mats, key_low, value_low, cross_key, cross_value, output, frames_grad
    )
    w_up, w_dn, w_o, w_cq, w_co, w_xk, w_xv, w_q, w_k, w_v = mats
    width_out = D // clips
    vec = lax.dynamic_slice_in_dim(vec, lax.axis_index("clip") * width_out, width_out, 1)
    return (
        output[None],
        frames_grad[None],
        text_grad[None],
        vec[4],
        vec[5],
        w_q,
        w_k,
        w_v,
        w_o,
        vec[0],
        vec[1],
        w_cq,
        w_xk,
        w_xv,
        w_co,
        vec[2],
        vec[3],
        w_up,
        w_dn,
    )


def solution(mesh):
    return jax.shard_map(
        shards,
        mesh=mesh,
        in_specs=(
            P("clip", "seq", None),
            P("clip", None, None),
            P("clip", None),
            P(),
            P(),
            P(),
            P(),
            P(),
            P(),
            P(),
            P(),
            P(),
            P(),
            P(),
            P(),
            P(),
            P(),
            P(),
            P(),
            P("clip", "seq", None),
        ),
        out_specs=(
            P("clip", "seq", None),
            P("clip", "seq", None),
            P("clip", None, None),
            P("clip"),
            P("clip"),
            P("clip", None),
            P("clip", None),
            P("clip", None),
            P("clip", None),
            P("clip"),
            P("clip"),
            P("clip", None),
            P("clip", None),
            P("clip", None),
            P("clip", None),
            P("clip"),
            P("clip"),
            P("clip", None),
            P("clip", None),
        ),
        check_vma=False,
    )
```

```python
import functools
import math

import jax
import jax.numpy as jnp
from jax import lax
from jax.experimental import pallas as pl
from jax.experimental.pallas import tpu as pltpu
from jax.sharding import PartitionSpec as P

D = 1024
HEADS = 16
HD = 64
TEXT = 64
CLIPS = 4


EPS = 1e-05
NEG = -1e30
SQRT_HALF = 0.7071067811865476
INV_ROOT_TWO_PI = 0.3989422804014327

bf = jnp.bfloat16
f32 = jnp.float32
T, W, H, B = 2048, 256, 4, 256
LOG2E = math.log2(math.e)
C2 = LOG2E / 8.0
NT = (((1,), (1,)), ((), ()))
NN = (((1,), (0,)), ((), ()))
TN = (((0,), (0,)), ((), ()))


def dg(a, b, d):
    return lax.dot_general(a, b, d, preferred_element_type=f32)


def lanemask(rows,h):
    l=lax.broadcasted_iota(jnp.int32,(rows,W),1)
    return (l//HD)==h
def add_blocks(out, ins, rows, cols):
    step = max(16, min(rows, 65536 // cols))

    def body(i, carry):
        r = pl.ds(pl.multiple_of(i * step, 16), step)
        total = ins[0][r, :].astype(f32)
        for one in ins[1:]:
            total = total + one[r, :].astype(f32)
        out[r, :] = total.astype(bf)
        return carry

    lax.fori_loop(0, rows // step, body, 0)


def each(count, fn):
    def body(i, x):
        fn(i)
        return x

    lax.fori_loop(0, count, body, 0)


def tile_of(i, size=256):
    return pl.ds(pl.multiple_of(i * size, size), size)


def unit_rows(v):
    center = v - jnp.mean(v, axis=-1, keepdims=True)
    scaled = lax.rsqrt(jnp.mean(center * center, axis=-1, keepdims=True) + EPS)
    return center * scaled, scaled


def norm_rows(src, gain, bias, dst, rows):
    def chunk(i):
        r = tile_of(i, 128)
        unit, _ = unit_rows(src[r, :])
        dst[r, :] = (unit * gain[...] + bias[...]).astype(bf)

    each(rows // 128, chunk)


def norm_back_rows(up, src, gain, add, dst, dst_low, rows):
    def chunk(i, sums):
        r = tile_of(i, 64)
        unit, scaled = unit_rows(src[r, :])
        u = up[r, :]
        along = u * gain[...]
        inner = (
            along
            - jnp.mean(along, axis=-1, keepdims=True)
            - unit * jnp.mean(along * unit, axis=-1, keepdims=True)
        )
        total = add[r, :].astype(f32) + inner * scaled
        dst[r, :] = total
        dst_low[r, :] = total.astype(bf)
        fold = lambda v: jnp.sum(v.reshape(8, 8, v.shape[1]), axis=0)
        return sums[0] + fold(u * unit), sums[1] + fold(u)

    zero = jnp.zeros((8, src.shape[1]), f32)
    a, b = lax.fori_loop(0, rows // 64, chunk, (zero, zero))
    return jnp.sum(a, axis=0, keepdims=True), jnp.sum(b, axis=0, keepdims=True)


def remote(src, dst, send, recv, **where):
    return pltpu.make_async_remote_copy(
        src_ref=src, dst_ref=dst, send_sem=send, recv_sem=recv, device_id=where,
        device_id_type=pl.DeviceIdType.MESH,
    )


def greet(env, halves):
    s, c, z, seqs = env["s"], env["c"], env["z"], env["seqs"]
    whom = [{"clip": 2 * z + 1 - c}, {"clip": beside(env)}]
    whom += [{"seq": lax.rem(s + k, seqs)} for k in range(1, seqs)]
    whom += [
        {"clip": 2 * (2 * lax.rem(env["zh"] + k, halves) + env["zl"]) + c} for k in range(1, halves)
    ]
    barrier = pltpu.get_barrier_semaphore()
    for one in whom:
        pl.semaphore_signal(barrier, inc=1, device_id=one, device_id_type=pl.DeviceIdType.MESH)
    pl.semaphore_wait(barrier, len(whom))


def greet_all(env, clips):
    s, seqs = env["s"], env["seqs"]
    b = 2 * env["z"] + env["c"]
    whom = [{"seq": lax.rem(s + k, seqs)} for k in range(1, seqs)]
    whom += [{"clip": lax.rem(b + k, clips)} for k in range(1, clips)]
    barrier = pltpu.get_barrier_semaphore()
    for one in whom:
        pl.semaphore_signal(barrier, inc=1, device_id=one, device_id_type=pl.DeviceIdType.MESH)
    pl.semaphore_wait(barrier, len(whom))


def place(seqs):
    b = lax.axis_index("clip")
    z = lax.div(b, 2)
    return dict(
        seqs=seqs, s=lax.axis_index("seq"), c=lax.rem(b, 2), z=z, zh=lax.div(z, 2), zl=lax.rem(z, 2)
    )


def beside(env):
    return 2 * (2 * env["zh"] + 1 - env["zl"]) + env["c"]


def kb_kernel(seqs, *refs):
    (
        att, x_ref, gb, ck, cv, owner, g2, b2, g3, b3,
        w_o, w_cq, w_co, w_up, w_dn, n1_hbm,
    ) = refs[:16]
    (x1, fo, vec, c_up, c_dn, c_o, c_cq, c_co, heads, n1_all, kq, vq) = refs[16:28]
    (
        ring, up_st, dn_st, up_rv, dn_rv, sq_rv, x2, n2, n3, n3t, cq, co, probs, u, ut, dh,
        acc, dn3, up_nr, up_fr, dn_sr, kv_low, kv_rv, ring_sem, st_send, st_recv, out_sem, n1_sem, head_sem, kv_sem,
        near_sem, far_sem, seq_sem,
    ) = refs[28:]
    env = place(seqs)
    s, c, z = env["s"], env["c"], env["z"]
    rows, d = x_ref.shape
    halves, rb = up_rv.shape[0], up_rv.shape[2]
    pairs, zl = 2 * halves, env["zl"]
    ppc, rbd = dn_st.shape[0], dn_st.shape[2]
    steps = w_up.shape[1] // d
    width = d // seqs
    texts = ck.shape[0]
    depth = ring.shape[0]

    items = [w_o, w_cq, w_co]
    for t in range(steps):
        items += [w_up.at[:, pl.ds(t * d, d)], w_dn.at[pl.ds(t * d, d), :]]
    items += [w_co, w_cq, w_o]

    def load(i):
        return pltpu.make_async_copy(items[i], ring.at[i % depth], ring_sem.at[i % depth])

    def take(i):
        load(i).wait()
        return ring.at[i % depth]

    def drop(i):
        if i + depth < len(items):
            load(i + depth).start()

    for i in range(depth):
        load(i).start()
    greet(env, halves)

    peers = [(k, lax.rem(s + k, seqs)) for k in range(1, seqs)]
    spots = pl.ds(pl.multiple_of(s * rows, rows), rows)
    by_x, by_y = s + 1 - 2 * lax.rem(s, 2), lax.rem(s + 2, 4)
    here = lambda who, part: n1_all.at[
        pl.ds(pl.multiple_of(who * rows + part * (rows // 2), rows // 2), rows // 2), :
    ]
    n1_out = [
        remote(n1_hbm, n1_all.at[spots, :], n1_sem.at[0, k], n1_sem.at[1, k], seq=to)
        for k, to in ((1, by_x), (2, by_y))
    ]
    n1_on = [
        remote(here(by_y, 0), here(by_y, 0), n1_sem.at[0, 3], n1_sem.at[1, 3], seq=by_x),
        remote(here(by_x, 1), here(by_x, 1), n1_sem.at[0, 4], n1_sem.at[1, 4], seq=by_y),
    ]
    n1_own = pltpu.make_async_copy(n1_hbm, n1_all.at[spots, :], n1_sem.at[0, 0])
    start(n1_out)
    n1_own.start()

    w = take(0)

    def f(t):
        x1[:, tile_of(t)] = x_ref[:, tile_of(t)].astype(f32) + dg(att[...], w[:, tile_of(t)], NN)

    each(d // 256, f)
    drop(0)
    norm_rows(x1, g2, b2, n2, rows)
    w = take(1)

    def f(t):
        cq[:, tile_of(t)] = dg(n2[...], w[:, tile_of(t)], NN).astype(bf)

    each(d // 256, f)
    drop(1)
    half = rows
    key_clip = lax.broadcasted_iota(jnp.int32, (half, texts), 1) // TEXT

    def masked(v, h):
        lane = lax.broadcasted_iota(jnp.int32, v.shape, 1)
        return jnp.where(lane // HD == h, v, jnp.zeros_like(v))

    def f(n):
        t, r = lax.div(n, rows // half), tile_of(lax.rem(n, rows // half), half)
        allowed = owner[r, :] == key_clip
        q, k, v = cq[r, tile_of(t)], ck[:, tile_of(t)], cv[:, tile_of(t)]
        total = jnp.zeros((half, 256), f32)
        for h in range(256 // HD):
            sc = jnp.where(allowed, dg(masked(q, h), k, NT), NEG)
            p = jnp.exp2((sc - jnp.max(sc, axis=-1, keepdims=True)) * C2)
            p = (p / jnp.sum(p, axis=-1, keepdims=True)).astype(bf)
            probs[t * (256 // HD) + h, r, :] = p
            total = total + dg(p, masked(v, h), NN)
        co[r, tile_of(t)] = total.astype(bf)

    each(d // 256 * (rows // half), f)
    w = take(2)

    def f(t):
        x2[:, tile_of(t)] = x1[:, tile_of(t)] + dg(co[...], w[:, tile_of(t)], NN)

    each(d // 256, f)
    drop(2)
    norm_rows(x2, g3, b3, n3, rows)

    def turn(src, dst):
        def f(t):
            dst[tile_of(t), :] = src[:, tile_of(t)].T

        each(d // 256, f)

    turn(n3, n3t)

    def swap(n, src, dst):
        return remote(src, dst, st_send.at[n], st_recv.at[n], clip=2 * z + 1 - c)

    def up_swap(t):
        return swap(2 * t, up_st.at[0, :, :, 1 - c], up_rv.at[:, :, :, pl.ds(t * d, d)])

    def dn_swap(t):
        return swap(2 * t + 1, dn_st.at[:, 1 - c], dn_rv.at[pl.ds(t * ppc, ppc)])

    def up_near(t):
        cols = pl.ds(t * d, d)
        return remote(
            up_rv.at[:, 1 - zl, :, cols], up_nr.at[:, :, cols], near_sem.at[0, t], near_sem.at[1, t],
            clip=beside(env),
        )

    def dn_seq(t):
        blocks = pl.ds(t * ppc, ppc)
        return [
            remote(
                dn_rv.at[blocks, :, pl.ds(pl.multiple_of(to * width, 128), width)], dn_sr.at[k - 1, blocks],
                seq_sem.at[0, t, k], seq_sem.at[1, t, k], seq=to,
            )
            for k, to in peers
        ]

    def up_out(t):
        cols = pl.ds(t * d, d)
        return pltpu.make_async_copy(up_fr.at[0, :, cols], c_up.at[:, cols], out_sem.at[2 * t])

    def up_far(t):
        cols = pl.ds(t * d, d)
        copies = []
        for k in range(1, halves):
            to = lax.rem(env["zh"] + k, halves)
            copies.append(
                remote(
                    up_nr.at[to, :, cols], up_fr.at[k - 1, :, cols], far_sem.at[0, t, k], far_sem.at[1, t, k],
                    clip=2 * (2 * to + zl) + c,
                )
            )
        return copies

    def dn_out(t):
        blocks = pl.ds(t * ppc, ppc)
        return pltpu.make_async_copy(dn_sr.at[0, blocks], c_dn.at[blocks], out_sem.at[2 * t + 1])

    def settle(t):
        cols = pl.ds(t * d, d)
        one = up_swap(t)
        one.wait_recv()
        for p in range(halves):
            for l in range(2):
                dst = up_rv.at[p, l, :, cols]
                add_blocks(dst, [dst, up_st.at[0, p, l, c]], rb, d)
        one.wait_send()
        up_near(t).start()
        one = dn_swap(t)
        one.wait_recv()
        for p in range(ppc):
            dst = dn_rv.at[t * ppc + p]
            add_blocks(dst, [dst, dn_st.at[p, c]], rbd, d)
        one.wait_send()
        start(dn_seq(t))

    mine = pl.ds(pl.multiple_of(s * width, 128), width)

    def settle_near(t):
        cols = pl.ds(t * d, d)
        one = up_near(t)
        one.wait_recv()
        for p in range(halves):
            dst = up_nr.at[p, :, cols]
            add_blocks(dst, [dst, up_rv.at[p, zl, :, cols]], rb, d)
        start(up_far(t))

    def settle_dn(t):
        arrive(dn_seq(t))
        for p in range(t * ppc, (t + 1) * ppc):
            add_blocks(
                dn_sr.at[0, p],
                [dn_rv.at[p, :, mine]] + [dn_sr.at[k - 1, p] for k, _ in peers],
                rbd,
                width,
            )
        dn_out(t).start()

    def settle_last(t):
        cols = pl.ds(t * d, d)
        arrive(up_far(t))
        others = [up_fr.at[k - 1, :, cols] for k in range(1, halves)]
        add_blocks(up_fr.at[0, :, cols], [up_nr.at[env["zh"], :, cols]] + others, rb, d)
        up_out(t).start()

    for t in range(steps):
        wu, wd = take(3 + 2 * t), take(4 + 2 * t)

        def f(i):
            h = dg(n3[...], wu[:, tile_of(i)], NN)
            du = dg(gb[...], wd[tile_of(i), :], NT)
            part = 0.5 * (1.0 + lax.erf(h * SQRT_HALF))
            slope = part + h * jnp.exp2(h * h * (-0.5 * LOG2E)) * INV_ROOT_TWO_PI
            dh[:, tile_of(i)] = (du * slope).astype(bf)
            act = (h * part).astype(bf)
            u[:, tile_of(i)] = act
            ut[tile_of(i), :] = act.T

        each(d // 256, f)
        if t > 0:
            settle(t - 1)
        if t > 2:
            settle_near(t - 3)

        def f(i, t=t):
            a = dg(u[...], wd[:, tile_of(i)], NN)
            b = dg(dh[...], wu[tile_of(i), :], NT)
            if t == 0:
                acc[:, tile_of(i)] = a
                dn3[:, tile_of(i)] = b
            else:
                acc[:, tile_of(i)] += a
                dn3[:, tile_of(i)] += b
            g = dg(n3t[...], dh[:, tile_of(i)], NN).astype(bf)
            up_st[0, :, :, :, :, tile_of(i)] = g.reshape(halves, 2, 2, rb, 256)
            g = dg(ut[...], gb[:, tile_of(i)], NN).astype(bf)
            dn_st[:, :, :, tile_of(i)] = g.reshape(ppc, 2, rbd, 256)

        each(d // 256, f)
        drop(3 + 2 * t)
        drop(4 + 2 * t)
        up_swap(t).start()
        dn_swap(t).start()

    def f(i):
        r = tile_of(i, 64)
        fo[r, :] = (x2[r, :] + acc[r, :]).astype(bf)

    each(rows // 64, f)
    base = 3 + 2 * steps
    settle(steps - 1)
    settle_near(steps - 3)
    arrive(n1_out)
    start(n1_on)
    low = u
    sums = norm_back_rows(dn3, x2, g3, gb, acc, low, rows)
    vec[2:3, :], vec[3:4, :] = sums
    w = take(base)
    dco = dh

    def f(t):
        dco[:, tile_of(t)] = dg(low[...], w[tile_of(t), :], NT).astype(bf)

    each(d // 256, f)
    drop(base)
    settle_near(steps - 2)

    def grad(n, slot, a, low):
        turn(a, n3t)

        def f(t):
            g = dg(n3t[...], low[:, tile_of(t)], NN).astype(bf)
            up_st[slot, :, :, :, :, tile_of(t)] = g.reshape(halves, 2, 2, rb, 256)

        each(d // 256, f)
        grad_swap(n, slot).start()

    def grad_swap(n, slot):
        return swap(2 * steps + n, up_st.at[slot, :, :, 1 - c], sq_rv.at[n])

    def grad_out(n):
        return pltpu.make_async_copy(sq_rv.at[n], (c_co, c_cq, c_o)[n], out_sem.at[2 * steps + n])

    def grad_settle(n, slot):
        one = grad_swap(n, slot)
        one.wait_recv()
        for p in range(halves):
            for l in range(2):
                add_blocks(sq_rv.at[n, p, l], [sq_rv.at[n, p, l], up_st.at[slot, p, l, c]], rb, d)
        one.wait_send()
        grad_out(n).start()

    grad(0, 0, co, low)
    dcq = n3

    def f(t):
        k, v = ck[:, tile_of(t)], cv[:, tile_of(t)]
        sum_k = jnp.zeros((texts, 256), f32)
        sum_v = jnp.zeros((texts, 256), f32)
        for n in range(rows // half):
            r = pl.ds(n * half, half)
            q, g = cq[r, tile_of(t)], dco[r, tile_of(t)]
            out = jnp.zeros((half, 256), f32)
            for h in range(256 // HD):
                p_low = probs[t * (256 // HD) + h, r, :]
                p = p_low.astype(f32)
                dp = dg(masked(g, h), v, NT)
                inner = jnp.sum(p * dp, axis=-1, keepdims=True)
                ds = (p * (dp - inner)).astype(bf)
                out = out + dg(ds, masked(k, h), NN)
                sum_k = sum_k + dg(ds, masked(q, h), TN)
                sum_v = sum_v + dg(p_low, masked(g, h), TN)
            dcq[r, tile_of(t)] = (out * 0.125).astype(bf)
        kv_low[0, :, tile_of(t)] = (sum_k * 0.125).astype(bf)
        kv_low[1, :, tile_of(t)] = sum_v.astype(bf)

    each(d // 256, f)
    kv_out = [
        remote(
            kv_low.at[:, :, pl.ds(pl.multiple_of(to * width, 128), width)], kv_rv.at[k - 1],
            kv_sem.at[0, k], kv_sem.at[1, k], seq=to,
        )
        for k, to in peers
    ]
    start(kv_out)
    settle_near(steps - 1)
    w = take(base + 1)
    dn2 = dn3

    def f(t):
        dn2[:, tile_of(t)] = dg(dcq[...], w[tile_of(t), :], NT)

    each(d // 256, f)
    drop(base + 1)
    sums = norm_back_rows(dn2, x1, g2, acc, x1, low, rows)
    vec[0:1, :], vec[1:2, :] = sums
    vec[4:8, :] = jnp.zeros((4, d), f32)
    w = take(base + 2)
    do = dh

    def f(t):
        do[:, tile_of(t)] = dg(low[...], w[tile_of(t), :], NT).astype(bf)

    each(d // 256, f)
    head_out = [
        remote(
            do.at[:, pl.ds(pl.multiple_of(to * width, 128), width)], heads.at[spots, :],
            head_sem.at[0, k], head_sem.at[1, k], seq=to,
        )
        for k, to in peers
    ]
    head_own = pltpu.make_async_copy(do.at[:, mine], heads.at[spots, :], head_sem.at[0, 0])
    start(head_out)
    head_own.start()
    grad_settle(0, 0)
    grad(1, 0, n2, dcq)
    for t in range(steps - 2):
        settle_dn(t)
        settle_last(t)
    grad_settle(1, 0)
    grad(2, 0, att, low)
    settle_dn(steps - 2)
    settle_last(steps - 2)
    grad_settle(2, 0)
    arrive(kv_out)
    for n, dst in enumerate((kq, vq)):
        total = kv_low[n, :, mine].astype(f32)
        for k in range(1, seqs):
            total = total + kv_rv[k - 1, n].astype(f32)
        dst[...] = total.astype(bf)
    settle_dn(steps - 1)
    settle_last(steps - 1)
    finish(kv_out)
    head_own.wait()
    n1_own.wait()
    for one in head_out + n1_on:
        one.wait()
    finish(n1_out)
    for t in range(steps):
        up_near(t).wait_send()
        finish(up_far(t))
        finish(dn_seq(t))
        up_out(t).wait()
        dn_out(t).wait()
    for n in range(3):
        grad_out(n).wait()


def kb(seqs, clips, att, x, gb, ck, cv, owner, g2, b2, g3, b3, w_o, w_cq, w_co, w_up, w_dn, n1):
    rows, d = x.shape
    pairs = clips // 2
    halves = pairs // 2
    rb, rbd = d // clips, w_dn.shape[0] // clips
    steps = w_up.shape[1] // d
    ppc = pairs // steps
    texts = ck.shape[0]
    width = d // seqs
    hbm = pl.BlockSpec(memory_space=pl.ANY)
    vmem = pl.BlockSpec(memory_space=pltpu.VMEM)
    low = lambda *shape: pltpu.VMEM(shape, bf)
    full = lambda *shape: pltpu.VMEM(shape, f32)
    s_low = lambda *shape: jax.ShapeDtypeStruct(shape, bf)
    dma = pltpu.SemaphoreType.DMA
    return pl.pallas_call(
        functools.partial(kb_kernel, seqs),
        out_shape=[
            jax.ShapeDtypeStruct((rows, d), f32),
            s_low(rows, d),
            jax.ShapeDtypeStruct((8, d), f32),
            s_low(rb, steps * d),
            s_low(pairs, rbd, width),
            s_low(halves, 2, rb, d),
            s_low(halves, 2, rb, d),
            s_low(halves, 2, rb, d),
            s_low(rows * seqs, width),
            s_low(rows * seqs, d),
            s_low(texts, width),
            s_low(texts, width),
        ],
        in_specs=[vmem] * 10 + [hbm] * 6,
        out_specs=[vmem] * 3 + [hbm] * 7 + [vmem] * 2,
        scratch_shapes=[
            low(4, d, d),
            low(1, halves, 2, 2, rb, d),
            low(ppc, 2, rbd, d),
            low(halves, 2, rb, steps * d),
            low(pairs, rbd, d),
            low(3, halves, 2, rb, d),
            full(rows, d),
            low(rows, d),
            low(rows, d),
            low(d, rows),
            low(rows, d),
            low(rows, d),
            low(d // HD, rows, texts),
            low(rows, d),
            low(d, rows),
            low(rows, d),
            full(rows, d),
            full(rows, d),
            low(halves, rb, steps * d),
            low(max(1, halves - 1), rb, steps * d),
            low(seqs - 1, pairs, rbd, width),
            low(2, texts, d),
            low(seqs - 1, 2, texts, width),
            dma((4,)),
            dma((2 * steps + 3,)),
            dma((2 * steps + 3,)),
            dma((2 * steps + 3,)),
            dma((2, 5)),
            dma((2, seqs)),
            dma((2, seqs)),
            dma((2, steps)),
            dma((2, steps, halves)),
            dma((2, steps, seqs)),
        ],
        compiler_params=pltpu.CompilerParams(
            collective_id=2, has_side_effects=True, vmem_limit_bytes=60 * 2**20
        ),
    )(
        att, x, gb, ck, cv, owner[:, None],
        *[v[None] for v in (g2, b2, g3, b3)],
        w_o, w_cq, w_co, w_up, w_dn, n1,
    )


def ka_kernel(seqs, *refs):
    x_ref, g1, b1, first, text, w_q, w_k, w_v, w_xk, w_xv = refs[:10]
    n1_out, o_out, lse_out, q_out, k_out, v_out, att, ck_out, cv_out = refs[10:19]
    (
        w_buf, wide, stage, held, vt, n1, o_ref, lse_ref, c_buf, w_sem, send, recv, push_send, push_recv, out_sem,
    ) = refs[19:]
    env = place(seqs)
    s = env["s"]
    rows, d = x_ref.shape
    pair = 2 * HD
    loads = [
        pltpu.make_async_copy(one, w_buf.at[n], w_sem.at[n]) for n, one in enumerate((w_q, w_k, w_v, w_xk, w_xv))
    ]
    start(loads)
    greet_seq(env)

    def f(i):
        r = tile_of(i, 64)
        wide[r, :] = x_ref[r, :].astype(f32)

    each(rows // 64, f)
    norm_rows(wide, g1, b1, n1, rows)
    outs = [pltpu.make_async_copy(n1, n1_out, out_sem.at[3])]
    start(outs)
    spots = pl.ds(pl.multiple_of(s * rows, rows), rows)
    peers = [(k, lax.rem(s + k, seqs)) for k in range(1, seqs)]

    def sends(g):
        return [
            remote(
                stage.at[:, :, pl.ds(pl.multiple_of(to * W + g * pair, 128), pair)],
                held.at[:, spots, pl.ds(g * pair, pair)],
                send.at[g, k], recv.at[g, k], seq=to,
            )
            for k, to in peers
        ]

    for one in loads[:3]:
        one.wait()
    first_sends = sends(0)
    for n, (k, to) in enumerate(peers):
        cols = pl.ds(pl.multiple_of(to * W, 128), W)
        for t in range(3):
            stage[t, :, cols] = dg(n1[...], w_buf[t, :, cols], NN).astype(bf)
        first_sends[n].start()
    cols = pl.ds(pl.multiple_of(s * W, 128), W)
    for t in range(3):
        held[t, spots, :] = dg(n1[...], w_buf[t, :, cols], NN).astype(bf)

    for n, one in enumerate((ck_out, cv_out)):
        loads[3 + n].wait()

        def f(t, n=n):
            c_buf[n, :, tile_of(t)] = dg(text[...], w_buf[3 + n, :, tile_of(t)], NN).astype(bf)

        each(d // 256, f)
        outs.append(pltpu.make_async_copy(c_buf.at[n], one, out_sem.at[4 + n]))
        outs[-1].start()

    lane = lax.broadcasted_iota(jnp.int32, (1, pair), 1) // HD
    kvi = lax.broadcasted_iota(jnp.int32, (rows, rows), 0)
    qi = lax.broadcasted_iota(jnp.int32, (rows, rows), 1)

    def qblock(g, i, masked):
        ln = pl.ds(g * pair, pair)
        r = tile_of(i, rows)
        q = held[0, r, ln]
        qm = [jnp.where(lane == h, q, jnp.zeros_like(q)) for h in range(2)]
        fst = first[:, r]

        def step(j, carry, diag):
            c = tile_of(j, rows)
            k = held[1, c, ln]
            out = []
            for h in range(2):
                m, l, acc = carry[h]
                sc = dg(k, qm[h], NT)
                if diag:
                    sc = jnp.where(kvi <= qi, sc, NEG)
                if masked:
                    sc = jnp.where(kvi + j * rows >= fst, sc, NEG)
                top = jnp.maximum(m, jnp.max(sc, axis=0, keepdims=True))
                p = jnp.exp2((sc - top) * C2)
                a = jnp.exp2((m - top) * C2)
                l = l * a + jnp.sum(p, axis=0, keepdims=True)
                acc = acc * a + dg(vt[h * HD : (h + 1) * HD, c], p.astype(bf), NN)
                out.append((top, l, acc))
            return tuple(out)

        carry = tuple(
            (jnp.full((1, rows), NEG, f32), jnp.zeros((1, rows), f32), jnp.zeros((HD, rows), f32))
            for _ in range(2)
        )
        carry = lax.fori_loop(0, i, lambda j, x: step(j, x, False), carry)
        carry = step(i, carry, True)
        ot = jnp.concatenate([acc / l for _, l, acc in carry], axis=0)
        o_ref[r, ln] = ot.T.astype(bf)
        for h in range(2):
            lse_ref[2 * g + h : 2 * g + h + 1, r] = carry[h][0] * C2 + jnp.log2(carry[h][1])

    def push(g, owner, away):
        src = o_ref.at[tile_of(owner, rows), pl.ds(g * pair, pair)]
        dst = att.at[:, pl.ds(pl.multiple_of(s * W + g * pair, 128), pair)]
        k = lax.rem(owner - s + seqs, seqs)
        if away:
            return remote(src, dst, push_send.at[g, owner], push_recv.at[g, k], seq=owner)
        return pltpu.make_async_copy(src, dst, push_send.at[g, owner])

    def send_rows(g, owner):
        @pl.when(s != owner)
        def _():
            push(g, owner, True).start()

        @pl.when(s == owner)
        def _():
            push(g, owner, False).start()

    lse_ref[4:8, :] = jnp.zeros((4, lse_ref.shape[1]), f32)
    for g in range(2):
        arrive(sends(g))
        if g == 0:
            start(sends(1))
        else:
            heads = [
                pltpu.make_async_copy(held.at[n], one, out_sem.at[n])
                for n, one in enumerate((q_out, k_out, v_out))
            ]
            start(heads)
            outs += heads

        def f(i, g=g):
            r = tile_of(i, rows)
            vt[:, r] = held[2, r, pl.ds(g * pair, pair)].T

        each(seqs, f)

        def f(i, g=g):
            qblock(g, i, False)
            send_rows(g, i)

        plain = TAIL // rows
        each(plain, f)
        for i in range(plain, seqs):
            qblock(g, i, True)
            send_rows(g, i)
    last = [pltpu.make_async_copy(o_ref, o_out, out_sem.at[6]), pltpu.make_async_copy(lse_ref, lse_out, out_sem.at[7])]
    start(last)
    for one in outs + last:
        one.wait()
    for g in range(2):
        finish(sends(g))
        for owner in range(seqs):
            @pl.when(s != owner)
            def _():
                push(g, owner, True).wait_send()

            @pl.when(s == owner)
            def _():
                push(g, owner, False).wait()
        for k in range(1, seqs):
            back = lax.rem(s - k + seqs, seqs)
            dst = att.at[:, pl.ds(pl.multiple_of(back * W + g * pair, 128), pair)]
            pltpu.make_async_copy(dst, dst, push_recv.at[g, k]).wait()


def greet_seq(env):
    s, seqs = env["s"], env["seqs"]
    barrier = pltpu.get_barrier_semaphore()
    for k in range(1, seqs):
        pl.semaphore_signal(
            barrier, inc=1, device_id={"seq": lax.rem(s + k, seqs)}, device_id_type=pl.DeviceIdType.MESH
        )
    pl.semaphore_wait(barrier, seqs - 1)


def ka(seqs, x, g1, b1, first, text, weights):
    rows, d = x.shape
    hbm = pl.BlockSpec(memory_space=pl.ANY)
    vmem = pl.BlockSpec(memory_space=pltpu.VMEM)
    dma = pltpu.SemaphoreType.DMA
    s_low = lambda *shape: jax.ShapeDtypeStruct(shape, bf)
    total = rows * seqs
    return pl.pallas_call(
        functools.partial(ka_kernel, seqs),
        out_shape=[
            s_low(rows, d),
            s_low(total, W),
            jax.ShapeDtypeStruct((8, total), f32),
            s_low(total, W),
            s_low(total, W),
            s_low(total, W),
            s_low(rows, d),
            s_low(text.shape[0], d),
            s_low(text.shape[0], d),
        ],
        in_specs=[vmem] * 5 + [hbm] * 5,
        out_specs=[hbm] * 9,
        scratch_shapes=[
            pltpu.VMEM((5, d, d), bf),
            pltpu.VMEM((rows, d), f32),
            pltpu.VMEM((3, rows, d), bf),
            pltpu.VMEM((3, total, W), bf),
            pltpu.VMEM((2 * HD, total), bf),
            pltpu.VMEM((rows, d), bf),
            pltpu.VMEM((total, W), bf),
            pltpu.VMEM((8, total), f32),
            pltpu.VMEM((2, text.shape[0], d), bf),
            dma((5,)),
            dma((2, seqs)),
            dma((2, seqs)),
            dma((2, seqs)),
            dma((2, seqs)),
            dma((8,)),
        ],
        compiler_params=pltpu.CompilerParams(
            collective_id=3, has_side_effects=True, vmem_limit_bytes=60 * 2**20
        ),
    )(x, g1[None], b1[None], first, text, *weights)


class Job:
    def __init__(self, steps, part, bufs, sems, out, env, halves):
        self.steps, self.part, self.out, self.env, self.halves = steps, part, out, env, halves
        self.r0, self.rm, self.rn, self.rf, self.rs = bufs
        self.sems = sems
        self.rb, self.n = part.shape[-2:]
        self.first = "split" in steps
        self.q = self.n // env["seqs"] if "seq" in steps or self.first else self.n
        self.done = self.rs if "seq" in steps else self.rf
        self.bare = steps == ("seq",)
        self.cored = self.r0 if "cores" in steps else (self.rs.at[0] if self.first else part)
        self.w = self.q if self.first else self.n

    def copy(self, stage, k, src, dst, **where):
        return remote(src, dst, self.sems.at[0, stage, k], self.sems.at[1, stage, k], **where)

    def cores(self):
        e = self.env
        return [
            self.copy(0, 0, self.part.at[:, :, 1 - e["c"]], self.r0, clip=2 * e["z"] + 1 - e["c"])
        ]

    def sum_cores(self):
        for p in range(self.halves):
            for l in range(2):
                one = self.r0.at[p, l]
                add_blocks(one, [one, self.part.at[p, l, self.env["c"]]], self.rb, self.n)

    def split(self):
        e, copies = self.env, []
        for k in range(1, e["seqs"]):
            to = lax.rem(e["s"] + k, e["seqs"])
            copies.append(
                self.copy(3, k - 1, self.part.at[:, :, :, self.columns(to)], self.rs.at[k - 1], seq=to)
            )
        return copies

    def sum_split(self):
        self.load().wait()
        for p in range(self.halves):
            for l in range(2):
                others = [self.rs.at[k, p, l] for k in range(self.env["seqs"] - 1)]
                add_blocks(self.rs.at[0, p, l], [self.rm.at[p, l]] + others, self.rb, self.q)

    def load(self):
        if self.first or self.bare:
            at = (slice(None),) * (len(self.part.shape) - 1) + (self.columns(self.env["s"]),)
            src = self.part.at[at]
            return pltpu.make_async_copy(src, self.rm, self.sems.at[0, 5, 0])
        src = self.part.at[:, self.env["zl"]] if "near" in self.steps else self.part.at[self.env["zh"]]
        return pltpu.make_async_copy(src, self.rm, self.sems.at[0, 5, 0])

    def near(self):
        return [self.copy(1, 0, self.cored.at[:, 1 - self.env["zl"]], self.rn, clip=beside(self.env))]

    def sum_near(self):
        loaded = "cores" not in self.steps and not self.first
        if loaded:
            self.load().wait()
        for p in range(self.halves):
            mine = self.rm.at[p] if loaded else self.cored.at[p, self.env["zl"]]
            add_blocks(self.rn.at[p], [self.rn.at[p], mine], self.rb, self.w)

    def far(self):
        e, copies = self.env, []
        src = self.rn if "near" in self.steps else self.part
        for k in range(1, self.halves):
            to = lax.rem(e["zh"] + k, self.halves)
            copies.append(
                self.copy(2, k - 1, src.at[to], self.rf.at[k - 1], clip=2 * (2 * to + e["zl"]) + e["c"])
            )
        return copies

    def sum_far(self):
        if "near" in self.steps:
            mine = self.rn.at[self.env["zh"]]
        else:
            self.load().wait()
            mine = self.rm
        add_blocks(self.rf.at[0], [mine] + [self.rf.at[k] for k in range(self.halves - 1)], self.rb, self.w)

    def columns(self, s):
        return pl.ds(pl.multiple_of(s * self.q, 128), self.q)

    def seq(self):
        e, copies = self.env, []
        for k in range(1, e["seqs"]):
            to = lax.rem(e["s"] + k, e["seqs"])
            src = self.part.at[:, self.columns(to)] if self.bare else self.rf.at[0, :, self.columns(to)]
            copies.append(self.copy(3, k - 1, src, self.rs.at[k - 1], seq=to))
        return copies

    def sum_seq(self):
        if self.bare:
            self.load().wait()
            mine = self.rm
        else:
            mine = self.rf.at[0, :, self.columns(self.env["s"])]
        others = [self.rs.at[k] for k in range(self.env["seqs"] - 1)]
        add_blocks(self.rs.at[0], [mine] + others, self.rb, self.q)

    def gather(self):
        e, copies = self.env, []
        for k in range(1, e["seqs"]):
            to = lax.rem(e["s"] + k, e["seqs"])
            copies.append(
                self.copy(4, k - 1, self.done.at[0], self.out.at[:, self.columns(e["s"])], seq=to)
            )
        return copies

    def keep(self):
        return pltpu.make_async_copy(
            self.done.at[0], self.out.at[:, self.columns(self.env["s"])], self.sems.at[1, 5, 0]
        )

    def spread(self):
        start(self.gather())
        self.keep().start()

    def close(self):
        for name in self.steps:
            finish(getattr(self, name)())
        finish(self.gather())
        self.keep().wait()
        arrive(self.gather())


def start(copies):
    for one in copies:
        one.start()


def arrive(copies):
    for one in copies:
        one.wait_recv()


def finish(copies):
    for one in copies:
        one.wait_send()


def job_bufs(steps, shape, seqs, halves):
    rb, n = shape[-2:]
    low = lambda use, *dims: pltpu.VMEM(dims if use else (16, 128), bf)
    cores, near, split = ("cores" in steps), ("near" in steps), ("split" in steps)
    q = n // seqs
    w = q if split else n
    mine = (halves, 2, rb, q) if split else ((halves, rb, n) if near else (rb, q))
    return [
        low(cores, halves, 2, rb, n),
        low(not cores, *mine),
        low(near, halves, rb, w),
        low("far" in steps, max(1, halves - 1), rb, w),
        pltpu.VMEM((seqs - 1, halves, 2, rb, q), bf) if split else low("seq" in steps, seqs - 1, rb, q),
    ]


LAST = pl.DeviceIdType.MESH


def kc_kernel(seqs, halves, *refs):
    (q_ref, k_ref, v_ref, o_ref, g_ref, lse_ref, first_ref) = refs[:7]
    (kq, vq, text, x_ref, dx1, g1, vec_in, n1_hbm, w_q, w_k, w_v, *parts) = refs[7:23]
    (frames_grad, vec, k_all, v_all, *outs) = refs[23:37]
    dq_s, dk_s, dv_s, dka, dva, n1_buf, wacc, wsum, wparts, dqkv, w_buf, dn1, vec_rv, low_buf, *rest = refs[37:]
    sems, push_send, push_recv, local_sem, kv_sem, vec_sem = rest[-6:]
    bufs = rest[:-6]
    env = place(seqs)
    s, c, z = env["s"], env["c"], env["z"]
    frames = T // seqs
    d = n1_hbm.shape[1]
    greet_all(env, 4 * halves)

    jobs = []
    for t, steps in enumerate(STEPS):
        src = parts[t] if t < 5 else wparts.at[t - 5]
        jobs.append(Job(steps, src, bufs[5 * t : 5 * t + 5], sems.at[t], outs[t], env, halves))
    up, down, go, gcq, gco, gxk, gxv, gq, gk, gv = jobs
    start(gco.split())
    start(up.seq())
    start(down.near())
    start(go.near())
    for one in (up, down, go, gcq, gco):
        one.load().start()
    width = kq.shape[1]
    spot = pl.ds(pl.multiple_of(s * width, 128), width)
    kv_out, kv_own = [], []
    for n, (src, dst) in enumerate(((kq, k_all), (vq, v_all))):
        for k in range(1, seqs):
            kv_out.append(
                remote(src, dst.at[:, spot], kv_sem.at[0, n, k], kv_sem.at[1, n, k], seq=lax.rem(s + k, seqs))
            )
        kv_own.append(pltpu.make_async_copy(src, dst.at[:, spot], kv_sem.at[0, n, 0]))
    start(kv_out)
    start(kv_own)
    loads = [pltpu.make_async_copy(n1_hbm, n1_buf, local_sem.at[0])]
    for n, one in enumerate((w_q, w_k, w_v)):
        loads.append(pltpu.make_async_copy(one, w_buf.at[n], local_sem.at[1 + n]))
    start(loads)

    def place_product(n, rb):
        wparts[n] = wacc[...].astype(bf).reshape(halves, 2, 2, rb, W)

    for n, src in enumerate((kq, vq)):
        wacc[...] = dg(text[...], src[...], TN)
        place_product(n, gxk.rb)
        start((gxk, gxv)[n].cores())

    dka[...] = jnp.zeros_like(dka)
    dva[...] = jnp.zeros_like(dva)

    lane = lax.broadcasted_iota(jnp.int32, (1, W), 1) // HD
    kvi = lax.broadcasted_iota(jnp.int32, (frames, frames), 0)
    qi = lax.broadcasted_iota(jnp.int32, (frames, frames), 1)

    def qblock(i, masked):
        r = pl.ds(i * frames, frames)
        q = q_ref[r, :]
        g = g_ref[r, :]
        both = g.astype(f32) * o_ref[r, :].astype(f32)
        hm = (
            lax.broadcasted_iota(jnp.int32, (8, W), 1) // HD == lax.broadcasted_iota(jnp.int32, (8, W), 0)
        ).astype(f32)
        delta = lax.dot_general(hm, both, NT, precision=lax.Precision.HIGHEST, preferred_element_type=f32)
        lse = lse_ref[:, r]
        fst = first_ref[:, r]
        zero = jnp.zeros_like(q)
        qm = [jnp.where(lane == h, q, zero) for h in range(H)]
        gm = [jnp.where(lane == h, g, zero) for h in range(H)]

        def tile(j, dq, diag):
            at = tile_of(j, frames)
            k = k_ref[at, :]
            v = v_ref[at, :]
            dv = jnp.zeros((frames, W), f32)
            dk = jnp.zeros((frames, W), f32)
            for h in range(H):
                p = jnp.exp2(dg(k, qm[h], NT) * C2 - lse[h : h + 1])
                if diag:
                    p = jnp.where(kvi <= qi, p, 0.0)
                if masked:
                    p = jnp.where(kvi + j * frames >= fst, p, 0.0)
                dp = dg(v, gm[h], NT)
                ds = (p * (dp - delta[h : h + 1])).astype(bf)
                dv = dv + dg(p.astype(bf), gm[h], NN)
                dk = dk + dg(ds, qm[h], NN)
                dq = dq + dg(ds, jnp.where(lane == h, k, jnp.zeros_like(k)), TN)
            dva[at, :] += dv
            dka[at, :] += dk
            return dq

        dq = jnp.zeros((frames, W), f32)
        dq = lax.fori_loop(0, i, lambda j, x: tile(j, x, False), dq)
        dq = tile(i, dq, True)
        dq_s[r, :] = (dq * 0.125).astype(bf)
        dk_s[r, :] = (dka[r, :] * 0.125).astype(bf)
        dv_s[r, :] = dva[r, :].astype(bf)

    lanes = pl.ds(pl.multiple_of(s * W, 128), W)
    moved = [(src, dqkv.at[n]) for n, src in enumerate((dq_s, dk_s, dv_s))]

    def pushes(owner):
        k = lax.rem(owner - s + seqs, seqs)
        rows = pl.ds(owner * frames, frames)
        return [
            pltpu.make_async_remote_copy(
                src_ref=src.at[rows, :],
                dst_ref=dst.at[:, lanes],
                send_sem=push_send.at[n, owner],
                recv_sem=push_recv.at[n, k],
                device_id={"seq": owner},
                device_id_type=LAST,
            )
            for n, (src, dst) in enumerate(moved)
        ]

    def keeps(owner):
        rows = pl.ds(owner * frames, frames)
        return [
            pltpu.make_async_copy(src.at[rows, :], dst.at[:, lanes], push_send.at[n, owner])
            for n, (src, dst) in enumerate(moved)
        ]

    for owner in reversed(range(seqs)):
        qblock(owner, (owner + 1) * frames > TAIL)

        @pl.when(s != owner)
        def _():
            start(pushes(owner))

        @pl.when(s == owner)
        def _():
            start(keeps(owner))

        if owner == seqs - 1:
            start(gcq.near())
            for one in (gxk, gxv):
                arrive(one.cores())
                one.sum_cores()
                start(one.near())
            arrive(up.seq())
            up.sum_seq()
            up.spread()
        if owner == seqs - 2:
            arrive(gco.split())
            gco.sum_split()
            start(gco.near())
            for one in (down, go):
                arrive(one.near())
                one.sum_near()
                start(one.far())

    loads[0].wait()
    for one in (gxk, gxv, gco, gcq):
        arrive(one.near())
        one.sum_near()
        start(one.far())

    def product(r, x):
        rows = tile_of(r, 512)
        left = n1_buf[rows, :]
        for n, src in enumerate((dq_s, dk_s, dv_s)):
            cols = pl.ds(n * W, W)
            add = dg(left, src[rows, :], TN)
            wsum[:, cols] = jnp.where(r == 0, add, wsum[:, cols] + add)
        return x

    lax.fori_loop(0, T // 512, product, 0)
    for n, one in enumerate((gq, gk, gv)):
        wparts[2 + n] = wsum[:, n * W : (n + 1) * W].astype(bf).reshape(halves, 2, 2, gq.rb, W)
        start(one.cores())
    arrive(down.far())
    down.sum_far()
    down.spread()
    for one in (gq, gk, gv):
        arrive(one.cores())
        one.sum_cores()
        start(one.near())
    arrive(go.far())
    go.sum_far()
    start(go.seq())
    for one in (gxk, gxv, gco):
        arrive(one.far())
        one.sum_far()
        one.spread()
    arrive(gcq.far())
    gcq.sum_far()
    start(gcq.seq())
    for one in (gq, gk, gv):
        arrive(one.near())
        one.sum_near()
        start(one.far())

    for k in range(1, seqs):
        for n in range(3):
            dst = dqkv.at[n, :, pl.ds(pl.multiple_of(lax.rem(s - k + seqs, seqs) * W, 128), W)]
            pltpu.make_async_copy(dst, dst, push_recv.at[n, k]).wait()
    for owner in range(seqs):
        @pl.when(s != owner)
        def _():
            finish(pushes(owner))

        @pl.when(s == owner)
        def _():
            for one in keeps(owner):
                one.wait()
    for n in range(3):
        loads[1 + n].wait()

        def f(t, n=n):
            add = dg(dqkv[n], w_buf[n, tile_of(t), :], NT)
            if n == 0:
                dn1[:, tile_of(t)] = add
            else:
                dn1[:, tile_of(t)] += add

        each(d // 256, f)

    def f(i):
        r = tile_of(i, 64)
        wide_x[r, :] = x_ref[r, :].astype(f32)

    wide_x = frames_grad
    each(frames // 64, f)
    vec[...] = vec_in[...]
    sums = norm_back_rows(dn1, wide_x, g1, dx1, frames_grad, low_buf, frames)
    vec[4:5, :], vec[5:6, :] = sums
    clips = 4 * halves
    b = 2 * z + c
    vec_rv[b] = vec[...]
    around = [
        remote(vec, vec_rv.at[b], vec_sem.at[0, k], vec_sem.at[1, k], clip=lax.rem(b + k, clips))
        for k in range(1, clips)
    ]
    start(around)
    for one in (go, gcq):
        arrive(one.seq())
        one.sum_seq()
        one.spread()
    for one in (gq, gk, gv):
        arrive(one.far())
        one.sum_far()
        one.spread()
    arrive(around)
    finish(around)
    total = vec_rv[0]
    for k in range(1, clips):
        total = total + vec_rv[k]
    vec[...] = total
    vec_rv[clips + s] = total
    along = [
        remote(
            vec, vec_rv.at[clips + s], vec_sem.at[0, clips + k], vec_sem.at[1, clips + k],
            seq=lax.rem(s + k, seqs),
        )
        for k in range(1, seqs)
    ]
    start(along)
    arrive(along)
    finish(along)
    total = vec_rv[clips]
    for k in range(1, seqs):
        total = total + vec_rv[clips + k]
    vec[...] = total

    for one in kv_out + kv_own:
        one.wait()
    for one in jobs:
        one.close()


OWN = ("cores", "near", "far")
STEPS = (("seq",), ("near", "far")) + (("near", "far", "seq"),) * 2 + (("split", "near", "far"),) + (OWN,) * 5
TAIL = 1536


def last_kernel(count, *refs):
    mats, (k_low, v_low, w_k, w_v, fo, fg) = refs[:count], refs[count : count + 6]
    outs, (text_out, fo_out, fg_out) = refs[count + 6 : 2 * count + 6], refs[2 * count + 6 : 2 * count + 9]
    rest = refs[2 * count + 9 :]
    low, full = rest[:count], rest[count : 2 * count]
    kv, w, text_grad, fo_buf, fg_buf, load_sem, save_sem, move_sem = rest[2 * count :]
    moves = [pltpu.make_async_copy(fo, fo_buf, move_sem.at[0]), pltpu.make_async_copy(fg, fg_buf, move_sem.at[1])]
    loads = [pltpu.make_async_copy(a, b, load_sem.at[n]) for n, (a, b) in enumerate(zip(mats, low))]
    for n, (src, dst) in enumerate(((k_low, kv.at[0]), (v_low, kv.at[1]), (w_k, w.at[0]), (w_v, w.at[1]))):
        loads.append(pltpu.make_async_copy(src, dst, load_sem.at[count + n]))
    saves = [pltpu.make_async_copy(a, b, save_sem.at[n]) for n, (a, b) in enumerate(zip(full, outs))]
    start(moves)
    start(loads)
    for one in moves:
        one.wait()
    moves = [pltpu.make_async_copy(fo_buf, fo_out, move_sem.at[0]), pltpu.make_async_copy(fg_buf, fg_out, move_sem.at[1])]
    start(moves)
    for n in range(count):
        loads[n].wait()
        rows, cols = low[n].shape
        step = max(16, min(rows, 65536 // cols))

        def f(i, n=n, step=step):
            r = tile_of(i, step)
            full[n][r, :] = low[n][r, :].astype(f32)

        each(rows // step, f)
        saves[n].start()
    for n in range(4):
        loads[count + n].wait()

    def f(t):
        rows = tile_of(t)
        text_grad[:, rows] = dg(kv[0], w[0, rows, :], NT) + dg(kv[1], w[1, rows, :], NT)

    each(w.shape[1] // 256, f)
    saves.append(pltpu.make_async_copy(text_grad, text_out, save_sem.at[count]))
    saves[-1].start()
    for one in saves + moves:
        one.wait()


def last(mats, k_low, v_low, w_k, w_v, fo, fg):
    hbm = pl.BlockSpec(memory_space=pl.ANY)
    count = len(mats)
    dma = pltpu.SemaphoreType.DMA
    shape = jax.ShapeDtypeStruct
    return pl.pallas_call(
        functools.partial(last_kernel, count),
        out_shape=[shape(one.shape, f32) for one in mats]
        + [shape(k_low.shape, f32), shape(fo.shape, bf), shape(fg.shape, f32)],
        in_specs=[hbm] * (count + 6),
        out_specs=[hbm] * (count + 3),
        scratch_shapes=[pltpu.VMEM(one.shape, bf) for one in mats]
        + [pltpu.VMEM(one.shape, f32) for one in mats]
        + [
            pltpu.VMEM((2,) + k_low.shape, bf),
            pltpu.VMEM((2,) + w_k.shape, bf),
            pltpu.VMEM(k_low.shape, f32),
            pltpu.VMEM(fo.shape, bf),
            pltpu.VMEM(fg.shape, f32),
            dma((count + 4,)),
            dma((count + 1,)),
            dma((2,)),
        ],
        compiler_params=pltpu.CompilerParams(vmem_limit_bytes=60 * 2**20),
    )(*mats, k_low, v_low, w_k, w_v, fo, fg)


def kc(seqs, clips, heads, lse, first, kq, vq, text, x, dx1, g1, vec, n1_all, weights, parts):
    halves = clips // 4
    rows, d = x.shape
    rb = d // clips
    shapes = [p.shape for p in parts] + [(halves, 2, 2, rb, W)] * 5
    bufs = []
    for steps, shape in zip(STEPS, shapes):
        bufs += job_bufs(steps, shape, seqs, halves)
    outs = [
        jax.ShapeDtypeStruct((rows, d), f32),
        jax.ShapeDtypeStruct((8, d), f32),
        jax.ShapeDtypeStruct((text.shape[0], d), bf),
        jax.ShapeDtypeStruct((text.shape[0], d), bf),
    ]
    for steps, shape in zip(STEPS, shapes):
        wide = 1 if "seq" in steps or "split" in steps else seqs
        outs.append(jax.ShapeDtypeStruct((shape[-2], shape[-1] * wide), bf))
    hbm = pl.BlockSpec(memory_space=pl.ANY)
    vmem = pl.BlockSpec(memory_space=pltpu.VMEM)
    most = max(seqs, halves)
    dma = pltpu.SemaphoreType.DMA
    return pl.pallas_call(
        functools.partial(kc_kernel, seqs, halves),
        out_shape=outs,
        in_specs=[vmem] * 14 + [hbm] * 9,
        out_specs=[vmem] * 2 + [hbm] * 12,
        scratch_shapes=[pltpu.VMEM((T, W), bf)] * 3
        + [pltpu.VMEM((T, W), f32)] * 2
        + [
            pltpu.VMEM((T, d), bf),
            pltpu.VMEM((d, W), f32),
            pltpu.VMEM((d, 3 * W), f32),
            pltpu.VMEM((5, halves, 2, 2, rb, W), bf),
            pltpu.VMEM((3, rows, d), bf),
            pltpu.VMEM((3, d, d), bf),
            pltpu.VMEM((rows, d), f32),
            pltpu.VMEM((4 * halves + seqs, 8, d), f32),
            pltpu.VMEM((rows, d), bf),
        ]
        + bufs
        + [
            dma((10, 2, 6, most)),
            dma((3, seqs)),
            dma((3, seqs)),
            dma((4,)),
            dma((2, 2, seqs)),
            dma((2, 4 * halves + seqs)),
        ],
        compiler_params=pltpu.CompilerParams(
            collective_id=1, has_side_effects=True, vmem_limit_bytes=60 * 2**20
        ),
    )(*heads, lse, first, kq, vq, text, x, dx1, g1[None], vec, n1_all, *weights, *parts)


def matmul(left, right):
    return jnp.dot(left, right, preferred_element_type=jnp.float32)


def left_times(left, right):
    return lax.dot_general(
        left, right, (((0,), (0,)), ((), ())), preferred_element_type=jnp.float32
    )


def right_times(left, right):
    return lax.dot_general(
        left, right, (((1,), (1,)), ((), ())), preferred_element_type=jnp.float32
    )


def norm_forward(values, gain, bias):
    center = values - jnp.mean(values, axis=-1, keepdims=True)
    scaled = lax.rsqrt(jnp.mean(center * center, axis=-1, keepdims=True) + EPS)
    unit = center * scaled
    return (unit * gain + bias, unit, scaled)


def norm_backward(upstream, unit, scaled, gain):
    along = upstream * gain
    inner = (
        along
        - jnp.mean(along, axis=-1, keepdims=True)
        - unit * jnp.mean(along * unit, axis=-1, keepdims=True)
    )
    return (inner * scaled, jnp.sum(upstream * unit, axis=0), jnp.sum(upstream, axis=0))


def gelu_slope(values):
    return (
        0.5 * (1.0 + lax.erf(values * SQRT_HALF))
        + values * jnp.exp(-0.5 * values * values) * INV_ROOT_TWO_PI
    )


def softmax_rows(scores):
    top = jnp.max(scores, axis=-1, keepdims=True)
    expo = jnp.exp(scores - top)
    total = jnp.sum(expo, axis=-1, keepdims=True)
    return (expo / total, top[..., 0] + jnp.log(total[..., 0]))


def shards(
    frames_in,
    text_states,
    clip_lengths,
    self_gain,
    self_bias,
    query_weight,
    key_weight,
    value_weight,
    output_weight,
    cross_gain,
    cross_bias,
    cross_query,
    cross_key,
    cross_value,
    cross_output,
    feed_gain,
    feed_bias,
    feed_upward,
    feed_downward,
    grad_out,
):
    count = lax.axis_size("seq")
    place = lax.axis_index("seq")
    local = frames_in.shape[1]
    total_frames = local * count
    block = min(512, total_frames)
    blocks = total_frames // block
    scale = HD ** (-0.5)
    lengths = clip_lengths[0]
    slot = jnp.arange(CLIPS, dtype=jnp.int32)
    ends = jnp.sum(jnp.where(slot[None, :] <= slot[:, None], lengths[None, :], 0), axis=1)
    begins = ends - lengths
    slots = jnp.arange(CLIPS, dtype=jnp.int32)
    positions = jnp.arange(total_frames, dtype=jnp.int32)
    owner_all = jnp.sum((ends[None, :] <= positions[:, None]).astype(jnp.int32), axis=1)
    first_all = jnp.sum(jnp.where(owner_all[:, None] == slots[None, :], begins[None, :], 0), axis=1)
    owner_mine = lax.dynamic_slice_in_dim(owner_all, place * local, local, 0)
    frames = frames_in[0].astype(jnp.float32)
    text = text_states[0]
    text_rows = text.shape[0]
    weights = (query_weight, key_weight, value_weight)
    normed_low, attended, log_totals, query_heads, key_heads, value_heads, attended_frames, cross_k, cross_v = ka(
        count, frames_in[0], self_gain, self_bias, first_all[None], text, weights + (cross_key, cross_value)
    )
    clips = lax.axis_size("clip")
    dx1, output, vec, c_up, c_dn, c_o, c_cq, c_co, grad_heads, normed_all, key_own, value_own = kb(
        count,
        clips,
        attended_frames,
        frames_in[0],
        grad_out[0],
        cross_k,
        cross_v,
        owner_mine,
        cross_gain,
        cross_bias,
        feed_gain,
        feed_bias,
        output_weight,
        cross_query,
        cross_output,
        feed_upward,
        feed_downward,
        normed_low,
    )
    frames_grad, vec, key_low, value_low, *mats = kc(
        count,
        clips,
        (query_heads, key_heads, value_heads, attended, grad_heads),
        log_totals,
        first_all[None],
        key_own,
        value_own,
        text,
        frames_in[0],
        dx1,
        self_gain,
        vec,
        normed_all,
        weights,
        (c_up, c_dn.reshape((-1, 2) + c_dn.shape[1:]), c_o, c_cq, c_co),
    )
    *mats, text_grad, output, frames_grad = last(
        mats, key_low, value_low, cross_key, cross_value, output, frames_grad
    )
    w_up, w_dn, w_o, w_cq, w_co, w_xk, w_xv, w_q, w_k, w_v = mats
    width_out = D // clips
    vec = lax.dynamic_slice_in_dim(vec, lax.axis_index("clip") * width_out, width_out, 1)
    return (
        output[None],
        frames_grad[None],
        text_grad[None],
        vec[4],
        vec[5],
        w_q,
        w_k,
        w_v,
        w_o,
        vec[0],
        vec[1],
        w_cq,
        w_xk,
        w_xv,
        w_co,
        vec[2],
        vec[3],
        w_up,
        w_dn,
    )


def solution(mesh):
    return jax.shard_map(
        shards,
        mesh=mesh,
        in_specs=(
            P("clip", "seq", None),
            P("clip", None, None),
            P("clip", None),
            P(),
            P(),
            P(),
            P(),
            P(),
            P(),
            P(),
            P(),
            P(),
            P(),
            P(),
            P(),
            P(),
            P(),
            P(),
            P(),
            P("clip", "seq", None),
        ),
        out_specs=(
            P("clip", "seq", None),
            P("clip", "seq", None),
            P("clip", None, None),
            P("clip"),
            P("clip"),
            P("clip", None),
            P("clip", None),
            P("clip", None),
            P("clip", None),
            P("clip"),
            P("clip"),
            P("clip", None),
            P("clip", None),
            P("clip", None),
            P("clip", None),
            P("clip"),
            P("clip"),
            P("clip", None),
            P("clip", None),
        ),
        check_vma=False,
    )
```
